32 devices in a mesh: dp: 8 (over y, x, core), mp: 4 (over z).
Axes of the slice: x: 2, y: 2, z: 4, core: 2. Of those that a mesh axis runs over, the one named last changes fastest.
Arguments:
- inputs: bfloat16 [96, 128, 768], P(('dp', 'mp')), may hold values from -6 to 6
- slot_valid: int32 [96, 128], P('dp'), may hold values from 0 to 1, as said below
- ln1_gain: float32 [2, 768], replicated, may hold values from 0.5 to 1.5
- ln1_bias: float32 [2, 768], replicated, may hold values from -2 to 2
- w_query: bfloat16 [2, 768, 768], replicated, may hold values from -0.21875 to 0.21875
- w_key: bfloat16 [2, 768, 768], replicated, may hold values from -0.21875 to 0.21875
- w_value: bfloat16 [2, 768, 768], replicated, may hold values from -0.21875 to 0.21875
- w_out: bfloat16 [2, 768, 768], replicated, may hold values from -0.875 to 0.875
- gate_logit: float32 [768], replicated, may hold values from -4 to 4
- ln2_gain: float32 [2, 768], replicated, may hold values from 0.5 to 1.5
- ln2_bias: float32 [2, 768], replicated, may hold values from -2 to 2
- w_up: bfloat16 [2, 768, 3072], P(None, None, 'mp'), may hold values from -0.21875 to 0.21875
- b_up: float32 [2, 3072], P(None, 'mp'), may hold values from -3 to 3
- w_down: bfloat16 [2, 3072, 768], P(None, 'mp'), may hold values from -0.109375 to 0.109375
- b_down: float32 [2, 768], replicated, may hold values from -2 to 2
- cotangent: bfloat16 [96, 128, 768], P(('dp', 'mp')), may hold values from -6 to 6
Outputs:
- outputs: bfloat16 [96, 128, 768], P(('dp', 'mp'))
- grad_inputs: float32 [96, 128, 768], P(('dp', 'mp'))
- grad_ln1_gain: float32 [2, 768], P(None, 'dp')
- grad_ln1_bias: float32 [2, 768], P(None, 'dp')
- grad_w_query: float32 [2, 768, 768], P(None, 'dp', 'mp')
- grad_w_key: float32 [2, 768, 768], P(None, 'dp', 'mp')
- grad_w_value: float32 [2, 768, 768], P(None, 'dp', 'mp')
- grad_w_out: float32 [2, 768, 768], P(None, 'dp', 'mp')
- grad_gate: float32 [768], P('dp')
- grad_ln2_gain: float32 [2, 768], P(None, 'dp')
- grad_ln2_bias: float32 [2, 768], P(None, 'dp')
- grad_w_up: float32 [2, 768, 3072], P(None, 'dp', 'mp')
- grad_b_up: float32 [2, 3072], P(None, 'mp')
- grad_w_down: float32 [2, 3072, 768], P(None, 'mp', 'dp')
- grad_b_down: float32 [2, 768], P(None, 'dp')
The draws below stay inside these ranges and needn't reach their ends.
Inputs may be any that keep to these rules, and one draw needn't show every extreme that they name: `slot_valid`: on every page slots 0 to 112 (the text blocks and the first visual slot) are 1.
All inputs are finite; a program needn't handle non-finite values.
Results may differ from the reference program's by a relative error of at most 0.02.
Values may be sent and summed in bfloat16 or wider, within the bound.
No kernel may reach another device: no remote copies, remote signals or barrier semaphores. Data moves between devices by JAX's collectives and lax.ppermute only.
A program may use at most 192 MiB of HBM per device.

```python
import math
from functools import partial
import jax
import jax.numpy as jnp
from jax import lax

D = 768
HEADS = 12
HEAD_SIZE = 64
FF = 3072
SLOTS = 128
TEXT = 112
LAYERS = 2
PAGES = 96


def draw_slot_valid(key, part):
    coins = jax.random.randint(key, (PAGES, SLOTS), 0, 10)
    slot_ids = lax.broadcasted_iota(jnp.int32, (PAGES, SLOTS), 1)
    return jnp.where(slot_ids <= TEXT, 1, jnp.where(coins < 7, 1, 0)).astype(jnp.int32)


def levels(own_key, shape, split, least, largest):
    factor_of, own = 1.0, jax.random.fold_in(own_key, 6)
    for axis_at, parts in split:
        heights = jnp.exp(jax.random.uniform(jax.random.fold_in(own, axis_at), (parts,), jnp.float32, least / len(split), largest / len(split)))
        factor_of = factor_of * jnp.repeat(heights, shape[axis_at] // parts).reshape([-1 if axis == axis_at else 1 for axis in range(len(shape))])
    return factor_of


def gaussian(key, extent, scale, most, pieces=(), kind=jnp.bfloat16):
    values = jax.random.normal(key, extent, jnp.float32) * scale
    if len(pieces) > 0:
        values = levels(key, extent, pieces, -0.22, 0.18) * values
    return jnp.clip(values, min=-most, max=most).astype(kind)


def setup_inputs(seed: int = 0) -> dict:
    seeds = jax.random.split(jax.random.key(seed), 17)
    inputs = gaussian(seeds[0], (PAGES, SLOTS, D), 1.0, 6.0, ((0, 32),))
    slot_valid = draw_slot_valid(jax.random.fold_in(seeds[16], 71), 0)
    ln1_gain = jnp.clip(1.0 + 0.1 * jax.random.normal(seeds[2], (LAYERS, D), jnp.float32), 0.5, 1.5)
    ln1_bias = gaussian(seeds[3], (LAYERS, D), 0.3, 2.0, (), jnp.float32)
    w_query = gaussian(seeds[4], (LAYERS, D, D), D ** -0.5, 0.21875)
    w_key = gaussian(seeds[5], (LAYERS, D, D), D ** -0.5, 0.21875)
    w_value = gaussian(seeds[6], (LAYERS, D, D), D ** -0.5, 0.21875)
    w_out = gaussian(seeds[7], (LAYERS, D, D), (D // 16) ** -0.5, 0.875)
    gate_logit = gaussian(seeds[8], (D,), 1.0, 4.0, (), jnp.float32)
    ln2_gain = jnp.clip(1.0 + 0.1 * jax.random.normal(seeds[9], (LAYERS, D), jnp.float32), 0.5, 1.5)
    ln2_bias = gaussian(seeds[10], (LAYERS, D), 0.3, 2.0, (), jnp.float32)
    w_up = gaussian(seeds[11], (LAYERS, D, FF), D ** -0.5, 0.21875, ((2, 4),))
    b_up = gaussian(seeds[12], (LAYERS, FF), 0.5, 3.0, ((1, 4),), jnp.float32)
    w_down = gaussian(seeds[13], (LAYERS, FF, D), FF ** -0.5, 0.109375, ((1, 4),))
    b_down = gaussian(seeds[14], (LAYERS, D), 0.3, 2.0, (), jnp.float32)
    cotangent = gaussian(seeds[15], (PAGES, SLOTS, D), 1.0, 6.0, ((0, 32),))
    return dict(inputs=inputs, slot_valid=slot_valid, ln1_gain=ln1_gain, ln1_bias=ln1_bias, w_query=w_query, w_key=w_key, w_value=w_value, w_out=w_out, gate_logit=gate_logit, ln2_gain=ln2_gain, ln2_bias=ln2_bias, w_up=w_up, b_up=b_up, w_down=w_down, b_down=b_down, cotangent=cotangent)


@jax.custom_vjp
def low(v):
    return lax.optimization_barrier(v.astype(jnp.bfloat16)).astype(jnp.float32)

@jax.custom_vjp
def low_back(v):
    return v

def low_keep(v):
    return (low(v), None)

def low_pass(kept, grad):
    return (grad,)

def back_keep(v):
    return (v, None)

def back_low(kept, grad):
    return (low(grad),)
low.defvjp(low_keep, low_pass)
low_back.defvjp(back_keep, back_low)
highest = lax.Precision.HIGHEST

def normalize(resid, gain, shift):
    center = lax.optimization_barrier(jnp.mean(resid, axis=-1, keepdims=True))
    centered = resid - center
    spread = lax.optimization_barrier(jnp.mean(centered * centered, axis=-1, keepdims=True))
    return centered * lax.rsqrt(spread + 1e-05) * gain + shift

def group_attention(block, crossed):
    queries, key_rows, value_rows, slot_valid = block
    scale = 1.0 / math.sqrt(HEAD_SIZE)
    raw = low_back(jnp.einsum('pshe,pthe->phst', queries, key_rows, precision=highest) * scale)
    allowed = (slot_valid == 1)[:, None, None, :]
    if crossed:
        query_text = lax.broadcasted_iota(jnp.int32, (SLOTS, SLOTS), 0) < TEXT
        key_text = lax.broadcasted_iota(jnp.int32, (SLOTS, SLOTS), 1) < TEXT
        allowed = jnp.logical_and(allowed, (query_text != key_text)[None, None])
    masked = jnp.where(allowed, raw, -1e+30)
    probs = low(jax.nn.softmax(masked, axis=-1))
    return jnp.einsum('phst,pthe->pshe', probs, value_rows, precision=highest)

def layer(resid, slot_valid, params, layer_index, crossed):
    ln1_gain, ln1_bias, w_query, w_key, w_value, w_out, gate_logit, ln2_gain, ln2_bias, w_up, b_up, w_down, b_down = params
    group = math.gcd(PAGES, 32)
    row_matrix = resid.reshape(PAGES * SLOTS, D)
    normed = low(normalize(row_matrix, ln1_gain[layer_index], ln1_bias[layer_index]))

    def project(weight):
        made = low(low_back(jnp.dot(normed, weight, precision=highest)))
        return made.reshape(PAGES // group, group, SLOTS, HEADS, HEAD_SIZE)
    queries = project(w_query[layer_index])
    key_rows = project(w_key[layer_index])
    value_rows = project(w_value[layer_index])
    valid_groups = slot_valid.reshape(PAGES // group, group, SLOTS)
    context = lax.map(jax.checkpoint(partial(group_attention, crossed=crossed)), (queries, key_rows, value_rows, valid_groups))
    context = low(low_back(context.reshape(PAGES * SLOTS, D)))
    branch = low_back(jnp.dot(context, w_out[layer_index], precision=highest))
    if crossed:
        branch = jax.nn.sigmoid(gate_logit) * branch
    mixed = row_matrix + branch
    normed_two = low(normalize(mixed, ln2_gain[layer_index], ln2_bias[layer_index]))
    upper = low_back(jnp.dot(normed_two, w_up[layer_index], precision=highest)) + b_up[layer_index]
    active = low(jax.nn.gelu(upper, approximate=False))
    down_part = low_back(jnp.dot(active, w_down[layer_index], precision=highest))
    return (mixed + down_part + b_down[layer_index]).reshape(PAGES, SLOTS, D)

def reference(inputs, slot_valid, ln1_gain, ln1_bias, w_query, w_key, w_value, w_out, gate_logit, ln2_gain, ln2_bias, w_up, b_up, w_down, b_down, cotangent):
    floats = tuple((value.astype(jnp.float32) for value in (ln1_gain, ln1_bias, w_query, w_key, w_value, w_out, gate_logit, ln2_gain, ln2_bias, w_up, b_up, w_down, b_down)))

    def forward(resid, params):
        middle = layer(resid, slot_valid, params, 0, True)
        return layer(middle, slot_valid, params, 1, False)
    result, pullback = jax.vjp(forward, inputs.astype(jnp.float32), floats)
    grad_resid, grads = pullback(cotangent.astype(jnp.float32))
    return (result.astype(jnp.bfloat16), grad_resid, grads[0], grads[1], grads[2], grads[3], grads[4], grads[5], grads[6], grads[7], grads[8], grads[9], grads[10], grads[11], grads[12])
```

```python
import functools

import jax
import jax.numpy as jnp
from jax import lax
from jax.experimental import pallas as pl
from jax.experimental.pallas import tpu as pltpu
from jax.sharding import PartitionSpec as P

HEADS = 12
TEXT = 112
F32 = jnp.float32
BF16 = jnp.bfloat16
VMEM_BYTES = 56 * 2**20


def dot(a, b, a_dim, b_dim):
    return lax.dot_general(a, b, (((a_dim,), (b_dim,)), ((), ())), preferred_element_type=F32)


def whiten(rows):
    centered = rows - jnp.mean(rows, axis=-1, keepdims=True)
    spread = jnp.mean(centered * centered, axis=-1, keepdims=True)
    inverse = lax.rsqrt(spread + 1e-05)
    return centered * inverse, inverse


def whiten_back(white, inverse, gain, grad):
    scaled = grad * gain
    first = jnp.mean(scaled, axis=-1, keepdims=True)
    second = jnp.mean(scaled * white, axis=-1, keepdims=True)
    return inverse * (scaled - first - white * second)


def column_sum(rows):
    return jnp.sum(rows, axis=0, keepdims=True)


def gelu_and_slope(values):
    size = jnp.abs(values)
    t = 1.0 / (1.0 + (0.3275911 * 0.7071067811865476) * size)
    bell = jnp.exp(-0.5 * values * values)
    poly = 0.5 * 1.061405429
    poly = poly * t + 0.5 * -1.453152027
    poly = poly * t + 0.5 * 1.421413741
    poly = poly * t + 0.5 * -0.284496736
    poly = poly * t + 0.5 * 0.254829592
    tail = poly * t * bell
    phi = jnp.where(values >= 0.0, 1.0 - tail, tail)
    return values * phi, phi + values * bell * 0.3989422804014327


def split_heads(pair):
    lane = lax.broadcasted_iota(jnp.int32, pair.shape, 1)
    first = lane < pair.shape[1] // 2
    zero = jnp.zeros_like(pair)
    return jnp.concatenate([jnp.where(first, pair, zero), jnp.where(first, zero, pair)], axis=0)


def join_heads(both):
    slots = both.shape[0] // 2
    lane = lax.broadcasted_iota(jnp.int32, (slots, both.shape[1]), 1)
    return jnp.where(lane < both.shape[1] // 2, both[:slots], both[slots:])


def start_copies(sources, targets, sems):
    copies = [
        pltpu.make_async_copy(source, target, sems.at[at])
        for at, (source, target) in enumerate(zip(sources, targets))
    ]
    for copy in copies:
        copy.start()
    return copies


def attend_kernel(layer, crossed, resid, mask, gain, shift, gate, wq, wk, wv, wo,
                  q_out, k_out, v_out, p_out, c_out, mixed, branch_out, held, sems):
    pages, slots = mask.shape[0], mask.shape[1]
    width = resid.shape[1]
    pairs = HEADS // 2
    pair_width = width // pairs
    scale = 1.0 / (width // HEADS) ** 0.5
    copies = start_copies(
        [w.at[layer] for w in (wq, wk, wv, wo)], [held.at[at] for at in range(4)], sems
    )
    white, _ = whiten(resid[...].astype(F32))
    normed = (white * gain[layer:layer + 1] + shift[layer:layer + 1]).astype(BF16)
    copies[0].wait()
    q_out[...] = (dot(normed, held[0], 1, 0).astype(BF16).astype(F32) * scale).astype(BF16)
    copies[1].wait()
    k_out[...] = dot(normed, held[1], 1, 0).astype(BF16)
    copies[2].wait()
    v_out[...] = dot(normed, held[2], 1, 0).astype(BF16)

    for page in range(pages):
        rows = slice(page * slots, (page + 1) * slots)
        bias = mask[page]
        for pair in range(pairs):
            cols = slice(pair * pair_width, (pair + 1) * pair_width)
            scores = dot(split_heads(k_out[rows, cols]), q_out[rows, cols], 1, 1)
            scores = scores.reshape(2, slots, slots) + bias[None]
            top = jnp.max(scores, axis=1, keepdims=True)
            raised = jnp.exp(scores - top)
            probs = raised * (1.0 / jnp.sum(raised, axis=1, keepdims=True))
            probs = probs.reshape(2 * slots, slots).astype(BF16)
            p_out[page, pair] = probs
            c_out[rows, cols] = dot(probs, split_heads(v_out[rows, cols]), 0, 0).astype(BF16)
    copies[3].wait()
    branch = dot(c_out[...], held[3], 1, 0)
    if crossed:
        branch_out[...] = branch.astype(BF16)
        branch = branch * jax.nn.sigmoid(gate[...])
    mixed[...] = resid[...].astype(F32) + branch


def attend(layer, crossed, resid, mask, gain, shift, gate, weights):
    rows, width = resid.shape
    pages, slots = mask.shape[:2]
    low = jax.ShapeDtypeStruct((rows, width), BF16)
    vmem = pl.BlockSpec(memory_space=pltpu.VMEM)
    outs = [low, low, low, jax.ShapeDtypeStruct((pages, HEADS // 2, 2 * slots, slots), BF16), low,
            jax.ShapeDtypeStruct((rows, width), F32)]
    if crossed:
        outs.append(low)

    def body(*refs):
        ins, rest = refs[:9], list(refs[9:])
        if not crossed:
            rest.insert(6, None)
        attend_kernel(layer, crossed, *ins, *rest)

    return pl.pallas_call(
        body,
        out_shape=outs,
        in_specs=[vmem] * 5 + [pl.BlockSpec(memory_space=pl.ANY)] * 4,
        out_specs=[vmem] * len(outs),
        scratch_shapes=[pltpu.VMEM((4, width, width), BF16), pltpu.SemaphoreType.DMA((4,))],
        compiler_params=pltpu.CompilerParams(vmem_limit_bytes=VMEM_BYTES),
        cost_estimate=pl.CostEstimate(flops=8 * rows * width * width, bytes_accessed=14 * 2**20, transcendentals=0),
    )(resid, mask, gain, shift, gate, *weights)


class Pieces:
    def __init__(self, arrays, plan, blocks, piece_rows):
        self.arrays, self.plan, self.blocks, self.piece_rows = arrays, plan, blocks, piece_rows

    def copies(self, refs, held, blocks, sems, shard):
        made = []
        for at, (array, index, kind, owner, place) in enumerate(self.plan):
            if owner != shard:
                continue
            if place is None:
                target = held[kind].at[shard]
            else:
                start = pl.multiple_of(blocks[place] * self.piece_rows, self.piece_rows)
                target = held[kind].at[shard, pl.ds(start, self.piece_rows)]
            made.append(pltpu.make_async_copy(refs[array].at[index], target, sems.at[at]))
        return made

    def start_and_wait(self, refs, held, blocks, sems, shards):
        step = pl.program_id(0)

        @pl.when(step == 0)
        def _():
            for shard in range(shards):
                for copy in self.copies(refs, held, blocks, sems, shard):
                    copy.start()

        def wait():
            for shard in range(shards):
                @pl.when(step == shard)
                def _():
                    for copy in self.copies(refs, held, blocks, sems, shard):
                        copy.wait()
        return wait


def feed_kernel(layer, pieces, blocks, mixed, gain, shift, b_up, b_down, *rest):
    count = len(pieces.arrays)
    refs = rest[:count]
    result, active_out, slope_out, up, down, low, total, sems = rest[count:]
    shards, width = up.shape[0], up.shape[2]
    step = pl.program_id(0)
    wait = pieces.start_and_wait(refs, (up, down), blocks, sems, shards)

    @pl.when(step == 0)
    def _():
        white, _ = whiten(mixed[...])
        low[...] = (white * gain[layer:layer + 1] + shift[layer:layer + 1]).astype(BF16)
        total[...] = mixed[...] + b_down[layer:layer + 1]

    wait()
    parts = 3
    part = width // parts
    for at in range(parts):
        cols = slice(at * part, (at + 1) * part)
        upper = dot(low[...], up[step, :, cols], 1, 0) + b_up[0, :, cols]
        active, slope = gelu_and_slope(upper)
        active = active.astype(BF16)
        active_out[0, :, cols] = active
        slope_out[0, :, cols] = slope.astype(BF16)
        total[...] += dot(active, down[step, cols, :], 1, 0)

    @pl.when(step == shards - 1)
    def _():
        result[...] = total[...].astype(result.dtype)


def feed(layer, mixed, gain, shift, b_up, b_down, pieces, out_type):
    rows, width = mixed.shape
    shards = b_up.shape[0]
    whole = lambda shape: pl.BlockSpec(shape, lambda step: (0,) * len(shape))
    each = lambda shape: pl.BlockSpec((1,) + shape, lambda step: (step,) + (0,) * len(shape))
    return pl.pallas_call(
        functools.partial(feed_kernel, layer, pieces),
        grid=(shards,),
        out_shape=[jax.ShapeDtypeStruct((rows, width), out_type)]
        + [jax.ShapeDtypeStruct((shards, rows, width), BF16)] * 2,
        in_specs=[pl.BlockSpec(memory_space=pltpu.SMEM), whole((rows, width)), whole(gain.shape), whole(shift.shape),
                  each((1, width)), whole(b_down.shape)]
        + [pl.BlockSpec(memory_space=pl.ANY)] * len(pieces.arrays),
        out_specs=[whole((rows, width)), each((rows, width)), each((rows, width))],
        scratch_shapes=[pltpu.VMEM((shards, width, width), BF16), pltpu.VMEM((shards, width, width), BF16),
                        pltpu.VMEM((rows, width), BF16), pltpu.VMEM((rows, width), F32),
                        pltpu.SemaphoreType.DMA((len(pieces.plan),))],
        compiler_params=pltpu.CompilerParams(vmem_limit_bytes=VMEM_BYTES),
        cost_estimate=pl.CostEstimate(flops=16 * rows * width * width, bytes_accessed=20 * 2**20, transcendentals=0),
    )(pieces.blocks, mixed, gain, shift, b_up, b_down, *pieces.arrays)


def turn_rows(rows, held, turned, blocks, order):
    held[...] = rows.T
    size = held.shape[0] // len(order)
    for at, place in enumerate(order):
        start = pl.multiple_of(blocks[place] * size, size)
        turned[at * size:(at + 1) * size] = held[pl.ds(start, size)]


def feed_back_kernel(layer, pieces, orders, blocks, grad_out, mixed, gain, shift, active, slope, *rest):
    count = len(pieces.arrays)
    refs = rest[:count]
    (grad_mixed, up_keep, up_send, down_keep, down_send, sums, up_sums,
     up, down, low, low_turned, normed_turned, held, total, sems) = rest[count:]
    shards = up.shape[0]
    half = up_keep.shape[1]
    step = pl.program_id(0)
    wait = pieces.start_and_wait(refs, (up, down), blocks, sems, shards)

    @pl.when(step == 0)
    def _():
        rows = grad_out[...].astype(F32)
        low[...] = rows.astype(BF16)
        sums[0:1] = column_sum(rows)
        turn_rows(low[...], held, low_turned, blocks, orders[1])
        white, _ = whiten(mixed[...])
        normed = (white * gain[layer:layer + 1] + shift[layer:layer + 1]).astype(BF16)
        turn_rows(normed, held, normed_turned, blocks, orders[0])
        total[...] = jnp.zeros_like(total)

    wait()
    made = dot(low_turned[...], active[0], 1, 0).astype(BF16)
    down_keep[0] = made[:half]
    down_send[0] = made[half:]
    upper = dot(low[...], down[step], 1, 1) * slope[0].astype(F32)
    up_sums[0] = column_sum(upper)
    upper_low = upper.astype(BF16)
    made = dot(normed_turned[...], upper_low, 1, 0).astype(BF16)
    up_keep[0] = made[:half]
    up_send[0] = made[half:]
    total[...] += dot(upper_low, up[step], 1, 1)

    @pl.when(step == shards - 1)
    def _():
        white, inverse = whiten(mixed[...])
        grad = total[...]
        sums[1:2] = column_sum(grad * white)
        sums[2:3] = column_sum(grad)
        grad_mixed[...] = grad_out[...].astype(F32) + whiten_back(white, inverse, gain[layer:layer + 1], grad)


def feed_back(layer, grad_out, mixed, gain, shift, active, slope, pieces, orders):
    rows, width = mixed.shape
    shards = active.shape[0]
    half = width // 2
    whole = lambda shape: pl.BlockSpec(shape, lambda step: (0,) * len(shape))
    each = lambda shape: pl.BlockSpec((1,) + shape, lambda step: (step,) + (0,) * len(shape))
    return pl.pallas_call(
        functools.partial(feed_back_kernel, layer, pieces, orders),
        grid=(shards,),
        out_shape=[jax.ShapeDtypeStruct((rows, width), F32)]
        + [jax.ShapeDtypeStruct((shards, half, width), BF16)] * 4
        + [jax.ShapeDtypeStruct((3, width), F32), jax.ShapeDtypeStruct((shards, 1, width), F32)],
        in_specs=[pl.BlockSpec(memory_space=pltpu.SMEM), whole((rows, width)), whole((rows, width)), whole(gain.shape),
                  whole(shift.shape), each((rows, width)), each((rows, width))]
        + [pl.BlockSpec(memory_space=pl.ANY)] * len(pieces.arrays),
        out_specs=[whole((rows, width))] + [each((half, width))] * 4 + [whole((3, width)), each((1, width))],
        scratch_shapes=[pltpu.VMEM((shards, width, width), BF16), pltpu.VMEM((shards, width, width), BF16),
                        pltpu.VMEM((rows, width), BF16), pltpu.VMEM((width, rows), BF16),
                        pltpu.VMEM((width, rows), BF16), pltpu.VMEM((width, rows), BF16),
                        pltpu.VMEM((rows, width), F32), pltpu.SemaphoreType.DMA((len(pieces.plan),))],
        compiler_params=pltpu.CompilerParams(vmem_limit_bytes=VMEM_BYTES),
        cost_estimate=pl.CostEstimate(flops=32 * rows * width * width, bytes_accessed=30 * 2**20, transcendentals=0),
    )(pieces.blocks, grad_out, mixed, gain, shift, active, slope, *pieces.arrays)


def attend_back_kernel(layer, crossed, orders, blocks, grad_mixed, resid, gain, shift, gate, q, k, v, p, context, branch,
                       wq, wk, wv, wo, grad_resid, first_keep, first_send, second_keep, second_send, sums,
                       held, turning, turned, gc, gq, gk, gv, sems):
    pages, slots = p.shape[0], p.shape[3]
    width = resid.shape[1]
    half = width // 2
    pairs = HEADS // 2
    pair_width = width // pairs
    scale = 1.0 / (width // HEADS) ** 0.5
    copies = start_copies(
        [w.at[layer] for w in (wo, wq, wk, wv)], [held.at[at] for at in range(4)], sems
    )
    grad = grad_mixed[...]
    if crossed:
        opened = jax.nn.sigmoid(gate[...])
        sums[2:3] = column_sum(grad * branch[...].astype(F32)) * (opened * (1.0 - opened))
        low = (grad * opened).astype(BF16)
    else:
        low = grad.astype(BF16)
    turn_rows(context[...], turning, turned, blocks, orders[1])
    made = dot(turned[...], low, 1, 0).astype(BF16)
    second_keep[1] = made[:half]
    second_send[1] = made[half:]
    copies[0].wait()
    gc[...] = dot(low, held[0], 1, 1).astype(BF16)

    for page in range(pages):
        rows = slice(page * slots, (page + 1) * slots)
        for pair in range(pairs):
            cols = slice(pair * pair_width, (pair + 1) * pair_width)
            probs_low = p[page, pair]
            probs = probs_low.astype(F32).reshape(2, slots, slots)
            grad_probs = dot(split_heads(v[rows, cols]), gc[rows, cols], 1, 1).reshape(2, slots, slots)
            delta = jnp.sum(probs * grad_probs, axis=1, keepdims=True)
            grad_scores = (probs * (grad_probs - delta)).astype(BF16).reshape(2 * slots, slots)
            gq[rows, cols] = (dot(grad_scores, split_heads(k[rows, cols]), 0, 0) * scale).astype(BF16)
            gk[rows, cols] = join_heads(dot(grad_scores, q[rows, cols], 1, 0)).astype(BF16)
            gv[rows, cols] = join_heads(dot(probs_low, gc[rows, cols], 1, 0)).astype(BF16)

    white, inverse = whiten(resid[...].astype(F32))
    normed = (white * gain[layer:layer + 1] + shift[layer:layer + 1]).astype(BF16)
    turn_rows(normed, turning, turned, blocks, orders[1])
    made = dot(turned[...], gv[...], 1, 0).astype(BF16)
    second_keep[0] = made[:half]
    second_send[0] = made[half:]
    turn_rows(normed, turning, turned, blocks, orders[0])
    for at, rows in enumerate((gq, gk)):
        made = dot(turned[...], rows[...], 1, 0).astype(BF16)
        first_keep[at] = made[:half]
        first_send[at] = made[half:]
    for copy in copies[1:]:
        copy.wait()
    total = dot(gq[...], held[1], 1, 1) + dot(gk[...], held[2], 1, 1) + dot(gv[...], held[3], 1, 1)
    sums[0:1] = column_sum(total * white)
    sums[1:2] = column_sum(total)
    grad_resid[...] = grad + whiten_back(white, inverse, gain[layer:layer + 1], total)


def attend_back(layer, crossed, grad_mixed, resid, gain, shift, gate, kept, weights, blocks, orders):
    rows, width = resid.shape
    half = width // 2
    vmem = pl.BlockSpec(memory_space=pltpu.VMEM)
    kept = list(kept)
    given = 6 + len(kept) + 4

    def body(*refs):
        ins, rest = list(refs[:given]), refs[given:]
        if not crossed:
            ins.insert(11, None)
        attend_back_kernel(layer, crossed, orders, *ins, *rest)

    low = pltpu.VMEM((rows, width), BF16)
    return pl.pallas_call(
        body,
        out_shape=[jax.ShapeDtypeStruct((rows, width), F32)]
        + [jax.ShapeDtypeStruct((2, half, width), BF16)] * 4
        + [jax.ShapeDtypeStruct((3 if crossed else 2, width), F32)],
        in_specs=[pl.BlockSpec(memory_space=pltpu.SMEM)] + [vmem] * (5 + len(kept))
        + [pl.BlockSpec(memory_space=pl.ANY)] * 4,
        out_specs=[vmem] * 6,
        scratch_shapes=[pltpu.VMEM((4, width, width), BF16), pltpu.VMEM((width, rows), BF16),
                        pltpu.VMEM((width, rows), BF16), low, low, low, low, pltpu.SemaphoreType.DMA((4,))],
        compiler_params=pltpu.CompilerParams(vmem_limit_bytes=VMEM_BYTES),
        cost_estimate=pl.CostEstimate(flops=16 * rows * width * width, bytes_accessed=24 * 2**20, transcendentals=0),
    )(blocks, grad_mixed, resid, gain, shift, gate, *kept, *(weights[at] for at in (0, 1, 2, 3)))


def swap(value, axis, bit):
    size = lax.axis_size(axis)
    return lax.ppermute(value, axis, [(at, at ^ bit) for at in range(size)])


class Eighths:
    bits = (1, 2, 4)
    orders = ((0, 4, 2, 6, 1, 5, 3, 7), (0, 2, 4, 6, 1, 3, 5, 7))

    def __init__(self):
        self.parts = 8
        self.blocks = lax.axis_index("dp") ^ jnp.arange(8, dtype=jnp.int32)

    def gather(self, w_up, w_down):
        layers, width, shard_width = w_up.shape
        rows = width // 8
        at = lax.axis_index("dp") * rows
        shards = lax.axis_size("mp")
        own = jnp.stack([lax.dynamic_slice_in_dim(w_up, at, rows, 1), lax.dynamic_slice_in_dim(w_down, at, rows, 1)], 1)
        made = []
        for layer in range(layers):
            mine = own[layer]
            far = [swap(mine, "mp", other) for other in range(1, shards)]
            ups = jnp.stack([piece[0] for piece in far])
            downs = jnp.stack([piece[1] for piece in far])
            ups_x = swap(ups, "dp", 2)
            downs_y = swap(downs, "dp", 4)
            ups_two = jnp.stack([ups, ups_x])
            downs_two = jnp.stack([downs, downs_y])
            ups_y = swap(ups_two, "dp", 4)
            downs_x = swap(downs_two, "dp", 2)
            halves = [ups_two, ups_y, downs_two, downs_x]
            arrays = [w_up, w_down] + halves + [swap(half, "dp", 1) for half in halves]
            plan = [(0, layer, 0, 0, None), (1, layer, 1, 0, None)]
            for core in range(2):
                for kind in range(2):
                    inner, outer = ((2, 4), (4, 2))[kind]
                    for second in range(2):
                        for first in range(2):
                            for other in range(1, shards):
                                place = core + inner * first + outer * second
                                plan.append((2 + 4 * core + 2 * kind + second, (first, other - 1), kind, other, place))
            made.append(Pieces(arrays, plan, self.blocks, rows))
        return made

    def order_hidden(self, bias):
        shards = lax.axis_size("mp")
        far = [bias] + [swap(bias, "mp", other) for other in range(1, shards)]
        return jnp.stack(far, 1)[:, :, None, :]

    def hidden_sums(self, sums):
        shards = lax.axis_size("mp")
        me = lax.axis_index("mp")
        return jnp.concatenate([lax.dynamic_slice_in_dim(sums[:, 0], me ^ at, 1, 0) for at in range(shards)])

    def add_rows(self, keep, send, first, second):
        size = keep.shape[1] // 4
        terms = [keep, swap(send, "dp", 1)]
        for bit, start in ((first, 2 * size), (second, size)):
            out = sum(term[:, start:2 * start].astype(F32) for term in terms).astype(BF16)
            terms.append(swap(out, "dp", bit))
        return [term[:, :size] for term in terms]

    def add_hidden(self, terms):
        shards = terms[0].shape[0]
        parts = [sum(term[at].astype(F32) for term in terms) for at in range(shards)]
        return parts[0] + sum(swap(parts[at].astype(BF16), "mp", at).astype(F32) for at in range(1, shards))

    def add_columns(self, terms):
        shards = lax.axis_size("mp")
        me = lax.axis_index("mp")
        share = terms[0].shape[-1] // shards
        whole = sum(term.astype(F32) for term in terms)
        parts = [lax.dynamic_slice_in_dim(whole, (me ^ at) * share, share, 2) for at in range(shards)]
        return parts[0] + sum(swap(parts[at].astype(BF16), "mp", at).astype(F32) for at in range(1, shards))

    def add_feed(self, keep, send, kind):
        return self.add_hidden(self.add_rows(keep, send, *((2, 4), (4, 2))[kind]))

    def add_attend(self, keep, send, kind):
        return self.add_columns(self.add_rows(keep, send, *((2, 4), (4, 2))[kind]))


class Anywhere:
    orders = ((0, 1), (0, 1))

    def __init__(self):
        self.blocks = jnp.arange(2, dtype=jnp.int32)

    def gather(self, w_up, w_down):
        shards = lax.axis_size("mp")
        made = []
        for layer in range(w_up.shape[0]):
            arrays = [lax.all_gather(w_up[layer], "mp"), lax.all_gather(w_down[layer], "mp")]
            plan = [(kind, at, kind, at, None) for kind in range(2) for at in range(shards)]
            made.append(Pieces(arrays, plan, self.blocks, 0))
        return made

    def order_hidden(self, bias):
        return lax.all_gather(bias, "mp", axis=1)[:, :, None, :]

    def hidden_sums(self, sums):
        return sums[:, 0]

    def add_feed(self, keep, send, kind):
        whole = jnp.concatenate([keep, send], 1)
        whole = lax.psum_scatter(whole, "mp", scatter_dimension=0, tiled=True)
        return lax.psum_scatter(whole[0].astype(F32), "dp", scatter_dimension=0, tiled=True)

    def add_attend(self, keep, send, kind):
        whole = jnp.concatenate([keep, send], 1)
        whole = lax.psum_scatter(whole, "mp", scatter_dimension=2, tiled=True)
        return lax.psum_scatter(whole.astype(F32), "dp", scatter_dimension=1, tiled=True)


def shards(inputs, slot_valid, ln1_gain, ln1_bias, w_query, w_key, w_value, w_out, gate_logit,
           ln2_gain, ln2_bias, w_up, b_up, w_down, b_down, cotangent):
    pages, slots, width = inputs.shape
    dp, mp = lax.axis_size("dp"), lax.axis_size("mp")
    way = Eighths() if dp == 8 and mp == 4 and width % (16 * dp) == 0 else Anywhere()
    blocks, orders = way.blocks, way.orders

    own_valid = lax.dynamic_slice_in_dim(slot_valid, lax.axis_index("mp") * pages, pages, 0) == 1
    key_text = lax.broadcasted_iota(jnp.int32, (slots, slots), 0) < TEXT
    query_text = lax.broadcasted_iota(jnp.int32, (slots, slots), 1) < TEXT
    live = jnp.broadcast_to(own_valid[:, :, None], (pages, slots, slots))
    masks = [
        jnp.where(jnp.logical_and(live, (key_text != query_text)[None]), 0.0, -1e30).astype(F32),
        jnp.where(live, 0.0, -1e30).astype(F32),
    ]
    gate = gate_logit[None]
    pieces = way.gather(w_up, w_down)
    hidden_bias = way.order_hidden(b_up)
    forward_weights = (w_query, w_key, w_value, w_out)
    backward_weights = (w_query, w_key, w_value, w_out)

    resid = inputs.reshape(pages * slots, width)
    kept = []
    for layer in range(2):
        crossed = layer == 0
        q, k, v, p, context, mixed, *branch = attend(
            layer, crossed, resid, masks[layer], ln1_gain, ln1_bias, gate, forward_weights)
        result, active, slope = feed(
            layer, mixed, ln2_gain, ln2_bias, hidden_bias[layer], b_down, pieces[layer], F32 if crossed else BF16)
        kept.append((resid, (q, k, v, p, context, *branch), mixed, active, slope))
        resid = result

    grad = cotangent.reshape(pages * slots, width)
    feed_grads, attend_grads, sums = [None] * 2, [None] * 2, [None] * 2
    for layer in (1, 0):
        crossed = layer == 0
        before, saved, mixed, active, slope = kept[layer]
        grad, up_keep, up_send, down_keep, down_send, feed_sums, up_sums = feed_back(
            layer, grad, mixed, ln2_gain, ln2_bias, active, slope, pieces[layer], orders)
        down_grad = way.add_feed(down_keep, down_send, 1)
        up_grad = way.add_feed(up_keep, up_send, 0)
        grad, first_keep, first_send, second_keep, second_send, attend_sums = attend_back(
            layer, crossed, grad, before, ln1_gain, ln1_bias, gate, saved, backward_weights, blocks, orders)
        first = way.add_attend(first_keep, first_send, 0)
        second = way.add_attend(second_keep, second_send, 1)
        feed_grads[layer] = (up_grad, down_grad.T)
        attend_grads[layer] = (first[0], first[1], second[0], second[1])
        sums[layer] = jnp.concatenate([feed_sums, attend_sums, way.hidden_sums(up_sums)])

    both = lax.psum(jnp.concatenate(sums), ("dp", "mp"))
    lines = width // dp
    mine = lax.dynamic_slice_in_dim(both, lax.axis_index("dp") * lines, lines, 1)
    early = sums[0].shape[0]
    pick = lambda first, second: jnp.stack([mine[first], mine[early + second]])
    me = lax.axis_index("mp")
    bup_grad = jnp.concatenate([
        lax.dynamic_slice_in_dim(both, 6 + me, 1, 0), lax.dynamic_slice_in_dim(both, early + 5 + me, 1, 0)])
    pairs = [jnp.stack([attend_grads[0][at], attend_grads[1][at]]) for at in range(4)]
    return (
        resid.reshape(pages, slots, width),
        grad.reshape(pages, slots, width),
        pick(3, 3),
        pick(4, 4),
        pairs[0],
        pairs[1],
        pairs[2],
        pairs[3],
        mine[5],
        pick(1, 1),
        pick(2, 2),
        jnp.stack([feed_grads[0][0], feed_grads[1][0]]),
        bup_grad,
        jnp.stack([feed_grads[0][1], feed_grads[1][1]]),
        pick(0, 0),
    )


def solution(mesh):
    rows = P(("dp", "mp"), None, None)
    return jax.shard_map(
        shards,
        mesh=mesh,
        in_specs=(rows, P("dp", None), P(), P(), P(), P(), P(), P(), P(), P(), P(), P(None, None, "mp"),
                  P(None, "mp"), P(None, "mp", None), P(), rows),
        out_specs=(rows, rows, P(None, "dp"), P(None, "dp"), P(None, "dp", "mp"), P(None, "dp", "mp"),
                   P(None, "dp", "mp"), P(None, "dp", "mp"), P("dp"), P(None, "dp"), P(None, "dp"),
                   P(None, "dp", "mp"), P(None, "mp"), P(None, "mp", "dp"), P(None, "dp")),
        check_vma=False,
    )
```

```python
import functools

import jax
import jax.numpy as jnp
from jax import lax
from jax.experimental import pallas as pl
from jax.experimental.pallas import tpu as pltpu
from jax.sharding import PartitionSpec as P

HEADS = 12
TEXT = 112
F32 = jnp.float32
BF16 = jnp.bfloat16
VMEM_BYTES = 56 * 2**20


def dot(a, b, a_dim, b_dim):
    return lax.dot_general(a, b, (((a_dim,), (b_dim,)), ((), ())), preferred_element_type=F32)


def whiten(rows):
    centered = rows - jnp.mean(rows, axis=-1, keepdims=True)
    spread = jnp.mean(centered * centered, axis=-1, keepdims=True)
    inverse = lax.rsqrt(spread + 1e-05)
    return centered * inverse, inverse


def whiten_back(white, inverse, gain, grad):
    scaled = grad * gain
    first = jnp.mean(scaled, axis=-1, keepdims=True)
    second = jnp.mean(scaled * white, axis=-1, keepdims=True)
    return inverse * (scaled - first - white * second)


def column_sum(rows):
    return jnp.sum(rows, axis=0, keepdims=True)


def gelu_and_slope(values):
    size = jnp.abs(values)
    t = 1.0 / (1.0 + (0.3275911 * 0.7071067811865476) * size)
    bell = jnp.exp(-0.5 * values * values)
    poly = 0.5 * 1.061405429
    poly = poly * t + 0.5 * -1.453152027
    poly = poly * t + 0.5 * 1.421413741
    poly = poly * t + 0.5 * -0.284496736
    poly = poly * t + 0.5 * 0.254829592
    tail = poly * t * bell
    phi = jnp.where(values >= 0.0, 1.0 - tail, tail)
    return values * phi, phi + values * bell * 0.3989422804014327


def split_heads(pair):
    lane = lax.broadcasted_iota(jnp.int32, pair.shape, 1)
    first = lane < pair.shape[1] // 2
    zero = jnp.zeros_like(pair)
    return jnp.concatenate([jnp.where(first, pair, zero), jnp.where(first, zero, pair)], axis=0)


def join_heads(both):
    slots = both.shape[0] // 2
    lane = lax.broadcasted_iota(jnp.int32, (slots, both.shape[1]), 1)
    return jnp.where(lane < both.shape[1] // 2, both[:slots], both[slots:])


def start_copies(sources, targets, sems):
    copies = [
        pltpu.make_async_copy(source, target, sems.at[at])
        for at, (source, target) in enumerate(zip(sources, targets))
    ]
    for copy in copies:
        copy.start()
    return copies


def attend_kernel(layer, crossed, resid, mask, gain, shift, gate, wq, wk, wv, wo,
                  q_out, k_out, v_out, p_out, c_out, mixed, branch_out, held, sems):
    pages, slots = mask.shape[0], mask.shape[1]
    width = resid.shape[1]
    pairs = HEADS // 2
    pair_width = width // pairs
    scale = 1.0 / (width // HEADS) ** 0.5
    copies = start_copies(
        [w.at[layer] for w in (wq, wk, wv, wo)], [held.at[at] for at in range(4)], sems
    )
    white, _ = whiten(resid[...].astype(F32))
    normed = (white * gain[layer:layer + 1] + shift[layer:layer + 1]).astype(BF16)
    copies[0].wait()
    q_out[...] = (dot(normed, held[0], 1, 0).astype(BF16).astype(F32) * scale).astype(BF16)
    copies[1].wait()
    k_out[...] = dot(normed, held[1], 1, 0).astype(BF16)
    copies[2].wait()
    v_out[...] = dot(normed, held[2], 1, 0).astype(BF16)

    for page in range(pages):
        rows = slice(page * slots, (page + 1) * slots)
        bias = mask[page]
        for pair in range(pairs):
            cols = slice(pair * pair_width, (pair + 1) * pair_width)
            scores = dot(split_heads(k_out[rows, cols]), q_out[rows, cols], 1, 1)
            scores = scores.reshape(2, slots, slots) + bias[None]
            top = jnp.max(scores, axis=1, keepdims=True)
            raised = jnp.exp(scores - top)
            probs = raised * (1.0 / jnp.sum(raised, axis=1, keepdims=True))
            probs = probs.reshape(2 * slots, slots).astype(BF16)
            p_out[page, pair] = probs
            c_out[rows, cols] = dot(probs, split_heads(v_out[rows, cols]), 0, 0).astype(BF16)
    copies[3].wait()
    branch = dot(c_out[...], held[3], 1, 0)
    if crossed:
        branch_out[...] = branch.astype(BF16)
        branch = branch * jax.nn.sigmoid(gate[...])
    mixed[...] = resid[...].astype(F32) + branch


def attend(layer, crossed, resid, mask, gain, shift, gate, weights, ties):
    rows, width = resid.shape
    pages, slots = mask.shape[:2]
    low = jax.ShapeDtypeStruct((rows, width), BF16)
    vmem = pl.BlockSpec(memory_space=pltpu.VMEM)
    outs = [low, low, low, jax.ShapeDtypeStruct((pages, HEADS // 2, 2 * slots, slots), BF16), low,
            jax.ShapeDtypeStruct((rows, width), F32)]
    if crossed:
        outs.append(low)

    def body(*refs):
        ins, rest = refs[:9], list(refs[9 + len(ties):])
        if not crossed:
            rest.insert(6, None)
        attend_kernel(layer, crossed, *ins, *rest)

    return pl.pallas_call(
        body,
        out_shape=outs,
        in_specs=[vmem] * 5 + [pl.BlockSpec(memory_space=pl.ANY)] * (4 + len(ties)),
        out_specs=[vmem] * len(outs),
        scratch_shapes=[pltpu.VMEM((4, width, width), BF16), pltpu.SemaphoreType.DMA((4,))],
        compiler_params=pltpu.CompilerParams(vmem_limit_bytes=VMEM_BYTES),
        cost_estimate=pl.CostEstimate(flops=8 * rows * width * width, bytes_accessed=14 * 2**20, transcendentals=0),
    )(resid, mask, gain, shift, gate, *weights, *ties)


class Pieces:
    def __init__(self, arrays, plan, blocks, piece_rows, tails):
        self.tails = tails
        self.arrays, self.plan, self.blocks, self.piece_rows = arrays, plan, blocks, piece_rows

    def copies(self, refs, held, blocks, sems, shard):
        made = []
        for at, (array, index, kind, owner, place) in enumerate(self.plan):
            if owner != shard:
                continue
            if place is None:
                target = held[kind].at[shard]
            elif isinstance(place, slice):
                target = held[kind].at[shard, place]
            else:
                start = pl.multiple_of(blocks[place] * self.piece_rows, self.piece_rows)
                target = held[kind].at[shard, pl.ds(start, self.piece_rows)]
            source = index(refs[array], blocks) if callable(index) else refs[array].at[index]
            made.append(pltpu.make_async_copy(source, target, sems.at[at]))
        return made

    def tail_specs(self, width):
        return [pl.BlockSpec((16, width), lambda step, last=tail.shape[0] // 16 - 1: (last, 0)) for tail in self.tails]

    def start_and_wait(self, refs, held, blocks, sems, shards):
        step = pl.program_id(0)

        @pl.when(step == 0)
        def _():
            for shard in range(shards):
                for copy in self.copies(refs, held, blocks, sems, shard):
                    copy.start()

        def wait():
            for shard in range(shards):
                @pl.when(step == shard)
                def _():
                    for copy in self.copies(refs, held, blocks, sems, shard):
                        copy.wait()
        return wait


def feed_kernel(layer, pieces, ties, blocks, mixed, gain, shift, b_down, *rest):
    count = len(pieces.arrays)
    tails, rest = rest[:len(pieces.tails)], rest[len(pieces.tails):]
    refs, rest = rest[:count], rest[count + ties:]
    result, active_out, slope_out, up, down, low, total, bias, sems = rest
    shards, width = up.shape[0], up.shape[2]
    step = pl.program_id(0)
    wait = pieces.start_and_wait(refs, (up, down), blocks, sems, shards)

    @pl.when(step == 0)
    def _():
        white, _ = whiten(mixed[...])
        low[...] = (white * gain[layer:layer + 1] + shift[layer:layer + 1]).astype(BF16)
        total[...] = mixed[...] + b_down[layer:layer + 1]
        for at, tail in enumerate(tails):
            bias[at] = column_sum(tail[...].astype(F32))

    wait()
    parts = 3
    part = width // parts
    for at in range(parts):
        cols = slice(at * part, (at + 1) * part)
        upper = dot(low[...], up[step, :, cols], 1, 0) + bias[step, :, cols]
        active, slope = gelu_and_slope(upper)
        active = active.astype(BF16)
        active_out[0, :, cols] = active
        slope_out[0, :, cols] = slope.astype(BF16)
        total[...] += dot(active, down[step, cols, :], 1, 0)

    @pl.when(step == shards - 1)
    def _():
        result[...] = total[...].astype(result.dtype)


def feed(layer, mixed, gain, shift, b_down, pieces, out_type, ties):
    rows, width = mixed.shape
    shards = len(pieces.tails)
    whole = lambda shape: pl.BlockSpec(shape, lambda step: (0,) * len(shape))
    each = lambda shape: pl.BlockSpec((1,) + shape, lambda step: (step,) + (0,) * len(shape))
    return pl.pallas_call(
        functools.partial(feed_kernel, layer, pieces, len(ties)),
        grid=(shards,),
        out_shape=[jax.ShapeDtypeStruct((rows, width), out_type)]
        + [jax.ShapeDtypeStruct((shards, rows, width), BF16)] * 2,
        in_specs=[pl.BlockSpec(memory_space=pltpu.SMEM), whole((rows, width)), whole(gain.shape), whole(shift.shape),
                  whole(b_down.shape)] + pieces.tail_specs(width)
        + [pl.BlockSpec(memory_space=pl.ANY)] * (len(pieces.arrays) + len(ties)),
        out_specs=[whole((rows, width)), each((rows, width)), each((rows, width))],
        scratch_shapes=[pltpu.VMEM((shards, width, width), BF16), pltpu.VMEM((shards, width, width), BF16),
                        pltpu.VMEM((rows, width), BF16), pltpu.VMEM((rows, width), F32),
                        pltpu.VMEM((shards, 1, width), F32), pltpu.SemaphoreType.DMA((len(pieces.plan),))],
        compiler_params=pltpu.CompilerParams(vmem_limit_bytes=VMEM_BYTES),
        cost_estimate=pl.CostEstimate(flops=16 * rows * width * width, bytes_accessed=20 * 2**20, transcendentals=0),
    )(pieces.blocks, mixed, gain, shift, b_down, *pieces.tails, *pieces.arrays, *ties)


ROWS_FIRST = ((0, 4, 2, 6, 1, 5, 3, 7), (0, 2, 4, 6, 1, 3, 5, 7))
PART_ORDERS = (0, 1, 0)
PART_STAGES = ("xyvu", "yuxv", "uxyv")
SHARD_ORDER = (0, 2, 1, 3)
LINKS = {"c": ("dp", 1), "x": ("dp", 2), "y": ("dp", 4), "u": ("mp", 1), "v": ("mp", 2), "w": ("mp", 3)}


def turn_rows(held, turned, blocks, order):
    if order is None:
        turned[...] = held[...]
        return
    size = held.shape[0] // len(order)
    for at, place in enumerate(order):
        start = pl.multiple_of(blocks[place] * size, size)
        turned[at * size:(at + 1) * size] = held[pl.ds(start, size)]


def put_blocks(made, keep, keep_at, send, send_at):
    rows = made.shape[0] // 8
    for half, (out, place) in enumerate(((keep, keep_at), (send, send_at))):
        for first in range(2):
            for second in range(2):
                at = (4 * half + 2 * first + second) * rows
                out[place(first, second)] = made[at:at + rows]


def feed_back_kernel(layer, pieces, joint, ties, blocks, grad_out, mixed, gain, shift, active, slope, *rest):
    count = len(pieces.arrays)
    refs, rest = rest[:count], rest[count + ties:]
    grads_count = 1 if joint else 4
    grad_mixed, sums, up_sums, *grads = rest[:3 + grads_count]
    up, down, low, low_turned, normed_turned, held, total, sems, *leaving = rest[3 + grads_count:]
    shards, width = up.shape[0], up.shape[2]
    part = width // 3
    step = pl.program_id(0)
    wait = pieces.start_and_wait(refs, (up, down), blocks, sems, shards)

    def put(kind, turned, right):
        if joint:
            grads[0][0, kind] = dot(turned[0], right, 1, 0).astype(BF16)
            return
        for at in range(3):
            made = dot(turned[PART_ORDERS[at]], right[:, at * part:(at + 1) * part], 1, 0).astype(BF16)
            place = ((lambda first, second: (first, second, 0, 0, kind)), (lambda first, second: (first, 0, second, 0, kind)),
                     (lambda first, second: (0, first, second, 0, kind)))[at]
            put_blocks(made, grads[at], place, leaving[0], lambda first, second: (step % 2, at, first, second, kind))

    def leave(step, at):
        place = ((at, slice(None), slice(None), step % 2, step // 2), (at, slice(None), step // 2, slice(None), step % 2),
                 (at, step // 2, slice(None), slice(None), step % 2))[at]
        return pltpu.make_async_copy(leaving[0].at[step % 2, at], grads[3].at[place], leaving[1].at[step % 2, at])

    if not joint:
        @pl.when(step >= 2)
        def _():
            for at in range(3):
                leave(step - 2, at).wait()

    @pl.when(step == 0)
    def _():
        rows = grad_out[...].astype(F32)
        low[...] = rows.astype(BF16)
        sums[...] = jnp.zeros_like(sums)
        sums[0:1] = column_sum(rows)
        white, _ = whiten(mixed[...])
        normed = (white * gain[layer:layer + 1] + shift[layer:layer + 1]).astype(BF16)
        for value, turned in ((low[...], low_turned), (normed, normed_turned)):
            held[...] = value.T
            for at in range(turned.shape[0]):
                turn_rows(held, turned.at[at], blocks, None if joint else ROWS_FIRST[at])
        total[...] = jnp.zeros_like(total)

    wait()
    put(1, low_turned, active[0])
    upper = dot(low[...], down[step], 1, 1) * slope[0].astype(F32)
    up_sums[0] = column_sum(upper)
    upper_low = upper.astype(BF16)
    put(0, normed_turned, upper_low)
    if not joint:
        for at in range(3):
            leave(step, at).start()
    total[...] += dot(upper_low, up[step], 1, 1)

    @pl.when(step == shards - 1)
    def _():
        white, inverse = whiten(mixed[...])
        grad = total[...]
        sums[1:2] = column_sum(grad * white)
        sums[2:3] = column_sum(grad)
        grad_mixed[...] = grad_out[...].astype(F32) + whiten_back(white, inverse, gain[layer:layer + 1], grad)
        if not joint:
            for before in (1, 0):
                for at in range(3):
                    leave(step - before, at).wait()


def feed_back(layer, grad_out, mixed, gain, shift, active, slope, pieces, joint, ties):
    rows, width = mixed.shape
    shards = active.shape[0]
    whole = lambda shape: pl.BlockSpec(shape, lambda step: (0,) * len(shape))
    each = lambda shape: pl.BlockSpec((1,) + shape, lambda step: (step,) + (0,) * len(shape))
    if joint:
        grads, specs = [jax.ShapeDtypeStruct((shards, 2, width, width), BF16)], [each((2, width, width))]
        leaving = []
    else:
        tile = (width // 8, width // 3)
        grads = [jax.ShapeDtypeStruct((2,) * 5 + tile, BF16)] * 3 + [jax.ShapeDtypeStruct((3,) + (2,) * 5 + tile, BF16)]
        leaving = [pltpu.VMEM((2, 3, 2, 2, 2) + tile, BF16), pltpu.SemaphoreType.DMA((2, 3))]
        specs = [
            pl.BlockSpec((2, 2, 1, 1, 2) + tile, lambda step: (0, 0, step % 2, step // 2, 0, 0, 0)),
            pl.BlockSpec((2, 1, 2, 1, 2) + tile, lambda step: (0, step // 2, 0, step % 2, 0, 0, 0)),
            pl.BlockSpec((1, 2, 2, 1, 2) + tile, lambda step: (step // 2, 0, 0, step % 2, 0, 0, 0)),
            pl.BlockSpec(memory_space=pl.ANY),
        ]
    turned = pltpu.VMEM((1 if joint else 2, width, rows), BF16)
    return pl.pallas_call(
        functools.partial(feed_back_kernel, layer, pieces, joint, len(ties)),
        grid=(shards,),
        out_shape=[jax.ShapeDtypeStruct((rows, width), F32), jax.ShapeDtypeStruct((8, width), F32),
                   jax.ShapeDtypeStruct((shards, 1, width), F32)] + grads,
        in_specs=[pl.BlockSpec(memory_space=pltpu.SMEM), whole((rows, width)), whole((rows, width)), whole(gain.shape),
                  whole(shift.shape), each((rows, width)), each((rows, width))]
        + [pl.BlockSpec(memory_space=pl.ANY)] * (len(pieces.arrays) + len(ties)),
        out_specs=[whole((rows, width)), whole((8, width)), each((1, width))] + specs,
        scratch_shapes=[pltpu.VMEM((shards, width, width), BF16), pltpu.VMEM((shards, width, width), BF16),
                        pltpu.VMEM((rows, width), BF16), turned, turned, pltpu.VMEM((width, rows), BF16),
                        pltpu.VMEM((rows, width), F32), pltpu.SemaphoreType.DMA((len(pieces.plan),))] + leaving,
        compiler_params=pltpu.CompilerParams(vmem_limit_bytes=VMEM_BYTES),
        cost_estimate=pl.CostEstimate(flops=32 * rows * width * width, bytes_accessed=30 * 2**20, transcendentals=0),
    )(pieces.blocks, grad_out, mixed, gain, shift, active, slope, *pieces.arrays, *ties)


def attend_back_kernel(layer, crossed, joint, blocks, grad_mixed, resid, gain, shift, gate, q, k, v, p, context, branch,
                       wq, wk, wv, wo, grad_resid, sums, grads,
                       held, turning, turned, gc, gq, gk, gv, sems):
    pages, slots = p.shape[0], p.shape[3]
    width = resid.shape[1]
    pairs = HEADS // 2
    pair_width = width // pairs
    scale = 1.0 / (width // HEADS) ** 0.5
    copies = start_copies(
        [w.at[layer] for w in (wo, wq, wk, wv)], [held.at[at] for at in range(4)], sems
    )
    sums[...] = jnp.zeros_like(sums)

    def put(at, right):
        made = dot(turned[...], right, 1, 0).astype(BF16)
        if joint:
            grads[0][at] = made
            return
        tile = width // 3
        for col in range(3):
            put_blocks(made[:, col * tile:(col + 1) * tile], grads[at // 2], lambda first, second: (first, second, at % 2, col),
                       grads[2], lambda first, second: (at // 2, first, second, at % 2, col))

    def turn(rows, order):
        turning[...] = rows.T
        turn_rows(turning, turned, blocks, None if joint else ROWS_FIRST[order])

    grad = grad_mixed[...]
    if crossed:
        opened = jax.nn.sigmoid(gate[...])
        sums[2:3] = column_sum(grad * branch[...].astype(F32)) * (opened * (1.0 - opened))
        low = (grad * opened).astype(BF16)
    else:
        low = grad.astype(BF16)
    turn(context[...], 1)
    put(3, low)
    copies[0].wait()
    gc[...] = dot(low, held[0], 1, 1).astype(BF16)

    for page in range(pages):
        rows = slice(page * slots, (page + 1) * slots)
        for pair in range(pairs):
            cols = slice(pair * pair_width, (pair + 1) * pair_width)
            probs_low = p[page, pair]
            probs = probs_low.astype(F32).reshape(2, slots, slots)
            grad_probs = dot(split_heads(v[rows, cols]), gc[rows, cols], 1, 1).reshape(2, slots, slots)
            delta = jnp.sum(probs * grad_probs, axis=1, keepdims=True)
            grad_scores = (probs * (grad_probs - delta)).astype(BF16).reshape(2 * slots, slots)
            gq[rows, cols] = (dot(grad_scores, split_heads(k[rows, cols]), 0, 0) * scale).astype(BF16)
            gk[rows, cols] = join_heads(dot(grad_scores, q[rows, cols], 1, 0)).astype(BF16)
            gv[rows, cols] = join_heads(dot(probs_low, gc[rows, cols], 1, 0)).astype(BF16)

    white, inverse = whiten(resid[...].astype(F32))
    normed = (white * gain[layer:layer + 1] + shift[layer:layer + 1]).astype(BF16)
    turn(normed, 1)
    put(2, gv[...])
    if not joint:
        turn_rows(turning, turned, blocks, ROWS_FIRST[0])
    put(0, gq[...])
    put(1, gk[...])
    for copy in copies[1:]:
        copy.wait()
    total = dot(gq[...], held[1], 1, 1) + dot(gk[...], held[2], 1, 1) + dot(gv[...], held[3], 1, 1)
    sums[0:1] = column_sum(total * white)
    sums[1:2] = column_sum(total)
    grad_resid[...] = grad + whiten_back(white, inverse, gain[layer:layer + 1], total)


def attend_back(layer, crossed, grad_mixed, resid, gain, shift, gate, kept, weights, blocks, joint, ties):
    rows, width = resid.shape
    vmem = pl.BlockSpec(memory_space=pltpu.VMEM)
    kept = list(kept)
    given = 6 + len(kept) + 4
    if joint:
        grads = [jax.ShapeDtypeStruct((4, width, width), BF16)]
    else:
        shape = (2, 2, 2, 3, width // 8, width // 3)
        grads = [jax.ShapeDtypeStruct(shape, BF16)] * 2 + [jax.ShapeDtypeStruct((2,) + shape, BF16)]

    def body(*refs):
        ins, rest = list(refs[:given]), refs[given + len(ties):]
        if not crossed:
            ins.insert(11, None)
        attend_back_kernel(layer, crossed, joint, *ins, *rest[:2], rest[2:2 + len(grads)], *rest[2 + len(grads):])

    low = pltpu.VMEM((rows, width), BF16)
    return pl.pallas_call(
        body,
        out_shape=[jax.ShapeDtypeStruct((rows, width), F32), jax.ShapeDtypeStruct((8, width), F32)] + grads,
        in_specs=[pl.BlockSpec(memory_space=pltpu.SMEM)] + [vmem] * (5 + len(kept))
        + [pl.BlockSpec(memory_space=pl.ANY)] * (4 + len(ties)),
        out_specs=[vmem] * (2 + len(grads)),
        scratch_shapes=[pltpu.VMEM((4, width, width), BF16), pltpu.VMEM((width, rows), BF16),
                        pltpu.VMEM((width, rows), BF16), low, low, low, low, pltpu.SemaphoreType.DMA((4,))],
        compiler_params=pltpu.CompilerParams(vmem_limit_bytes=VMEM_BYTES),
        cost_estimate=pl.CostEstimate(flops=16 * rows * width * width, bytes_accessed=24 * 2**20, transcendentals=0),
    )(blocks, grad_mixed, resid, gain, shift, gate, *kept, *weights, *ties)


def pack_kernel(layers, rows, block, bias, w_up, w_down, *rest):
    outs, sems = rest[:layers], rest[layers]
    start = pl.multiple_of(block[0] * rows, rows)
    sources = [w.at[layer, pl.ds(start, rows)] for layer in range(layers) for w in (w_up, w_down)]
    targets = [out.at[pl.ds(kind * rows, rows)] for out in outs for kind in range(2)]
    copies = start_copies(sources, targets, sems)
    for layer, out in enumerate(outs):
        out[2 * rows:] = bias_terms(bias[layer:layer + 1])
    for copy in copies:
        copy.wait()


def bias_terms(bias):
    top = bias.astype(BF16)
    left = bias - top.astype(F32)
    middle = left.astype(BF16)
    bottom = (left - middle.astype(F32)).astype(BF16)
    row = lax.broadcasted_iota(jnp.int32, (16, bias.shape[1]), 0)
    terms = [jnp.broadcast_to(term.astype(F32), row.shape) for term in (top, middle, bottom)]
    zero = jnp.zeros(row.shape, F32)
    chosen = jnp.where(row == 0, terms[0], jnp.where(row == 1, terms[1], jnp.where(row == 2, terms[2], zero)))
    return chosen.astype(BF16)


def pack(w_up, w_down, b_up, block):
    layers, width, shard = w_up.shape
    rows = width // 8
    out = jax.ShapeDtypeStruct((2 * rows + 16, shard), BF16)
    vmem = pl.BlockSpec(memory_space=pltpu.VMEM)
    return pl.pallas_call(
        functools.partial(pack_kernel, layers, rows),
        out_shape=[out] * layers,
        in_specs=[pl.BlockSpec(memory_space=pltpu.SMEM), vmem] + [pl.BlockSpec(memory_space=pl.ANY)] * 2,
        out_specs=[vmem] * layers,
        scratch_shapes=[pltpu.SemaphoreType.DMA((2 * layers,))],
        cost_estimate=pl.CostEstimate(flops=0, bytes_accessed=4 * layers * rows * shard * 4, transcendentals=0),
    )(block, b_up, w_up, w_down)


class Chain:
    def __init__(self, token):
        self.token, self.pending = token, []

    def need(self, *places):
        self.pending += places

    def tie(self, *values):
        count = len(values)
        out = lax.optimization_barrier((*values, self.token, *(held[key] for held, key in self.pending)))
        self.token = out[count]
        for (held, key), value in zip(self.pending, out[count + 1:]):
            held[key] = value
        self.pending = []
        return out[0] if count == 1 else out[:count]

    def ties(self):
        out, self.pending = [self.token] + [held[key] for held, key in self.pending], []
        return out


def places(values):
    return [(values, at) for at in range(len(values))]


def swap(value, axis, bit):
    size = lax.axis_size(axis)
    return lax.ppermute(value, axis, [(at, at ^ bit) for at in range(size)])


class Flow:
    def __init__(self, keep, send, place, size, stages):
        self.terms = [(flat(keep), 0)]
        self.send, self.place, self.size, self.stages = flat(send), place, size, stages

    def crossed(self, arrived):
        self.terms.append((arrived, self.place))


def flat(value):
    return value.reshape((-1,) + value.shape[-2:])


def feed_flows(grads):
    *keeps, send = grads
    size = flat(keeps[0]).shape[0]
    return [Flow(keeps[at], send, at * size, size, PART_STAGES[at]) for at in range(3)]


def attend_flows(grads):
    *keeps, send = grads
    size = flat(keeps[0]).shape[0]
    return [Flow(keeps[at], send, at * size, size, stages) for at, stages in enumerate(("xy", "yx"))]


class Reads:
    def __init__(self):
        self.arrays = []

    def at(self, array):
        for at, known in enumerate(self.arrays):
            if known is array:
                return at
        self.arrays.append(array)
        return len(self.arrays) - 1

    def places(self, terms):
        return [(self.at(array), place) for array, place in terms]


def as_block(value):
    tile = value.shape[1] // 3
    parts = [value[:, at * tile:(at + 1) * tile] for at in range(3)]
    return jnp.concatenate(parts + [jnp.zeros_like(parts[0])], axis=0).astype(BF16)


def from_block(block):
    value = block.astype(F32)
    rows = value.shape[0] // 4
    return jnp.concatenate([value[at * rows:(at + 1) * rows] for at in range(3)], axis=1)


def add_small_parts(parts, blocks, out):
    out[...] = jnp.zeros_like(out)
    for layer in range(2):
        fed, attended, up = parts[3 * layer:3 * layer + 3]
        base = 10 * layer
        out[base:base + 3] = fed[0:3]
        out[base + 3:base + 6] = attended[0:3]
        for slot in range(len(SHARD_ORDER)):
            out[pl.ds(base + 6 + blocks[8 + slot], 1)] = up[slot]


def exchange_kernel(plan, blocks, *refs):
    sends, columns, ends, small, small_terms, small_ends, array_count, small_count, tie_count, out_count = plan
    arrays, refs = refs[:array_count], refs[array_count:]
    small_ins, refs = refs[:small_count], refs[small_count + tie_count:]
    outs, refs = refs[:out_count], list(refs[out_count:])
    own = refs.pop(0) if columns else None
    small_out = refs.pop(0) if small == "new" else None
    out_sems, sems = refs.pop(), refs.pop()
    at, groups = 0, []
    wanted = [(size, terms) for _, _, size, terms in sends] + list(columns)
    if small_terms:
        wanted.append((1, small_terms))
    for size, terms in wanted:
        held, waits = refs.pop(0), []
        for term, (array, place) in enumerate(terms):
            waits.append(pltpu.make_async_copy(arrays[array].at[pl.ds(place, size)], held.at[term], sems.at[at]))
            at += 1
        groups.append((waits, held))
    leaving, ahead = [], 3

    def begin(number):
        if number < len(groups):
            for copy in groups[number][0]:
                copy.start()

    for number in range(ahead):
        begin(number)

    def arrive(number):
        for copy in groups[number][0]:
            copy.wait()
        begin(number + ahead)

    def leave(made, out, place, size):
        leaving.append(pltpu.make_async_copy(made, outs[out].at[pl.ds(place, size)], out_sems.at[len(leaving)]))
        leaving[-1].start()

    for number, (out, place, size, terms) in enumerate(sends):
        held, made = groups[number][1], refs.pop(0)
        arrive(number)

        def add(block, carry, held=held, made=made, terms=terms):
            values = [held[term, block] for term in range(len(terms))]
            while len(values) > 1:
                values = [values[at] + values[at + 1] if at + 1 < len(values) else values[at]
                          for at in range(0, len(values), 2)]
            made[block] = values[0]
            return carry

        lax.fori_loop(0, size, add, 0)
        leave(made, out, place, size)
    if columns:
        turned, far = refs.pop(0), refs.pop(0)
        shards = len(SHARD_ORDER)
        share = turned.shape[2] // 4
        for flow, (size, terms) in enumerate(columns):
            held = groups[len(sends) + flow][1]
            arrive(len(sends) + flow)
            for line in range(2):
                parts = []
                for tile in range(size // 2):
                    total = held[0, line * (size // 2) + tile].astype(F32)
                    for term in range(1, len(terms)):
                        total = total + held[term, line * (size // 2) + tile].astype(F32)
                    parts.append(total)
                whole = jnp.concatenate(parts, axis=1)
                to = (2 * flow + line) * share
                for shard in range(shards):
                    turned[shard ^ blocks[8], :, to:to + share] = whole[:, shard * share:(shard + 1) * share]
        own[...] = turned[0]
        tile = far.shape[3]
        for other in range(1, shards):
            for cut in range(3):
                far[other - 1, cut] = turned[other, :, cut * tile:(cut + 1) * tile].astype(BF16)
            leave(far.at[other - 1], *ends[other - 1], 3)
    if small:
        made = refs.pop(0)
        if small == "new":
            add_small_parts(small_ins, blocks, small_out)
            total = small_out[...]
        else:
            total = small_ins[0][...]
            held = groups[-1][1]
            arrive(len(groups) - 1)
            for term in range(len(small_terms)):
                total = total + from_block(held[term, 0])
        made[0] = as_block(total)
        for out, place in small_ends:
            leave(made, out, place, 1)
    for copy in leaving:
        copy.wait()


class Rounds:
    def __init__(self, blocks):
        self.blocks, self.arrived = blocks, []

    def exchange(self, flows, ending=(), small=None, ties=(), crossing=()):
        reads, sends, sizes = Reads(), [], {}

        def room(letter, size):
            place = sizes.get(letter, 0)
            sizes[letter] = place + size
            return list(sizes).index(letter), place

        moved = []
        for flow in flows:
            letter, flow.stages = flow.stages[0], flow.stages[1:]
            flow.size //= 2
            out, place = room(letter, flow.size)
            for cut in range(0, flow.size, 8):
                sends.append((out, place + cut, min(8, flow.size - cut),
                              [(reads.at(array), start + flow.size + cut) for array, start in flow.terms]))
            moved.append((flow.terms, letter, place))
        tile = flat(flows[0].terms[0][0]).shape[1:]
        width = 3 * tile[1]
        columns = [(flow.size, reads.places(flow.terms)) for pair in ending for flow in pair]
        ends = [room(letter, 3) for letter in "uvw"] if columns else []
        mode, small_terms, small_ins, small_ends = "", [], [], []
        if small is not None:
            mode, letters = small.next()
            small_ins = small.parts if mode == "new" else [small.own]
            small_terms = [] if mode == "new" else reads.places(small.terms)
            small_ends = [room(letter, 1) for letter in letters]
        order = list(sizes)
        outs = [jax.ShapeDtypeStruct((sizes[letter],) + tile, BF16) for letter in order]
        held = [pltpu.VMEM((len(terms), size) + tile, BF16) for _, _, size, terms in sends]
        held += [pltpu.VMEM((len(terms), size) + tile, BF16) for size, terms in columns]
        if small_terms:
            held.append(pltpu.VMEM((len(small_terms), 1) + tile, BF16))
        held += [pltpu.VMEM((size,) + tile, BF16) for _, _, size, _ in sends]
        more = []
        if columns:
            held += [pltpu.VMEM((len(SHARD_ORDER), tile[0], width), F32), pltpu.VMEM((3, 3) + tile, BF16)]
            more.append(jax.ShapeDtypeStruct((tile[0], width), F32))
        if mode:
            held.append(pltpu.VMEM((1,) + tile, BF16))
        if mode == "new":
            more.append(jax.ShapeDtypeStruct((24, width), F32))
        ties = [*self.arrived, *ties]
        copies = sum(len(terms) for *_, terms in sends) + sum(len(terms) for _, terms in columns) + len(small_terms)
        anywhere, vmem = pl.BlockSpec(memory_space=pl.ANY), pl.BlockSpec(memory_space=pltpu.VMEM)
        plan = (sends, columns, ends, mode, small_terms, small_ends, len(reads.arrays), len(small_ins), len(ties), len(outs))
        made = pl.pallas_call(
            functools.partial(exchange_kernel, plan),
            out_shape=outs + more,
            in_specs=[pl.BlockSpec(memory_space=pltpu.SMEM)] + [anywhere] * len(reads.arrays) + [vmem] * len(small_ins)
            + [anywhere] * len(ties),
            out_specs=[anywhere] * len(outs) + [vmem] * len(more),
            scratch_shapes=held + [pltpu.SemaphoreType.DMA((copies,)),
                                   pltpu.SemaphoreType.DMA((len(sends) + len(ends) + len(small_ends),))],
            compiler_params=pltpu.CompilerParams(vmem_limit_bytes=VMEM_BYTES),
        )(self.blocks, *reads.arrays, *small_ins, *ties)
        made = list(made)
        rest = made[len(outs):]
        self.made = made[:len(outs)]
        going = self.made + [flows[0].send for flows in crossing]
        going = lax.optimization_barrier(going)
        arrived = {letter: swap(value, *LINKS[letter]) for letter, value in zip(order, going)}
        self.arrived = list(arrived.values())
        for flows, send in zip(crossing, going[len(outs):]):
            self.arrived.append(swap(send, *LINKS["c"]))
            for flow in flows:
                flow.crossed(self.arrived[-1])
        for terms, letter, place in moved:
            terms.append((arrived[letter], place))
        for pair in ending:
            pair[0].own = rest.pop(0)
            pair[0].far = [(arrived[letter], place) for letter, (_, place) in zip("uvw", ends)]
        if mode:
            if mode == "new":
                small.own = rest.pop(0)
            small.terms += [(arrived[letter], place) for letter, (_, place) in zip(letters, small_ends)]

    def cross(self, flows):
        arrived = swap(flows[0].send, *LINKS["c"])
        for flow in flows:
            flow.crossed(arrived)
        self.arrived.append(arrived)


class Small:
    def __init__(self, parts):
        self.parts, self.terms, self.stages = parts, [], ["c", "x", "y", "uvw"]

    def next(self):
        letters = self.stages.pop(0)
        return ("new" if letters == "c" else "old"), letters


def finish_kernel(plan, array_count, *refs):
    feeds, far, small = plan
    arrays, refs = refs[:array_count], refs[array_count:]
    owns, small_own, refs = refs[:2], refs[2], refs[3:]
    up, down, *attends, both = refs[:7]
    held, held_far, held_small, sems = refs[7:]
    copies = []

    def fetch(array, place, size, target):
        copies.append(pltpu.make_async_copy(arrays[array].at[pl.ds(place, size)], target, sems.at[len(copies)]))
        copies[-1].start()

    for layer, part, term, array, place in feeds:
        fetch(array, place, 2, held.at[layer, part, term])
    for layer, other, array, place in far:
        fetch(array, place, 3, held_far.at[layer, other])
    for term, (array, place) in enumerate(small):
        fetch(array, place, 1, held_small.at[term])
    for copy in copies:
        copy.wait()
    terms, tile = held.shape[2], held.shape[5]
    for layer in range(2):
        for part in range(3):
            total = held[layer, part, 0].astype(F32)
            for term in range(1, terms):
                total = total + held[layer, part, term].astype(F32)
            up[layer, :, part * tile:(part + 1) * tile] = total[0]
            down[layer, part * tile:(part + 1) * tile, :] = total[1].T
        total = owns[layer][...]
        for other in range(3):
            total = total + jnp.concatenate([held_far[layer, other, cut].astype(F32) for cut in range(3)], axis=1)
        share = total.shape[1] // 4
        for at, out in enumerate(attends):
            out[layer] = total[:, at * share:(at + 1) * share]
    total = small_own[...]
    for term in range(len(small)):
        total = total + from_block(held_small[term, 0])
    both[...] = total


def finish(feeds, attends, small):
    reads = Reads()
    feed_plan = [(layer, part, term, reads.at(array), place) for layer, flows in enumerate(feeds)
                 for part, flow in enumerate(flows) for term, (array, place) in enumerate(flow.terms)]
    far_plan = [(layer, other, reads.at(array), place) for layer, pair in enumerate(attends)
                for other, (array, place) in enumerate(pair[0].far)]
    small_plan = reads.places(small.terms)
    rows, tile = feeds[0][0].terms[0][0].shape[1:]
    width, terms = 3 * tile, len(feeds[0][0].terms)
    anywhere, vmem = pl.BlockSpec(memory_space=pl.ANY), pl.BlockSpec(memory_space=pltpu.VMEM)
    return pl.pallas_call(
        functools.partial(finish_kernel, (feed_plan, far_plan, small_plan), len(reads.arrays)),
        out_shape=[jax.ShapeDtypeStruct((2, rows, width), F32), jax.ShapeDtypeStruct((2, width, rows), F32)]
        + [jax.ShapeDtypeStruct((2, rows, width // 4), F32)] * 4 + [jax.ShapeDtypeStruct((24, width), F32)],
        in_specs=[anywhere] * len(reads.arrays) + [vmem] * 3,
        out_specs=[vmem] * 7,
        scratch_shapes=[pltpu.VMEM((2, 3, terms, 2, rows, tile), BF16), pltpu.VMEM((2, 3, 3, rows, tile), BF16),
                        pltpu.VMEM((len(small_plan), 1, rows, tile), BF16),
                        pltpu.SemaphoreType.DMA((len(feed_plan) + len(far_plan) + len(small_plan),))],
        compiler_params=pltpu.CompilerParams(vmem_limit_bytes=VMEM_BYTES),
    )(*reads.arrays, attends[0][0].own, attends[1][0].own, small.own)


def far_pieces(layer, w_up, w_down, owns, halves, crossed, blocks):
    rows = w_up.shape[1] // 8
    arrays = [w_up, w_down] + halves + crossed
    plan = [(0, layer, 0, 0, None), (1, layer, 1, 0, None)]
    for core in range(2):
        for kind, (inner, outer) in enumerate(((2, 4), (4, 2))):
            for second in range(2):
                for first in range(2):
                    for other in (1, 2, 3):
                        place = core + inner * first + outer * second
                        plan.append((2 + 4 * core + 2 * kind + second, (first, other - 1), kind,
                                     SHARD_ORDER.index(other), place))
    return Pieces(arrays, plan, blocks, rows, [owns[at] for at in SHARD_ORDER])


def all_pieces(layer, own, w_up, w_down, blocks):
    rows = w_up.shape[1] // 8
    pieces = lax.all_gather(own, ("dp", "mp"))
    plan = [(0, layer, 0, 0, None), (1, layer, 1, 0, None)]
    for slot in (1, 2, 3):
        for kind in range(2):
            for at in range(8):
                source = lambda ref, held, slot=slot, kind=kind, at=at: ref.at[
                    4 * at + held[8 + slot], pl.ds(kind * rows, rows)]
                plan.append((2, source, kind, slot, slice(at * rows, (at + 1) * rows)))
    tails = [own] + [lax.dynamic_index_in_dim(pieces, blocks[8 + slot], 0, False)[2 * rows:] for slot in (1, 2, 3)]
    return Pieces([w_up, w_down, pieces], plan, blocks, rows, tails)


def gathered_pieces(layer, w_up, w_down, b_up, blocks):
    arrays = [lax.all_gather(w_up[layer], "mp"), lax.all_gather(w_down[layer], "mp")]
    shards = arrays[0].shape[0]
    plan = [(kind, at, kind, at, None) for kind in range(2) for at in range(shards)]
    bias = lax.all_gather(b_up[layer:layer + 1], "mp")
    return Pieces(arrays, plan, blocks, 0, [bias_terms(bias[at]) for at in range(shards)])


def sum_feed_anywhere(grads):
    both = lax.psum_scatter(grads, "mp", scatter_dimension=0, tiled=True)[0]
    both = lax.psum_scatter(both.astype(F32), "dp", scatter_dimension=1, tiled=True)
    return both[0], both[1].T


def sum_attend_anywhere(grads):
    whole = lax.psum_scatter(grads, "mp", scatter_dimension=2, tiled=True)
    return lax.psum_scatter(whole.astype(F32), "dp", scatter_dimension=1, tiled=True)


def shards(inputs, slot_valid, ln1_gain, ln1_bias, w_query, w_key, w_value, w_out, gate_logit,
           ln2_gain, ln2_bias, w_up, b_up, w_down, b_down, cotangent):
    pages, slots, width = inputs.shape
    dp, mp = lax.axis_size("dp"), lax.axis_size("mp")
    paired = dp == 8 and mp == 4 and width % (16 * dp) == 0
    if paired:
        blocks = jnp.concatenate([
            lax.axis_index("dp") ^ jnp.arange(8, dtype=jnp.int32),
            lax.axis_index("mp") ^ jnp.array(SHARD_ORDER, jnp.int32)])
    else:
        blocks = jnp.arange(2, dtype=jnp.int32)

    own_valid = lax.dynamic_slice_in_dim(slot_valid, lax.axis_index("mp") * pages, pages, 0) == 1
    key_text = lax.broadcasted_iota(jnp.int32, (slots, slots), 0) < TEXT
    query_text = lax.broadcasted_iota(jnp.int32, (slots, slots), 1) < TEXT
    live = jnp.broadcast_to(own_valid[:, :, None], (pages, slots, slots))
    masks = [
        jnp.where(jnp.logical_and(live, (key_text != query_text)[None]), 0.0, -1e30).astype(F32),
        jnp.where(live, 0.0, -1e30).astype(F32),
    ]
    gate = gate_logit[None]
    weights = (w_query, w_key, w_value, w_out)
    first_rows = inputs.reshape(pages * slots, width)
    cotangent = cotangent.reshape(pages * slots, width)
    got = {"grad": None}

    def attend_layer(layer, rows, ties):
        return attend(layer, layer == 0, rows, masks[layer], ln1_gain, ln1_bias, gate, weights, ties)

    def feed_layer(layer, rows, pieces, ties):
        return feed(layer, rows, ln2_gain, ln2_bias, b_down, pieces, (F32, BF16)[layer], ties)

    def feed_back_layer(layer, ties):
        rows, active, slope, pieces = got["feed", layer]
        got["mixed_grad"], got["feed_sums", layer], got["up_sums", layer], *got["feed_grads", layer] = feed_back(
            layer, (got["grad"], cotangent)[layer], rows, ln2_gain, ln2_bias, active, slope, pieces, not paired, ties)

    def attend_back_layer(layer, ties):
        rows, kept = got["attend", layer]
        got["grad"], got["attend_sums", layer], *got["attend_grads", layer] = attend_back(
            layer, layer == 0, got["mixed_grad"], rows, ln1_gain, ln1_bias, gate, (*kept[:5], *kept[6:]), weights,
            blocks, not paired, ties)

    if paired:
        owns = pack(w_up, w_down, b_up, blocks)
        rows = width // 8
        chain = Chain(owns[0])
        far = lambda own: [swap(own, "mp", other) for other in (1, 2, 3)]
        split = lambda pieces: (jnp.stack([piece[:rows] for piece in pieces]),
                                jnp.stack([piece[rows:2 * rows] for piece in pieces]))
        other_core = lambda *values: [swap(value, "dp", 1) for value in values]

        far_0 = far(owns[0])
        kept_0 = list(attend_layer(0, first_rows, ()))
        chain.need((kept_0, 5))
        far_0 = list(chain.tie(*far_0))
        ups, downs = chain.tie(*split(far_0))
        near_0 = chain.tie(swap(ups, "dp", 2), swap(downs, "dp", 4))
        ups_0, downs_0 = chain.tie(jnp.stack([ups, near_0[0]]), jnp.stack([downs, near_0[1]]))
        side_0 = [swap(ups_0, "dp", 4), swap(downs_0, "dp", 2)]
        core_0 = other_core(ups_0, downs_0)
        side_0 = chain.tie(*side_0)
        core_0 += other_core(*side_0)
        pieces_0 = far_pieces(0, w_up, w_down, [owns[0]] + far_0, [ups_0, side_0[0], downs_0, side_0[1]],
                              [core_0[at] for at in (0, 2, 1, 3)], blocks)
        result_0, active_0, slope_0 = feed_layer(0, kept_0[5], pieces_0, chain.ties())
        kept_1 = attend_layer(1, result_0, ())
        pieces_1 = all_pieces(1, owns[1], w_up, w_down, blocks)
    else:
        pieces_0 = gathered_pieces(0, w_up, w_down, b_up, blocks)
        pieces_1 = gathered_pieces(1, w_up, w_down, b_up, blocks)
        kept_0 = attend_layer(0, first_rows, ())
        result_0, active_0, slope_0 = feed_layer(0, kept_0[5], pieces_0, ())
        kept_1 = attend_layer(1, result_0, ())

    result_1, active_1, slope_1 = feed_layer(1, kept_1[5], pieces_1, ())
    got["feed", 0] = kept_0[5], active_0, slope_0, pieces_0
    got["feed", 1] = kept_1[5], active_1, slope_1, pieces_1
    got["attend", 0], got["attend", 1] = (first_rows, kept_0), (result_0, kept_1)

    if paired:
        rounds = Rounds(blocks)
        feed_back_layer(1, ())
        feeds, attends = {1: feed_flows(got["feed_grads", 1])}, {}
        rounds.cross(feeds[1])
        attend_back_layer(1, ())
        attends[1] = attend_flows(got["attend_grads", 1])
        rounds.exchange(feeds[1], ties=[got["attend_sums", 1]], crossing=[attends[1]])
        feed_back_layer(0, rounds.made)
        feeds[0] = feed_flows(got["feed_grads", 0])
        rounds.exchange(feeds[1] + attends[1], ties=[got["feed_sums", 0]], crossing=[feeds[0]])
        attend_back_layer(0, rounds.made)
        attends[0] = attend_flows(got["attend_grads", 0])
        small = Small([got[name, layer] for layer in (0, 1) for name in ("feed_sums", "attend_sums", "up_sums")])
        rounds.exchange(feeds[0] + feeds[1] + attends[1], small=small, crossing=[attends[0]])
        rounds.exchange(feeds[0] + attends[0] + feeds[1], [attends[1]], small)
        rounds.exchange(feeds[0] + attends[0], small=small)
        rounds.exchange(feeds[0], [attends[0]], small)
        row_of = lambda row, layer: row + 10 * layer
        up_grad, down_grad, *attend_grads, both = finish([feeds[0], feeds[1]], [attends[0], attends[1]], small)
    else:
        for layer in (1, 0):
            feed_back_layer(layer, ())
            attend_back_layer(layer, ())
        feed_grads = [sum_feed_anywhere(got["feed_grads", layer][0]) for layer in (0, 1)]
        up_grad, down_grad = (jnp.stack([feed_grads[layer][at] for layer in (0, 1)]) for at in range(2))
        sums = [sum_attend_anywhere(got["attend_grads", layer][0]) for layer in (0, 1)]
        attend_grads = [jnp.stack([sums[0][at], sums[1][at]]) for at in range(4)]
        both = lax.psum(jnp.concatenate([part for layer in (0, 1) for part in (
            got["feed_sums", layer][:3], got["attend_sums", layer][:3], got["up_sums", layer][:, 0])]), ("dp", "mp"))
        later = both.shape[0] // 2
        row_of = lambda row, layer: row + later * layer

    lines = width // dp
    mine = lax.dynamic_slice_in_dim(both, lax.axis_index("dp") * lines, lines, 1)
    pick = lambda row: jnp.stack([mine[row_of(row, 0)], mine[row_of(row, 1)]])
    me = lax.axis_index("mp")
    bup_grad = jnp.concatenate([
        lax.dynamic_slice_in_dim(both, row_of(6, 0) + me, 1, 0), lax.dynamic_slice_in_dim(both, row_of(6, 1) + me, 1, 0)])
    return (
        result_1.reshape(pages, slots, width),
        got["grad"].reshape(pages, slots, width),
        pick(3),
        pick(4),
        *attend_grads,
        mine[5],
        pick(1),
        pick(2),
        up_grad,
        bup_grad,
        down_grad,
        pick(0),
    )


def solution(mesh):
    rows = P(("dp", "mp"), None, None)
    return jax.shard_map(
        shards,
        mesh=mesh,
        in_specs=(rows, P("dp", None), P(), P(), P(), P(), P(), P(), P(), P(), P(), P(None, None, "mp"),
                  P(None, "mp"), P(None, "mp", None), P(), rows),
        out_specs=(rows, rows, P(None, "dp"), P(None, "dp"), P(None, "dp", "mp"), P(None, "dp", "mp"),
                   P(None, "dp", "mp"), P(None, "dp", "mp"), P("dp"), P(None, "dp"), P(None, "dp"),
                   P(None, "dp", "mp"), P(None, "mp"), P(None, "mp", "dp"), P(None, "dp")),
        check_vma=False,
    )
```

```python
import functools

import jax
import jax.numpy as jnp
from jax import lax
from jax.experimental import pallas as pl
from jax.experimental.pallas import tpu as pltpu
from jax.sharding import PartitionSpec as P

HEADS = 12
TEXT = 112
F32 = jnp.float32
BF16 = jnp.bfloat16
VMEM_BYTES = 56 * 2**20


def dot(a, b, a_dim, b_dim):
    return lax.dot_general(a, b, (((a_dim,), (b_dim,)), ((), ())), preferred_element_type=F32)


def whiten(rows):
    centered = rows - jnp.mean(rows, axis=-1, keepdims=True)
    spread = jnp.mean(centered * centered, axis=-1, keepdims=True)
    inverse = lax.rsqrt(spread + 1e-05)
    return centered * inverse, inverse


def whiten_back(white, inverse, gain, grad):
    scaled = grad * gain
    first = jnp.mean(scaled, axis=-1, keepdims=True)
    second = jnp.mean(scaled * white, axis=-1, keepdims=True)
    return inverse * (scaled - first - white * second)


def column_sum(rows):
    return jnp.sum(rows, axis=0, keepdims=True)


def gelu_and_slope(values):
    size = jnp.abs(values)
    t = 1.0 / (1.0 + (0.3275911 * 0.7071067811865476) * size)
    bell = jnp.exp(-0.5 * values * values)
    poly = 0.5 * 1.061405429
    poly = poly * t + 0.5 * -1.453152027
    poly = poly * t + 0.5 * 1.421413741
    poly = poly * t + 0.5 * -0.284496736
    poly = poly * t + 0.5 * 0.254829592
    tail = poly * t * bell
    phi = jnp.where(values >= 0.0, 1.0 - tail, tail)
    return values * phi, phi + values * bell * 0.3989422804014327


def split_heads(pair):
    lane = lax.broadcasted_iota(jnp.int32, pair.shape, 1)
    first = lane < pair.shape[1] // 2
    zero = jnp.zeros_like(pair)
    return jnp.concatenate([jnp.where(first, pair, zero), jnp.where(first, zero, pair)], axis=0)


def join_heads(both):
    slots = both.shape[0] // 2
    lane = lax.broadcasted_iota(jnp.int32, (slots, both.shape[1]), 1)
    return jnp.where(lane < both.shape[1] // 2, both[:slots], both[slots:])


def start_copies(sources, targets, sems):
    copies = [
        pltpu.make_async_copy(source, target, sems.at[at])
        for at, (source, target) in enumerate(zip(sources, targets))
    ]
    for copy in copies:
        copy.start()
    return copies


class Arriving:
    def __init__(self, source, held, sem):
        self.copy, self.held, self.here = pltpu.make_async_copy(source, held, sem), held, False
        self.copy.start()

    def __getitem__(self, at):
        if not self.here:
            self.copy.wait()
            self.here = True
        return self.held[at]


class Leaving:
    def __init__(self, sems):
        self.sems, self.copies = sems, []

    def send(self, held, target):
        self.copies.append(pltpu.make_async_copy(held, target, self.sems.at[len(self.copies)]))
        self.copies[-1].start()

    def wait(self):
        for copy in self.copies:
            copy.wait()


def attend_kernel(layer, crossed, resid, mask, gain, shift, gate, wq, wk, wv, wo,
                  outs, made, held, sems, out_sems):
    q_out, k_out, v_out, p_out, c_out, mixed, *branch_out = made
    leaving = Leaving(out_sems)
    pages, slots = mask.shape[0], mask.shape[1]
    width = resid.shape[1]
    pairs = HEADS // 2
    pair_width = width // pairs
    scale = 1.0 / (width // HEADS) ** 0.5
    copies = start_copies(
        [w.at[layer] for w in (wq, wk, wv, wo)], [held.at[at] for at in range(4)], sems
    )
    white, _ = whiten(resid[...].astype(F32))
    normed = (white * gain[layer:layer + 1] + shift[layer:layer + 1]).astype(BF16)
    copies[0].wait()
    q_out[...] = (dot(normed, held[0], 1, 0).astype(BF16).astype(F32) * scale).astype(BF16)
    leaving.send(q_out, outs[0])
    copies[1].wait()
    k_out[...] = dot(normed, held[1], 1, 0).astype(BF16)
    leaving.send(k_out, outs[1])
    copies[2].wait()
    v_out[...] = dot(normed, held[2], 1, 0).astype(BF16)
    leaving.send(v_out, outs[2])

    for page in range(pages):
        rows = slice(page * slots, (page + 1) * slots)
        bias = mask[page]
        for pair in range(pairs):
            cols = slice(pair * pair_width, (pair + 1) * pair_width)
            scores = dot(split_heads(k_out[rows, cols]), q_out[rows, cols], 1, 1)
            scores = scores.reshape(2, slots, slots) + bias[None]
            top = jnp.max(scores, axis=1, keepdims=True)
            raised = jnp.exp(scores - top)
            probs = raised * (1.0 / jnp.sum(raised, axis=1, keepdims=True))
            probs = probs.reshape(2 * slots, slots).astype(BF16)
            p_out[page, pair] = probs
            c_out[rows, cols] = dot(probs, split_heads(v_out[rows, cols]), 0, 0).astype(BF16)
        leaving.send(p_out.at[page], outs[3].at[page])
    leaving.send(c_out, outs[4])
    copies[3].wait()
    for page in range(pages):
        rows = slice(page * slots, (page + 1) * slots)
        branch = dot(c_out[rows], held[3], 1, 0)
        if crossed:
            branch_out[0][rows] = branch.astype(BF16)
            branch = branch * jax.nn.sigmoid(gate[...])
            leaving.send(branch_out[0].at[rows], outs[6].at[rows])
        mixed[rows] = resid[rows].astype(F32) + branch
        leaving.send(mixed.at[rows], outs[5].at[rows])
    leaving.wait()


def attend(layer, crossed, resid, mask, gain, shift, gate, weights, ties):
    rows, width = resid.shape
    pages, slots = mask.shape[:2]
    low = jax.ShapeDtypeStruct((rows, width), BF16)
    vmem = pl.BlockSpec(memory_space=pltpu.VMEM)
    outs = [low, low, low, jax.ShapeDtypeStruct((pages, HEADS // 2, 2 * slots, slots), BF16), low,
            jax.ShapeDtypeStruct((rows, width), F32)]
    if crossed:
        outs.append(low)

    def body(*refs):
        ins, rest = refs[:9], refs[9 + len(ties):]
        attend_kernel(layer, crossed, *ins, rest[:len(outs)], rest[len(outs):2 * len(outs)], *rest[2 * len(outs):])

    return pl.pallas_call(
        body,
        out_shape=outs,
        in_specs=[vmem] * 5 + [pl.BlockSpec(memory_space=pl.ANY)] * (4 + len(ties)),
        out_specs=[pl.BlockSpec(memory_space=pl.ANY)] * len(outs),
        scratch_shapes=[pltpu.VMEM(out.shape, out.dtype) for out in outs]
        + [pltpu.VMEM((4, width, width), BF16), pltpu.SemaphoreType.DMA((4,)),
           pltpu.SemaphoreType.DMA((4 + (2 + crossed) * pages,))],
        compiler_params=pltpu.CompilerParams(vmem_limit_bytes=VMEM_BYTES),
        cost_estimate=pl.CostEstimate(flops=8 * rows * width * width, bytes_accessed=14 * 2**20, transcendentals=0),
    )(resid, mask, gain, shift, gate, *weights, *ties)


class Pieces:
    def __init__(self, arrays, plan, blocks, tails):
        self.arrays, self.plan, self.blocks, self.tails = arrays, plan, blocks, tails

    def copies(self, refs, held, blocks, sems, first=0, last=None):
        return [
            pltpu.make_async_copy(refs[array] if index is None else refs[array].at[index],
                                  held[kind].at[target(blocks[0])], sems.at[at])
            for at, (array, index, kind, target) in list(enumerate(self.plan))[first:last]
        ]

    def held(self, width):
        shape = (2, 2, 2, len(self.tails), width // 8, width)
        return [pltpu.VMEM(shape, BF16), pltpu.VMEM(shape, BF16)]

    def tail_specs(self, width):
        return [pl.BlockSpec((16, width), lambda step, last=tail.shape[0] // 16 - 1: (last, 0)) for tail in self.tails]

    def start_and_wait(self, refs, held, blocks, sems):
        step = pl.program_id(0)

        @pl.when(step == 0)
        def _():
            for copy in self.copies(refs, held, blocks, sems):
                copy.start()

        def wait():
            @pl.when(step == 0)
            def _():
                for copy in self.copies(refs, held, blocks, sems, 0, 2):
                    copy.wait()

            @pl.when(step == 1)
            def _():
                for copy in self.copies(refs, held, blocks, sems, 2):
                    copy.wait()
        return wait


def feed_kernel(layer, pieces, ties, blocks, mixed, gain, shift, b_down, *rest):
    count = len(pieces.arrays)
    tails, rest = rest[:len(pieces.tails)], rest[len(pieces.tails):]
    refs, rest = rest[:count], rest[count + ties:]
    result, active_out, slope_out, up, down, low, total, bias, sems = rest
    shards, width = up.shape[3], up.shape[5]
    step = pl.program_id(0)
    wait = pieces.start_and_wait(refs, (up, down), blocks, sems)

    @pl.when(step == 0)
    def _():
        white, _ = whiten(mixed[...])
        low[...] = (white * gain[layer:layer + 1] + shift[layer:layer + 1]).astype(BF16)
        total[...] = mixed[...] + b_down[layer:layer + 1]
        for at, tail in enumerate(tails):
            bias[at] = column_sum(tail[...].astype(F32))

    wait()
    parts = 3
    part = width // parts
    for at in range(parts):
        cols = slice(at * part, (at + 1) * part)
        upper = dot(low[...], up[:, :, :, step, :, cols].reshape(width, part), 1, 0) + bias[step, :, cols]
        active, slope = gelu_and_slope(upper)
        active = active.astype(BF16)
        active_out[0, :, cols] = active
        slope_out[0, :, cols] = slope.astype(BF16)
        total[...] += dot(active, down[:, :, :, step].reshape(width, width)[cols], 1, 0)

    @pl.when(step == shards - 1)
    def _():
        result[...] = total[...].astype(result.dtype)


def feed(layer, mixed, gain, shift, b_down, pieces, out_type, ties):
    rows, width = mixed.shape
    shards = len(pieces.tails)
    whole = lambda shape: pl.BlockSpec(shape, lambda step: (0,) * len(shape))
    each = lambda shape: pl.BlockSpec((1,) + shape, lambda step: (step,) + (0,) * len(shape))
    return pl.pallas_call(
        functools.partial(feed_kernel, layer, pieces, len(ties)),
        grid=(shards,),
        out_shape=[jax.ShapeDtypeStruct((rows, width), out_type)]
        + [jax.ShapeDtypeStruct((shards, rows, width), BF16)] * 2,
        in_specs=[pl.BlockSpec(memory_space=pltpu.SMEM), whole((rows, width)), whole(gain.shape), whole(shift.shape),
                  whole(b_down.shape)] + pieces.tail_specs(width)
        + [pl.BlockSpec(memory_space=pl.ANY)] * (len(pieces.arrays) + len(ties)),
        out_specs=[whole((rows, width)), each((rows, width)), each((rows, width))],
        scratch_shapes=[*pieces.held(width),
                        pltpu.VMEM((rows, width), BF16), pltpu.VMEM((rows, width), F32),
                        pltpu.VMEM((shards, 1, width), F32), pltpu.SemaphoreType.DMA((len(pieces.plan),))],
        compiler_params=pltpu.CompilerParams(vmem_limit_bytes=VMEM_BYTES),
        cost_estimate=pl.CostEstimate(flops=16 * rows * width * width, bytes_accessed=20 * 2**20, transcendentals=0),
    )(pieces.blocks, mixed, gain, shift, b_down, *pieces.tails, *pieces.arrays, *ties)


ROWS_FIRST = ((0, 4, 2, 6, 1, 5, 3, 7), (0, 2, 4, 6, 1, 3, 5, 7))
PART_ORDERS = (0, 1, 0)
PART_STAGES = ("xyvu", "yuxv", "uxyv")
SHARD_ORDER = (0, 2, 1, 3)
LINKS = {"c": ("dp", 1), "x": ("dp", 2), "y": ("dp", 4), "u": ("mp", 1), "v": ("mp", 2), "w": ("mp", 3)}


def turn_rows(held, turned, blocks, order):
    if order is None:
        turned[...] = held[...]
        return
    size = held.shape[0] // len(order)
    for at, place in enumerate(order):
        start = pl.multiple_of(blocks[place] * size, size)
        turned[at * size:(at + 1) * size] = held[pl.ds(start, size)]


def put_blocks(made, keep, send, place):
    rows = made.shape[0] // 8
    for half, out in enumerate((keep, send)):
        for first in range(2):
            for second in range(2):
                at = (4 * half + 2 * first + second) * rows
                out[place(first, second)] = made[at:at + rows]


def feed_back_kernel(layer, pieces, joint, ties, blocks, grad_out, mixed, gain, shift, active, slope, *rest):
    count = len(pieces.arrays)
    refs, rest = rest[:count], rest[count + ties:]
    grads_count = 1 if joint else 2
    grad_mixed, sums, up_sums, *grads = rest[:3 + grads_count]
    up, down, low, low_turned, normed_turned, held, total, sems = rest[3 + grads_count:]
    shards, width = up.shape[3], up.shape[5]
    part = width // 3
    step = pl.program_id(0)
    wait = pieces.start_and_wait(refs, (up, down), blocks, sems)

    def put(kind, turned, right):
        if joint:
            grads[0][0, kind] = dot(turned[0], right, 1, 0).astype(BF16)
            return
        for at in range(3):
            made = dot(turned[PART_ORDERS[at]], right[:, at * part:(at + 1) * part], 1, 0).astype(BF16)
            put_blocks(made, *grads, lambda first, second: (0, at, kind, first, second))

    @pl.when(step == 0)
    def _():
        rows = grad_out[...].astype(F32)
        low[...] = rows.astype(BF16)
        sums[...] = jnp.zeros_like(sums)
        sums[0:1] = column_sum(rows)
        white, _ = whiten(mixed[...])
        normed = (white * gain[layer:layer + 1] + shift[layer:layer + 1]).astype(BF16)
        for value, turned in ((low[...], low_turned), (normed, normed_turned)):
            held[...] = value.T
            for at in range(turned.shape[0]):
                turn_rows(held, turned.at[at], blocks, None if joint else ROWS_FIRST[at])
        total[...] = jnp.zeros_like(total)

    wait()
    put(1, low_turned, active[0])
    upper = dot(low[...], down[:, :, :, step].reshape(width, width), 1, 1) * slope[0].astype(F32)
    up_sums[0] = column_sum(upper)
    upper_low = upper.astype(BF16)
    put(0, normed_turned, upper_low)
    total[...] += dot(upper_low, up[:, :, :, step].reshape(width, width), 1, 1)

    @pl.when(step == shards - 1)
    def _():
        white, inverse = whiten(mixed[...])
        grad = total[...]
        sums[1:2] = column_sum(grad * white)
        sums[2:3] = column_sum(grad)
        grad_mixed[...] = grad_out[...].astype(F32) + whiten_back(white, inverse, gain[layer:layer + 1], grad)


def feed_back(layer, grad_out, mixed, gain, shift, active, slope, pieces, joint, ties):
    rows, width = mixed.shape
    shards = active.shape[0]
    whole = lambda shape: pl.BlockSpec(shape, lambda step: (0,) * len(shape))
    each = lambda shape: pl.BlockSpec((1,) + shape, lambda step: (step,) + (0,) * len(shape))
    if joint:
        grads = [(2, width, width)]
    else:
        grads = [(3, 2, 2, 2, width // 8, width // 3)] * 2
    turned = pltpu.VMEM((1 if joint else 2, width, rows), BF16)
    return pl.pallas_call(
        functools.partial(feed_back_kernel, layer, pieces, joint, len(ties)),
        grid=(shards,),
        out_shape=[jax.ShapeDtypeStruct((rows, width), F32), jax.ShapeDtypeStruct((8, width), F32),
                   jax.ShapeDtypeStruct((shards, 1, width), F32)]
        + [jax.ShapeDtypeStruct((shards,) + shape, BF16) for shape in grads],
        in_specs=[pl.BlockSpec(memory_space=pltpu.SMEM), whole((rows, width)), whole((rows, width)), whole(gain.shape),
                  whole(shift.shape), each((rows, width)), each((rows, width))]
        + [pl.BlockSpec(memory_space=pl.ANY)] * (len(pieces.arrays) + len(ties)),
        out_specs=[whole((rows, width)), whole((8, width)), each((1, width))] + [each(shape) for shape in grads],
        scratch_shapes=[*pieces.held(width),
                        pltpu.VMEM((rows, width), BF16), turned, turned, pltpu.VMEM((width, rows), BF16),
                        pltpu.VMEM((rows, width), F32), pltpu.SemaphoreType.DMA((len(pieces.plan),))],
        compiler_params=pltpu.CompilerParams(vmem_limit_bytes=VMEM_BYTES),
        cost_estimate=pl.CostEstimate(flops=32 * rows * width * width, bytes_accessed=30 * 2**20, transcendentals=0),
    )(pieces.blocks, grad_out, mixed, gain, shift, active, slope, *pieces.arrays, *ties)


def attend_back_kernel(layer, crossed, joint, blocks, grad_mixed, resid, gain, shift, gate, q, k, v, p, context, branch,
                       wq, wk, wv, wo, resid_out, sums, outs, grad_resid, grads, landing,
                       held, turning, turned, gc, gq, gk, gv, sems, out_sems):
    pages, slots = p.shape[0], p.shape[3]
    width = resid.shape[1]
    pairs = HEADS // 2
    pair_width = width // pairs
    scale = 1.0 / (width // HEADS) ** 0.5
    number = iter(range(16))
    arrive = lambda source, target: Arriving(source, target, sems.at[next(number)])
    land = iter(landing)
    context, grad_mixed = arrive(context, next(land)), arrive(grad_mixed, next(land))
    if crossed:
        branch = arrive(branch, next(land))
    w_out = arrive(wo.at[layer], held.at[0])
    v, p, k, q = (arrive(value, next(land)) for value in (v, p, k, q))
    resid = arrive(resid, next(land))
    w_query, w_key, w_value = (arrive(w.at[layer], held.at[at + 1]) for at, w in enumerate((wq, wk, wv)))
    leaving = Leaving(out_sems)
    sums[...] = jnp.zeros_like(sums)

    def put(at, right):
        made = dot(turned[...], right, 1, 0).astype(BF16)
        if joint:
            grads[0][at] = made
            return
        tile = width // 3
        for col in range(3):
            put_blocks(made[:, col * tile:(col + 1) * tile], *grads,
                       lambda first, second: (at // 2, first, second, at % 2, col))

    def turn(rows, order):
        turning[...] = rows.T
        turn_rows(turning, turned, blocks, None if joint else ROWS_FIRST[order])

    grad = grad_mixed[...]
    if crossed:
        opened = jax.nn.sigmoid(gate[...])
        sums[2:3] = column_sum(grad * branch[...].astype(F32)) * (opened * (1.0 - opened))
        low = (grad * opened).astype(BF16)
    else:
        low = grad.astype(BF16)
    turn(context[...], 1)
    put(3, low)
    gc[...] = dot(low, w_out[...], 1, 1).astype(BF16)

    for page in range(pages):
        rows = slice(page * slots, (page + 1) * slots)
        for pair in range(pairs):
            cols = slice(pair * pair_width, (pair + 1) * pair_width)
            probs_low = p[page, pair]
            probs = probs_low.astype(F32).reshape(2, slots, slots)
            grad_probs = dot(split_heads(v[rows, cols]), gc[rows, cols], 1, 1).reshape(2, slots, slots)
            delta = jnp.sum(probs * grad_probs, axis=1, keepdims=True)
            grad_scores = (probs * (grad_probs - delta)).astype(BF16).reshape(2 * slots, slots)
            gq[rows, cols] = (dot(grad_scores, split_heads(k[rows, cols]), 0, 0) * scale).astype(BF16)
            gk[rows, cols] = join_heads(dot(grad_scores, q[rows, cols], 1, 0)).astype(BF16)
            gv[rows, cols] = join_heads(dot(probs_low, gc[rows, cols], 1, 0)).astype(BF16)

    white, inverse = whiten(resid[...].astype(F32))
    normed = (white * gain[layer:layer + 1] + shift[layer:layer + 1]).astype(BF16)
    turn(normed, 1)
    put(2, gv[...])
    if not joint:
        for made, out in zip(grads, outs):
            leaving.send(made.at[1], out.at[1])
    if not joint:
        turn_rows(turning, turned, blocks, ROWS_FIRST[0])
    put(0, gq[...])
    put(1, gk[...])
    for made, out in zip(grads, outs):
        if joint:
            leaving.send(made, out)
        else:
            leaving.send(made.at[0], out.at[0])
    total = dot(gq[...], w_query[...], 1, 1) + dot(gk[...], w_key[...], 1, 1) + dot(gv[...], w_value[...], 1, 1)
    sums[0:1] = column_sum(total * white)
    sums[1:2] = column_sum(total)
    grad_resid[...] = grad + whiten_back(white, inverse, gain[layer:layer + 1], total)
    leaving.send(grad_resid, resid_out)
    leaving.wait()


def attend_back(layer, crossed, grad_mixed, resid, gain, shift, gate, kept, weights, blocks, joint, ties):
    rows, width = resid.shape
    vmem = pl.BlockSpec(memory_space=pltpu.VMEM)
    kept = list(kept)
    given = 6 + len(kept) + 4
    if joint:
        grads = [jax.ShapeDtypeStruct((4, width, width), BF16)]
    else:
        grads = [jax.ShapeDtypeStruct((2, 2, 2, 2, 3, width // 8, width // 3), BF16)] * 2

    def body(*refs):
        ins, rest = list(refs[:given]), refs[given + len(ties):]
        if not crossed:
            ins.insert(11, None)
        count = len(grads)
        resid_out, sums, outs, resid_made, rest = rest[0], rest[1], rest[2:2 + count], rest[2 + count], rest[3 + count:]
        attend_back_kernel(layer, crossed, joint, *ins, resid_out, sums, outs, resid_made, rest[:count],
                           rest[count:count + len(landing)], *rest[count + len(landing):])

    low = pltpu.VMEM((rows, width), BF16)
    like = lambda value: pltpu.VMEM(value.shape, value.dtype)
    q, k, v, p, context, *branch = kept
    landing = [like(value) for value in (context, grad_mixed, *branch, v, p, k, q, resid)]
    anywhere = pl.BlockSpec(memory_space=pl.ANY)
    return pl.pallas_call(
        body,
        out_shape=[jax.ShapeDtypeStruct((rows, width), F32), jax.ShapeDtypeStruct((8, width), F32)] + grads,
        in_specs=[pl.BlockSpec(memory_space=pltpu.SMEM)] + [anywhere] * 2 + [vmem] * 3
        + [anywhere] * (len(kept) + 4 + len(ties)),
        out_specs=[anywhere, vmem] + [anywhere] * len(grads),
        scratch_shapes=[pltpu.VMEM((rows, width), F32)] + [like(grad) for grad in grads] + landing
        + [pltpu.VMEM((4, width, width), BF16), pltpu.VMEM((width, rows), BF16), pltpu.VMEM((width, rows), BF16),
           low, low, low, low, pltpu.SemaphoreType.DMA((16,)), pltpu.SemaphoreType.DMA((5,))],
        compiler_params=pltpu.CompilerParams(vmem_limit_bytes=VMEM_BYTES),
        cost_estimate=pl.CostEstimate(flops=16 * rows * width * width, bytes_accessed=24 * 2**20, transcendentals=0),
    )(blocks, grad_mixed, resid, gain, shift, gate, *kept, *weights, *ties)


def pack_kernel(layers, rows, block, bias, w_up, w_down, *rest):
    outs, sems = rest[:layers], rest[layers]
    start = pl.multiple_of(block[0] * rows, rows)
    sources = [w.at[layer, pl.ds(start, rows)] for layer in range(layers) for w in (w_up, w_down)]
    targets = [out.at[pl.ds(kind * rows, rows)] for out in outs for kind in range(2)]
    copies = start_copies(sources, targets, sems)
    for layer, out in enumerate(outs):
        out[2 * rows:] = bias_terms(bias[layer:layer + 1])
    for copy in copies:
        copy.wait()


def bias_terms(bias):
    top = bias.astype(BF16)
    left = bias - top.astype(F32)
    middle = left.astype(BF16)
    bottom = (left - middle.astype(F32)).astype(BF16)
    row = lax.broadcasted_iota(jnp.int32, (16, bias.shape[1]), 0)
    terms = [jnp.broadcast_to(term.astype(F32), row.shape) for term in (top, middle, bottom)]
    zero = jnp.zeros(row.shape, F32)
    chosen = jnp.where(row == 0, terms[0], jnp.where(row == 1, terms[1], jnp.where(row == 2, terms[2], zero)))
    return chosen.astype(BF16)


def pack(w_up, w_down, b_up, block):
    layers, width, shard = w_up.shape
    rows = width // 8
    out = jax.ShapeDtypeStruct((2 * rows + 16, shard), BF16)
    vmem = pl.BlockSpec(memory_space=pltpu.VMEM)
    return pl.pallas_call(
        functools.partial(pack_kernel, layers, rows),
        out_shape=[out] * layers,
        in_specs=[pl.BlockSpec(memory_space=pltpu.SMEM), vmem] + [pl.BlockSpec(memory_space=pl.ANY)] * 2,
        out_specs=[vmem] * layers,
        scratch_shapes=[pltpu.SemaphoreType.DMA((2 * layers,))],
        cost_estimate=pl.CostEstimate(flops=0, bytes_accessed=4 * layers * rows * shard * 4, transcendentals=0),
    )(block, b_up, w_up, w_down)


class Chain:
    def __init__(self, token):
        self.token, self.pending = token, []

    def need(self, *places):
        self.pending += places

    def tie(self, *values):
        count = len(values)
        out = lax.optimization_barrier((*values, self.token, *(held[key] for held, key in self.pending)))
        self.token = out[count]
        for (held, key), value in zip(self.pending, out[count + 1:]):
            held[key] = value
        self.pending = []
        return out[0] if count == 1 else out[:count]

    def ties(self):
        out, self.pending = [self.token] + [held[key] for held, key in self.pending], []
        return out


def places(values):
    return [(values, at) for at in range(len(values))]


def swap(value, axis, bit):
    size = lax.axis_size(axis)
    return lax.ppermute(value, axis, [(at, at ^ bit) for at in range(size)])


class Flow:
    def __init__(self, keep, index, bits, stages):
        self.wide, self.index, self.bits, self.stages, self.terms = [keep], list(index), bits, stages, []
        self.tile = keep.shape[-2:]

    def halve(self):
        bit, self.bits = self.bits[0], self.bits[1:]
        leaves = list(self.index)
        leaves[bit], self.index[bit] = 1, 0
        return tuple(leaves)

    def order(self, shape):
        open_dims = [dim for dim, at in enumerate(self.index) if at is None]
        ranked = list(self.bits) + [dim for dim in open_dims if dim not in self.bits]
        sizes = [shape[dim] for dim in open_dims]
        places = [()]
        for dim in ranked:
            places = [place + (at,) for place in places for at in range(shape[dim])]
        return sizes, [tuple(place[ranked.index(dim)] for dim in open_dims) for place in places]


def feed_flows(grads):
    keep = grads[0].reshape((2, 2) + grads[0].shape[1:])
    bits = ((4, 5, 1, 0), (4, 0, 5, 1), (0, 4, 5, 1))
    return [Flow(keep, (None, None, at, None, None, None), bits[at], PART_STAGES[at]) for at in range(3)]


def attend_flows(grads):
    return [Flow(grads[0], (at, None, None, None, None), (1, 2), stages) for at, stages in enumerate(("xy", "yx"))]


class Reads:
    def __init__(self):
        self.arrays = []

    def at(self, array):
        for at, known in enumerate(self.arrays):
            if known is array:
                return at
        self.arrays.append(array)
        return len(self.arrays) - 1

    def places(self, terms):
        return [(self.at(array), place) for array, place in terms]


def as_block(value):
    tile = value.shape[1] // 3
    parts = [value[:, at * tile:(at + 1) * tile] for at in range(3)]
    return jnp.concatenate(parts + [jnp.zeros_like(parts[0])], axis=0).astype(BF16)


def from_block(block):
    value = block.astype(F32)
    rows = value.shape[0] // 4
    return jnp.concatenate([value[at * rows:(at + 1) * rows] for at in range(3)], axis=1)


def add_small_parts(parts, blocks, out):
    out[...] = jnp.zeros_like(out)
    for layer in range(2):
        fed, attended, up = parts[3 * layer:3 * layer + 3]
        base = 10 * layer
        out[base:base + 3] = fed[0:3]
        out[base + 3:base + 6] = attended[0:3]
        for slot in range(len(SHARD_ORDER)):
            out[pl.ds(base + 6 + blocks[8 + slot], 1)] = up[slot]


def exchange_kernel(plan, blocks, *refs):
    (sizes, reads, sends, column_count, ends, small, small_terms, small_ends,
     array_count, small_count, tie_count) = plan
    arrays, refs = refs[:array_count], refs[array_count:]
    small_ins, refs = refs[:small_count], refs[small_count + tie_count:]
    outs, refs = refs[:len(sizes)], list(refs[len(sizes):])
    own = refs.pop(0) if column_count else None
    small_out = refs.pop(0) if small == "new" else None
    out_sems, sems = refs.pop(), refs.pop()
    mades = [refs.pop(0) for _ in sizes]
    copies, groups = [], []

    def fetch(source, target):
        copies.append(pltpu.make_async_copy(source, target, sems.at[len(copies)]))
        copies[-1].start()
        return copies[-1]

    for wide, _, terms, size in reads:
        held_wide = refs.pop(0)
        held = refs.pop(0) if terms else None
        waits = [fetch(arrays[array].at[index], held_wide.at[at]) for at, (array, index) in enumerate(wide)]
        waits += [fetch(arrays[array].at[pl.ds(place, size)], held.at[at]) for at, (array, place) in enumerate(terms)]
        groups.append((waits, held_wide, held))
    held_small = refs.pop(0) if small_terms else None
    small_waits = [fetch(arrays[array].at[pl.ds(place, 1)], held_small.at[at]) for at, (array, place) in enumerate(small_terms)]

    def arrive(number):
        waits, held_wide, held = groups[number]
        for copy in waits:
            copy.wait()
        wide, _, terms, _ = reads[number]
        return lambda block, place: [held_wide[(at,) + place] for at in range(len(wide))] + [
            held[at, block] for at in range(len(terms))]

    for number, (out, start, order) in enumerate(sends):
        values_of = arrive(number)
        for block, place in enumerate(order):
            values = values_of(block, place)
            while len(values) > 1:
                values = [values[at] + values[at + 1] if at + 1 < len(values) else values[at]
                          for at in range(0, len(values), 2)]
            mades[out][start + block] = values[0]
    if column_count:
        turned = refs.pop(0)
        shards = len(SHARD_ORDER)
        share = turned.shape[2] // 4
        for flow in range(column_count):
            values_of = arrive(len(sends) + flow)
            lines, tiles = reads[len(sends) + flow][1]
            for line in range(lines):
                parts = []
                for tile in range(tiles):
                    total = None
                    for value in values_of(line * tiles + tile, (line, tile)):
                        total = value.astype(F32) if total is None else total + value.astype(F32)
                    parts.append(total)
                whole = jnp.concatenate(parts, axis=1)
                to = (2 * flow + line) * share
                for shard in range(shards):
                    turned[shard ^ blocks[8], :, to:to + share] = whole[:, shard * share:(shard + 1) * share]
        own[...] = turned[0]
        tile = mades[0].shape[2]
        for other in range(1, shards):
            out, start = ends[other - 1]
            for cut in range(3):
                mades[out][start + cut] = turned[other, :, cut * tile:(cut + 1) * tile].astype(BF16)
    if small:
        if small == "new":
            add_small_parts(small_ins, blocks, small_out)
            total = small_out[...]
        else:
            total = small_ins[0][...]
            for copy in small_waits:
                copy.wait()
            for term in range(len(small_terms)):
                total = total + from_block(held_small[term, 0])
        for out, start in small_ends:
            mades[out][start] = as_block(total)
    leaving = [pltpu.make_async_copy(made, outs[at], out_sems.at[at]) for at, made in enumerate(mades)]
    for copy in leaving:
        copy.start()
    for copy in leaving:
        copy.wait()


class Rounds:
    def __init__(self, blocks):
        self.blocks, self.arrived = blocks, []

    def exchange(self, flows, ending=(), small=None, ties=(), crossing=()):
        known, reads, sends, sizes = Reads(), [], [], {}

        def room(letter, size):
            place = sizes.get(letter, 0)
            sizes[letter] = place + size
            return list(sizes).index(letter), place

        def read(flow, index, skipped):
            shape = flow.wide[0].shape
            open_sizes, order = flow.order(shape)
            size = len(order)
            wide = [(known.at(array), tuple(slice(None) if at is None else at for at in index)) for array in flow.wide]
            reads.append((wide, open_sizes, [(known.at(array), start + skipped * size) for array, start in flow.terms], size))
            return size, order

        moved = []
        for flow in flows:
            letter, flow.stages = flow.stages[0], flow.stages[1:]
            size, order = read(flow, flow.halve(), 1)
            out, place = room(letter, size)
            sends.append((out, place, order))
            moved.append((flow.terms, letter, place))
        tile = flows[0].tile
        width = 3 * tile[1]
        for pair in ending:
            for flow in pair:
                read(flow, flow.index, 0)
        column_count = len(reads) - len(sends)
        ends = [room(letter, 3) for letter in "uvw"] if column_count else []
        mode, small_terms, small_ins, small_ends = "", [], [], []
        if small is not None:
            mode, letters = small.next()
            small_ins = small.parts if mode == "new" else [small.own]
            small_terms = [] if mode == "new" else known.places(small.terms)
            small_ends = [room(letter, 1) for letter in letters]
        order = list(sizes)
        outs = [jax.ShapeDtypeStruct((sizes[letter],) + tile, BF16) for letter in order]
        held = [pltpu.VMEM((sizes[letter],) + tile, BF16) for letter in order]
        for wide, open_sizes, terms, size in reads:
            held.append(pltpu.VMEM((len(wide), *open_sizes) + tile, BF16))
            if terms:
                held.append(pltpu.VMEM((len(terms), size) + tile, BF16))
        if small_terms:
            held.append(pltpu.VMEM((len(small_terms), 1) + tile, BF16))
        more = []
        if column_count:
            held.append(pltpu.VMEM((len(SHARD_ORDER), tile[0], width), F32))
            more.append(jax.ShapeDtypeStruct((tile[0], width), F32))
        if mode == "new":
            more.append(jax.ShapeDtypeStruct((24, width), F32))
        ties = [*self.arrived, *ties]
        copies = sum(len(wide) + len(terms) for wide, _, terms, _ in reads) + len(small_terms)
        anywhere, vmem = pl.BlockSpec(memory_space=pl.ANY), pl.BlockSpec(memory_space=pltpu.VMEM)
        plan = ([sizes[letter] for letter in order], reads, sends, column_count, ends, mode, small_terms, small_ends,
                len(known.arrays), len(small_ins), len(ties))
        made = list(pl.pallas_call(
            functools.partial(exchange_kernel, plan),
            out_shape=outs + more,
            in_specs=[pl.BlockSpec(memory_space=pltpu.SMEM)] + [anywhere] * len(known.arrays) + [vmem] * len(small_ins)
            + [anywhere] * len(ties),
            out_specs=[anywhere] * len(outs) + [vmem] * len(more),
            scratch_shapes=held + [pltpu.SemaphoreType.DMA((copies,)), pltpu.SemaphoreType.DMA((len(outs),))],
            compiler_params=pltpu.CompilerParams(vmem_limit_bytes=VMEM_BYTES),
        )(self.blocks, *known.arrays, *small_ins, *ties))
        rest = made[len(outs):]
        self.made = made[:len(outs)]
        going = lax.optimization_barrier(self.made + [send for _, send in crossing])
        arrived = {letter: swap(value, *LINKS[letter]) for letter, value in zip(order, going)}
        self.arrived = list(arrived.values())
        for (crossed, _), send in zip(crossing, going[len(outs):]):
            self.cross(crossed, send)
        for terms, letter, place in moved:
            terms.append((arrived[letter], place))
        for pair in ending:
            pair[0].own = rest.pop(0)
            pair[0].far = [(arrived[letter], place) for letter, (_, place) in zip("uvw", ends)]
        if mode:
            if mode == "new":
                small.own = rest.pop(0)
            small.terms += [(arrived[letter], place) for letter, (_, place) in zip(letters, small_ends)]

    def cross(self, flows, send):
        arrived = swap(send, *LINKS["c"])
        self.arrived.append(arrived)
        for flow in flows:
            flow.wide.append(arrived.reshape(flow.wide[0].shape))


class Small:
    def __init__(self, parts):
        self.parts, self.terms, self.stages = parts, [], ["c", "x", "y", "uvw"]

    def next(self):
        letters = self.stages.pop(0)
        return ("new" if letters == "c" else "old"), letters


def finish_kernel(plan, array_count, blocks, *refs):
    wides, feeds, far, small = plan
    arrays, refs = refs[:array_count], refs[array_count:]
    owns, small_own, refs = refs[:2], refs[2], refs[3:]
    up, down, *attends = refs[:6]
    smalls, gate, hidden = refs[6:11], refs[11], refs[12]
    held_wide, held, held_far, held_small, sems = refs[13:]
    copies = []

    def fetch(array, place, size, target):
        copies.append(pltpu.make_async_copy(arrays[array].at[pl.ds(place, size)], target, sems.at[len(copies)]))
        copies[-1].start()

    for layer, term, array in wides:
        copies.append(pltpu.make_async_copy(
            arrays[array].at[0, 0, :, :, 0, 0], held_wide.at[layer, term], sems.at[len(copies)]))
        copies[-1].start()
    for layer, part, term, array, place in feeds:
        fetch(array, place, 2, held.at[layer, part, term])
    for layer, other, array, place in far:
        fetch(array, place, 3, held_far.at[layer, other])
    for term, (array, place) in enumerate(small):
        fetch(array, place, 1, held_small.at[term])
    for copy in copies:
        copy.wait()
    terms, tile = held.shape[2], held.shape[5]
    for layer in range(2):
        for part in range(3):
            total = held_wide[layer, 0, part].astype(F32) + held_wide[layer, 1, part].astype(F32)
            for term in range(terms):
                total = total + held[layer, part, term].astype(F32)
            up[layer, :, part * tile:(part + 1) * tile] = total[0]
            down[layer, :, part * tile:(part + 1) * tile] = total[1]
        total = owns[layer][...]
        for other in range(3):
            total = total + jnp.concatenate([held_far[layer, other, cut].astype(F32) for cut in range(3)], axis=1)
        share = total.shape[1] // 4
        for at, out in enumerate(attends):
            out[layer] = total[:, at * share:(at + 1) * share]
    total = small_own[...]
    for term in range(len(small)):
        total = total + from_block(held_small[term, 0])
    lines = total.shape[1] // 8
    mine = jnp.where(blocks[0] == 0, total[:, :lines], 0.0)
    for place in range(1, 8):
        mine = mine + jnp.where(blocks[0] == place, total[:, place * lines:(place + 1) * lines], 0.0)
    for layer in range(2):
        base = 10 * layer
        for row, out in zip((3, 4, 1, 2, 0), smalls):
            out[layer:layer + 1] = mine[base + row:base + row + 1]
        shard = jnp.zeros((1, total.shape[1]), F32)
        for at in range(4):
            shard = shard + jnp.where(blocks[8] == at, total[base + 6 + at:base + 7 + at], 0.0)
        hidden[layer:layer + 1] = shard
    gate[...] = mine[5:6]


def finish(feeds, attends, small, blocks):
    reads = Reads()
    wide_plan = [(layer, term, reads.at(array)) for layer, flows in enumerate(feeds)
                 for term, array in enumerate(flows[0].wide)]
    feed_plan = [(layer, part, term, reads.at(array), place) for layer, flows in enumerate(feeds)
                 for part, flow in enumerate(flows) for term, (array, place) in enumerate(flow.terms)]
    far_plan = [(layer, other, reads.at(array), place) for layer, pair in enumerate(attends)
                for other, (array, place) in enumerate(pair[0].far)]
    small_plan = reads.places(small.terms)
    rows, tile = feeds[0][0].tile
    width, terms = 3 * tile, len(feeds[0][0].terms)
    anywhere, vmem = pl.BlockSpec(memory_space=pl.ANY), pl.BlockSpec(memory_space=pltpu.VMEM)
    return pl.pallas_call(
        functools.partial(finish_kernel, (wide_plan, feed_plan, far_plan, small_plan), len(reads.arrays)),
        out_shape=[jax.ShapeDtypeStruct((2, rows, width), F32)] * 2
        + [jax.ShapeDtypeStruct((2, rows, width // 4), F32)] * 4 + [jax.ShapeDtypeStruct((2, rows), F32)] * 5
        + [jax.ShapeDtypeStruct((1, rows), F32), jax.ShapeDtypeStruct((2, width), F32)],
        in_specs=[pl.BlockSpec(memory_space=pltpu.SMEM)] + [anywhere] * len(reads.arrays) + [vmem] * 3,
        out_specs=[vmem] * 13,
        scratch_shapes=[pltpu.VMEM((2, 2, 3, 2, rows, tile), BF16), pltpu.VMEM((2, 3, terms, 2, rows, tile), BF16),
                        pltpu.VMEM((2, 3, 3, rows, tile), BF16),
                        pltpu.VMEM((len(small_plan), 1, rows, tile), BF16),
                        pltpu.SemaphoreType.DMA((len(wide_plan) + len(feed_plan) + len(far_plan) + len(small_plan),))],
        compiler_params=pltpu.CompilerParams(vmem_limit_bytes=VMEM_BYTES),
    )(blocks, *reads.arrays, attends[0][0].own, attends[1][0].own, small.own)


def eighths(weights):
    return weights.reshape(weights.shape[:-2] + (2, 2, 2, weights.shape[-2] // 8, weights.shape[-1]))


def in_order(bit, own, other):
    first = (lax.axis_index("dp") & bit) == 0
    return jnp.stack([jnp.where(first, own, other), jnp.where(first, other, own)])


def far_pieces(layer, w_up, w_down, tails, halves, crossed, blocks):
    arrays = [eighths(w_up), eighths(w_down)] + halves + crossed
    every, rest = slice(None), pl.ds(1, len(tails) - 1)
    plan = [(kind, layer, kind, lambda me: (every, every, every, 0)) for kind in range(2)]
    for core in range(2):
        for second in range(2):
            plan.append((2 + 4 * core + second, None, 0, lambda me, core=core, second=second: (
                ((me >> 2) & 1) ^ second, every, (me & 1) ^ core, rest)))
            plan.append((4 + 4 * core + second, None, 1, lambda me, core=core, second=second: (
                every, ((me >> 1) & 1) ^ second, (me & 1) ^ core, rest)))
    return Pieces(arrays, plan, blocks, tails)


def gathered_pieces(layer, w_up, w_down, b_up, blocks):
    arrays = [eighths(lax.all_gather(weights[layer], "mp")) for weights in (w_up, w_down)]
    shards = arrays[0].shape[0]
    plan = [(kind, at, kind, lambda me, at=at: (slice(None),) * 3 + (at,)) for at in range(shards) for kind in range(2)]
    bias = lax.all_gather(b_up[layer:layer + 1], "mp")
    return Pieces(arrays, plan, blocks, [bias_terms(bias[at]) for at in range(shards)])


def sum_feed_anywhere(grads):
    both = lax.psum_scatter(grads, "mp", scatter_dimension=0, tiled=True)[0]
    both = lax.psum_scatter(both.astype(F32), "dp", scatter_dimension=1, tiled=True)
    return both[0], both[1].T


def sum_attend_anywhere(grads):
    whole = lax.psum_scatter(grads, "mp", scatter_dimension=2, tiled=True)
    return lax.psum_scatter(whole.astype(F32), "dp", scatter_dimension=1, tiled=True)


def shards(inputs, slot_valid, ln1_gain, ln1_bias, w_query, w_key, w_value, w_out, gate_logit,
           ln2_gain, ln2_bias, w_up, b_up, w_down, b_down, cotangent):
    pages, slots, width = inputs.shape
    dp, mp = lax.axis_size("dp"), lax.axis_size("mp")
    paired = dp == 8 and mp == 4 and width % (16 * dp) == 0
    if paired:
        blocks = jnp.concatenate([
            lax.axis_index("dp") ^ jnp.arange(8, dtype=jnp.int32),
            lax.axis_index("mp") ^ jnp.array(SHARD_ORDER, jnp.int32)])
    else:
        blocks = jnp.arange(2, dtype=jnp.int32)

    own_valid = lax.dynamic_slice_in_dim(slot_valid, lax.axis_index("mp") * pages, pages, 0) == 1
    key_text = lax.broadcasted_iota(jnp.int32, (slots, slots), 0) < TEXT
    query_text = lax.broadcasted_iota(jnp.int32, (slots, slots), 1) < TEXT
    live = jnp.broadcast_to(own_valid[:, :, None], (pages, slots, slots))
    masks = [
        jnp.where(jnp.logical_and(live, (key_text != query_text)[None]), 0.0, -1e30).astype(F32),
        jnp.where(live, 0.0, -1e30).astype(F32),
    ]
    gate = gate_logit[None]
    weights = (w_query, w_key, w_value, w_out)
    first_rows = inputs.reshape(pages * slots, width)
    cotangent = cotangent.reshape(pages * slots, width)
    got = {"grad": None}

    def attend_layer(layer, rows, ties):
        return attend(layer, layer == 0, rows, masks[layer], ln1_gain, ln1_bias, gate, weights, ties)

    def feed_layer(layer, rows, pieces, ties):
        return feed(layer, rows, ln2_gain, ln2_bias, b_down, pieces, (F32, BF16)[layer], ties)

    def feed_back_layer(layer, ties):
        rows, active, slope, pieces = got["feed", layer]
        got["mixed_grad"], got["feed_sums", layer], got["up_sums", layer], *got["feed_grads", layer] = feed_back(
            layer, (got["grad"], cotangent)[layer], rows, ln2_gain, ln2_bias, active, slope, pieces, not paired, ties)

    def attend_back_layer(layer, ties):
        rows, kept = got["attend", layer]
        got["grad"], got["attend_sums", layer], *got["attend_grads", layer] = attend_back(
            layer, layer == 0, got["mixed_grad"], rows, ln1_gain, ln1_bias, gate, (*kept[:5], *kept[6:]), weights,
            blocks, not paired, ties)

    if paired:
        owns = pack(w_up, w_down, b_up, blocks)
        rows = width // 8
        chain = Chain(owns[0])
        far = lambda own: [swap(own, "mp", other) for other in SHARD_ORDER[1:]]
        split = lambda pieces: (jnp.stack([piece[:rows] for piece in pieces]),
                                jnp.stack([piece[rows:2 * rows] for piece in pieces]))
        other_core = lambda *values: [swap(value, "dp", 1) for value in values]

        far_0 = far(owns[0])
        kept_0 = list(attend_layer(0, first_rows, ()))
        chain.need((kept_0, 5))
        far_0 = list(chain.tie(*far_0))
        ups, downs = chain.tie(*split(far_0))
        near_0 = [swap(ups, "dp", 2), swap(downs, "dp", 4)]
        far_1 = far(chain.tie(owns[1]))
        near_0 = chain.tie(*near_0)
        ups_0, downs_0 = chain.tie(in_order(2, ups, near_0[0]), in_order(4, downs, near_0[1]))
        side_0 = [swap(ups_0, "dp", 4), swap(downs_0, "dp", 2)]
        ups_0, downs_0, *side_0 = chain.tie(ups_0, downs_0, *side_0)
        far_1 = list(chain.tie(*far_1))
        ups, downs = chain.tie(*split(far_1))
        near_1 = [swap(ups, "dp", 2), swap(downs, "dp", 4)]
        core_0 = other_core(ups_0, side_0[0], downs_0, side_0[1])
        pieces_0 = far_pieces(0, w_up, w_down, [owns[0]] + far_0, [ups_0, side_0[0], downs_0, side_0[1]], core_0, blocks)
        fed_0 = list(feed_layer(0, kept_0[5], pieces_0, chain.ties()))
        chain.need((fed_0, 0))
        near_1 = chain.tie(*near_1)
        result_0, active_0, slope_0 = fed_0
        ups_1, downs_1 = chain.tie(in_order(2, ups, near_1[0]), in_order(4, downs, near_1[1]))
        side_1 = [swap(ups_1, "dp", 4), swap(downs_1, "dp", 2)]
        kept_1 = list(attend_layer(1, result_0, chain.ties()))
        chain.need((kept_1, 5))
        side_1 = chain.tie(*side_1)
        core_1 = other_core(ups_1, side_1[0], downs_1, side_1[1])
        pieces_1 = far_pieces(1, w_up, w_down, [owns[1]] + far_1, [ups_1, side_1[0], downs_1, side_1[1]], core_1, blocks)
    else:
        pieces_0 = gathered_pieces(0, w_up, w_down, b_up, blocks)
        pieces_1 = gathered_pieces(1, w_up, w_down, b_up, blocks)
        kept_0 = attend_layer(0, first_rows, ())
        result_0, active_0, slope_0 = feed_layer(0, kept_0[5], pieces_0, ())
        kept_1 = attend_layer(1, result_0, ())

    result_1, active_1, slope_1 = feed_layer(1, kept_1[5], pieces_1, ())
    got["feed", 0] = kept_0[5], active_0, slope_0, pieces_0
    got["feed", 1] = kept_1[5], active_1, slope_1, pieces_1
    got["attend", 0], got["attend", 1] = (first_rows, kept_0), (result_0, kept_1)

    if paired:
        rounds = Rounds(blocks)
        feed_back_layer(1, ())
        feeds, attends = {1: feed_flows(got["feed_grads", 1])}, {}
        rounds.cross(feeds[1], got["feed_grads", 1][1])
        attend_back_layer(1, ())
        attends[1] = attend_flows(got["attend_grads", 1])
        rounds.exchange(feeds[1], ties=[got["attend_sums", 1]], crossing=[(attends[1], got["attend_grads", 1][1])])
        feed_back_layer(0, rounds.made)
        feeds[0] = feed_flows(got["feed_grads", 0])
        rounds.exchange(feeds[1] + attends[1], ties=[got["feed_sums", 0]], crossing=[(feeds[0], got["feed_grads", 0][1])])
        attend_back_layer(0, rounds.made)
        attends[0] = attend_flows(got["attend_grads", 0])
        small = Small([got[name, layer] for layer in (0, 1) for name in ("feed_sums", "attend_sums", "up_sums")])
        rounds.exchange(feeds[0] + feeds[1] + attends[1], small=small, crossing=[(attends[0], got["attend_grads", 0][1])])
        rounds.exchange(feeds[0] + attends[0] + feeds[1], [attends[1]], small)
        rounds.exchange(feeds[0] + attends[0], small=small)
        rounds.exchange(feeds[0], [attends[0]], small)
        up_grad, down_turned, *rest = finish([feeds[0], feeds[1]], [attends[0], attends[1]], small, blocks)
        down_grad = jnp.swapaxes(down_turned, 1, 2)
        attend_grads, small_grads, gate_grad, bup_grad = rest[:4], rest[4:9], rest[9][0], rest[10]
    else:
        for layer in (1, 0):
            feed_back_layer(layer, ())
            attend_back_layer(layer, ())
        feed_grads = [sum_feed_anywhere(got["feed_grads", layer][0]) for layer in (0, 1)]
        up_grad, down_grad = (jnp.stack([feed_grads[layer][at] for layer in (0, 1)]) for at in range(2))
        sums = [sum_attend_anywhere(got["attend_grads", layer][0]) for layer in (0, 1)]
        attend_grads = [jnp.stack([sums[0][at], sums[1][at]]) for at in range(4)]
        both = lax.psum(jnp.concatenate([part for layer in (0, 1) for part in (
            got["feed_sums", layer][:3], got["attend_sums", layer][:3], got["up_sums", layer][:, 0])]), ("dp", "mp"))
        later, lines, me = both.shape[0] // 2, width // dp, lax.axis_index("mp")
        mine = lax.dynamic_slice_in_dim(both, lax.axis_index("dp") * lines, lines, 1)
        small_grads = [jnp.stack([mine[row], mine[later + row]]) for row in (3, 4, 1, 2, 0)]
        gate_grad = mine[5]
        bup_grad = jnp.concatenate([lax.dynamic_slice_in_dim(both, row + me, 1, 0) for row in (6, later + 6)])

    return (
        result_1.reshape(pages, slots, width),
        got["grad"].reshape(pages, slots, width),
        small_grads[0],
        small_grads[1],
        *attend_grads,
        gate_grad,
        small_grads[2],
        small_grads[3],
        up_grad,
        bup_grad,
        down_grad,
        small_grads[4],
    )


def solution(mesh):
    rows = P(("dp", "mp"), None, None)
    return jax.shard_map(
        shards,
        mesh=mesh,
        in_specs=(rows, P("dp", None), P(), P(), P(), P(), P(), P(), P(), P(), P(), P(None, None, "mp"),
                  P(None, "mp"), P(None, "mp", None), P(), rows),
        out_specs=(rows, rows, P(None, "dp"), P(None, "dp"), P(None, "dp", "mp"), P(None, "dp", "mp"),
                   P(None, "dp", "mp"), P(None, "dp", "mp"), P("dp"), P(None, "dp"), P(None, "dp"),
                   P(None, "dp", "mp"), P(None, "mp"), P(None, "mp", "dp"), P(None, "dp")),
        check_vma=False,
    )
```

```python
import functools

import jax
import jax.numpy as jnp
from jax import lax
from jax.experimental import pallas as pl
from jax.experimental.pallas import tpu as pltpu
from jax.sharding import PartitionSpec as P

HEADS = 12
TEXT = 112
F32 = jnp.float32
BF16 = jnp.bfloat16
VMEM_BYTES = 62 * 2**20


def dot(a, b, a_dim, b_dim):
    return lax.dot_general(a, b, (((a_dim,), (b_dim,)), ((), ())), preferred_element_type=F32)


def whiten(rows):
    centered = rows - jnp.mean(rows, axis=-1, keepdims=True)
    spread = jnp.mean(centered * centered, axis=-1, keepdims=True)
    inverse = lax.rsqrt(spread + 1e-05)
    return centered * inverse, inverse


def whiten_back(white, inverse, gain, grad):
    scaled = grad * gain
    first = jnp.mean(scaled, axis=-1, keepdims=True)
    second = jnp.mean(scaled * white, axis=-1, keepdims=True)
    return inverse * (scaled - first - white * second)


def column_sum(rows):
    return jnp.sum(rows, axis=0, keepdims=True)


def gelu_and_slope(values):
    size = jnp.abs(values)
    t = 1.0 / (1.0 + (0.3275911 * 0.7071067811865476) * size)
    bell = jnp.exp(-0.5 * values * values)
    poly = 0.5 * 1.061405429
    poly = poly * t + 0.5 * -1.453152027
    poly = poly * t + 0.5 * 1.421413741
    poly = poly * t + 0.5 * -0.284496736
    poly = poly * t + 0.5 * 0.254829592
    tail = poly * t * bell
    phi = jnp.where(values >= 0.0, 1.0 - tail, tail)
    return values * phi, phi + values * bell * 0.3989422804014327


def split_heads(pair):
    lane = lax.broadcasted_iota(jnp.int32, pair.shape, 1)
    first = lane < pair.shape[1] // 2
    zero = jnp.zeros_like(pair)
    return jnp.concatenate([jnp.where(first, pair, zero), jnp.where(first, zero, pair)], axis=0)


def join_heads(both):
    slots = both.shape[0] // 2
    lane = lax.broadcasted_iota(jnp.int32, (slots, both.shape[1]), 1)
    return jnp.where(lane < both.shape[1] // 2, both[:slots], both[slots:])


def start_copies(sources, targets, sems):
    copies = [
        pltpu.make_async_copy(source, target, sems.at[at])
        for at, (source, target) in enumerate(zip(sources, targets))
    ]
    for copy in copies:
        copy.start()
    return copies


class Arriving:
    def __init__(self, source, held, sem):
        self.copy, self.held, self.here = pltpu.make_async_copy(source, held, sem), held, False
        self.copy.start()

    def __getitem__(self, at):
        if not self.here:
            self.copy.wait()
            self.here = True
        return self.held[at]


class Leaving:
    def __init__(self, sems):
        self.sems, self.copies = sems, []

    def send(self, held, target):
        self.copies.append(pltpu.make_async_copy(held, target, self.sems.at[len(self.copies)]))
        self.copies[-1].start()

    def wait(self):
        for copy in self.copies:
            copy.wait()


def attend_kernel(layer, crossed, resid, mask, gain, shift, gate, wq, wk, wv, wo,
                  outs, made, held, sems, out_sems):
    q_out, k_out, v_out, p_out, c_out, mixed, *branch_out = made
    leaving = Leaving(out_sems)
    pages, slots = mask.shape[0], mask.shape[1]
    width = resid.shape[1]
    pairs = HEADS // 2
    pair_width = width // pairs
    scale = 1.0 / (width // HEADS) ** 0.5
    copies = start_copies(
        [w.at[layer] for w in (wq, wk, wv, wo)], [held.at[at] for at in range(4)], sems
    )
    white, _ = whiten(resid[...].astype(F32))
    normed = (white * gain[layer:layer + 1] + shift[layer:layer + 1]).astype(BF16)
    copies[0].wait()
    q_out[...] = (dot(normed, held[0], 1, 0).astype(BF16).astype(F32) * scale).astype(BF16)
    leaving.send(q_out, outs[0])
    copies[1].wait()
    k_out[...] = dot(normed, held[1], 1, 0).astype(BF16)
    leaving.send(k_out, outs[1])
    copies[2].wait()
    v_out[...] = dot(normed, held[2], 1, 0).astype(BF16)
    leaving.send(v_out, outs[2])

    for page in range(pages):
        rows = slice(page * slots, (page + 1) * slots)
        bias = mask[page]
        for pair in range(pairs):
            cols = slice(pair * pair_width, (pair + 1) * pair_width)
            scores = dot(split_heads(k_out[rows, cols]), q_out[rows, cols], 1, 1)
            scores = scores.reshape(2, slots, slots) + bias[None]
            top = jnp.max(scores, axis=1, keepdims=True)
            raised = jnp.exp(scores - top)
            probs = raised * (1.0 / jnp.sum(raised, axis=1, keepdims=True))
            probs = probs.reshape(2 * slots, slots).astype(BF16)
            p_out[page, pair] = probs
            c_out[rows, cols] = dot(probs, split_heads(v_out[rows, cols]), 0, 0).astype(BF16)
        leaving.send(p_out.at[page], outs[3].at[page])
    leaving.send(c_out, outs[4])
    copies[3].wait()
    for page in range(pages):
        rows = slice(page * slots, (page + 1) * slots)
        branch = dot(c_out[rows], held[3], 1, 0)
        if crossed:
            branch_out[0][rows] = branch.astype(BF16)
            branch = branch * jax.nn.sigmoid(gate[...])
            leaving.send(branch_out[0].at[rows], outs[6].at[rows])
        mixed[rows] = resid[rows].astype(F32) + branch
        leaving.send(mixed.at[rows], outs[5].at[rows])
    leaving.wait()


def attend(layer, crossed, resid, mask, gain, shift, gate, weights, ties):
    rows, width = resid.shape
    pages, slots = mask.shape[:2]
    low = jax.ShapeDtypeStruct((rows, width), BF16)
    vmem = pl.BlockSpec(memory_space=pltpu.VMEM)
    outs = [low, low, low, jax.ShapeDtypeStruct((pages, HEADS // 2, 2 * slots, slots), BF16), low,
            jax.ShapeDtypeStruct((rows, width), F32)]
    if crossed:
        outs.append(low)

    def body(*refs):
        ins, rest = refs[:9], refs[9 + len(ties):]
        attend_kernel(layer, crossed, *ins, rest[:len(outs)], rest[len(outs):2 * len(outs)], *rest[2 * len(outs):])

    return pl.pallas_call(
        body,
        out_shape=outs,
        in_specs=[vmem] * 5 + [pl.BlockSpec(memory_space=pl.ANY)] * (4 + len(ties)),
        out_specs=[pl.BlockSpec(memory_space=pl.ANY)] * len(outs),
        scratch_shapes=[pltpu.VMEM(out.shape, out.dtype) for out in outs]
        + [pltpu.VMEM((4, width, width), BF16), pltpu.SemaphoreType.DMA((4,)),
           pltpu.SemaphoreType.DMA((4 + (2 + crossed) * pages,))],
        compiler_params=pltpu.CompilerParams(vmem_limit_bytes=VMEM_BYTES),
        cost_estimate=pl.CostEstimate(flops=8 * rows * width * width, bytes_accessed=14 * 2**20, transcendentals=0),
    )(resid, mask, gain, shift, gate, *weights, *ties)


class Pieces:
    def __init__(self, arrays, plan, blocks, tails):
        self.arrays, self.plan, self.blocks, self.tails = arrays, plan, blocks, tails

    def copies(self, refs, held, blocks, sems, first=0, last=None):
        return [
            pltpu.make_async_copy(refs[array] if index is None else refs[array].at[index],
                                  held[kind].at[target(blocks[0])], sems.at[at])
            for at, (array, index, kind, target) in list(enumerate(self.plan))[first:last]
        ]

    def held(self, width):
        shape = (2, 2, 2, len(self.tails), width // 8, width)
        return [pltpu.VMEM(shape, BF16), pltpu.VMEM(shape, BF16)]

    def tail_specs(self, width):
        return [pl.BlockSpec((16, width), lambda step, last=tail.shape[0] // 16 - 1: (last, 0)) for tail in self.tails]

    def start_and_wait(self, refs, held, blocks, sems):
        step = pl.program_id(0)

        @pl.when(step == 0)
        def _():
            for copy in self.copies(refs, held, blocks, sems):
                copy.start()

        def wait():
            @pl.when(step == 0)
            def _():
                for copy in self.copies(refs, held, blocks, sems, 0, 2):
                    copy.wait()

            @pl.when(step == 1)
            def _():
                for copy in self.copies(refs, held, blocks, sems, 2):
                    copy.wait()
        return wait


def feed_kernel(layer, pieces, ties, blocks, mixed, gain, shift, b_down, *rest):
    count = len(pieces.arrays)
    tails, rest = rest[:len(pieces.tails)], rest[len(pieces.tails):]
    refs, rest = rest[:count], rest[count + ties:]
    result, active_out, slope_out, up, down, low, total, bias, sems = rest
    shards, width = up.shape[3], up.shape[5]
    step = pl.program_id(0)
    wait = pieces.start_and_wait(refs, (up, down), blocks, sems)

    @pl.when(step == 0)
    def _():
        white, _ = whiten(mixed[...])
        low[...] = (white * gain[layer:layer + 1] + shift[layer:layer + 1]).astype(BF16)
        total[...] = mixed[...] + b_down[layer:layer + 1]
        for at, tail in enumerate(tails):
            bias[at] = column_sum(tail[...].astype(F32))

    wait()
    parts = 3
    part = width // parts
    for at in range(parts):
        cols = slice(at * part, (at + 1) * part)
        upper = dot(low[...], up[:, :, :, step, :, cols].reshape(width, part), 1, 0) + bias[step, :, cols]
        active, slope = gelu_and_slope(upper)
        active = active.astype(BF16)
        active_out[0, :, cols] = active
        slope_out[0, :, cols] = slope.astype(BF16)
        total[...] += dot(active, down[:, :, :, step].reshape(width, width)[cols], 1, 0)

    @pl.when(step == shards - 1)
    def _():
        result[...] = total[...].astype(result.dtype)


def feed(layer, mixed, gain, shift, b_down, pieces, out_type, ties):
    rows, width = mixed.shape
    shards = len(pieces.tails)
    whole = lambda shape: pl.BlockSpec(shape, lambda step: (0,) * len(shape))
    each = lambda shape: pl.BlockSpec((1,) + shape, lambda step: (step,) + (0,) * len(shape))
    return pl.pallas_call(
        functools.partial(feed_kernel, layer, pieces, len(ties)),
        grid=(shards,),
        out_shape=[jax.ShapeDtypeStruct((rows, width), out_type)]
        + [jax.ShapeDtypeStruct((shards, rows, width), BF16)] * 2,
        in_specs=[pl.BlockSpec(memory_space=pltpu.SMEM), whole((rows, width)), whole(gain.shape), whole(shift.shape),
                  whole(b_down.shape)] + pieces.tail_specs(width)
        + [pl.BlockSpec(memory_space=pl.ANY)] * (len(pieces.arrays) + len(ties)),
        out_specs=[whole((rows, width)), each((rows, width)), each((rows, width))],
        scratch_shapes=[*pieces.held(width),
                        pltpu.VMEM((rows, width), BF16), pltpu.VMEM((rows, width), F32),
                        pltpu.VMEM((shards, 1, width), F32), pltpu.SemaphoreType.DMA((len(pieces.plan),))],
        compiler_params=pltpu.CompilerParams(vmem_limit_bytes=VMEM_BYTES),
        cost_estimate=pl.CostEstimate(flops=16 * rows * width * width, bytes_accessed=20 * 2**20, transcendentals=0),
    )(pieces.blocks, mixed, gain, shift, b_down, *pieces.tails, *pieces.arrays, *ties)


ROWS_ORDER = (0, 4, 2, 6, 1, 5, 3, 7)
PART_STAGES = (("xyvu", "yuxv", "uxyv"), ("xyvu", "yuxv", "uxyv"))
SHARD_ORDER = (0, 2, 1, 3)
LINKS = {"c": ("dp", 1), "x": ("dp", 2), "y": ("dp", 4), "u": ("mp", 1), "v": ("mp", 2), "w": ("mp", 3)}


def turn_rows(held, turned, blocks, order):
    if order is None:
        turned[...] = held[...]
        return
    size = held.shape[0] // len(order)
    for at, place in enumerate(order):
        start = pl.multiple_of(blocks[place] * size, size)
        turned[at * size:(at + 1) * size] = held[pl.ds(start, size)]


def put_blocks(made, keep, send, place):
    rows = made.shape[0] // 8
    for half, out in enumerate((keep, send)):
        for first in range(2):
            for second in range(2):
                at = (4 * half + 2 * first + second) * rows
                out[place(first, second)] = made[at:at + rows]


def feed_back_kernel(layer, pieces, joint, ties, blocks, grad_out, mixed, gain, shift, active, slope, *rest):
    count = len(pieces.arrays)
    refs, rest = rest[:count], rest[count + ties:]
    grads_count = 1 if joint else 2
    grad_mixed, sums, up_sums, *grads = rest[:3 + grads_count]
    up, down, low, low_turned, normed_turned, held, total, sems = rest[3 + grads_count:]
    shards, width = up.shape[3], up.shape[5]
    part = width // 3
    step = pl.program_id(0)
    wait = pieces.start_and_wait(refs, (up, down), blocks, sems)

    def put(kind, turned, right):
        made = dot(turned[...], right, 1, 0).astype(BF16)
        if joint:
            grads[0][0, kind] = made
            return
        for at in range(3):
            put_blocks(made[:, at * part:(at + 1) * part], *grads, lambda first, second: (0, at, kind, first, second))

    @pl.when(step == 0)
    def _():
        rows = grad_out[...].astype(F32)
        low[...] = rows.astype(BF16)
        sums[...] = jnp.zeros_like(sums)
        sums[0:1] = column_sum(rows)
        white, _ = whiten(mixed[...])
        normed = (white * gain[layer:layer + 1] + shift[layer:layer + 1]).astype(BF16)
        for value, turned in ((low[...], low_turned), (normed, normed_turned)):
            held[...] = value.T
            turn_rows(held, turned, blocks, None if joint else ROWS_ORDER)
        total[...] = jnp.zeros_like(total)

    wait()
    put(1, low_turned, active[0])
    upper = dot(low[...], down[:, :, :, step].reshape(width, width), 1, 1) * slope[0].astype(F32)
    up_sums[0] = column_sum(upper)
    upper_low = upper.astype(BF16)
    put(0, normed_turned, upper_low)
    total[...] += dot(upper_low, up[:, :, :, step].reshape(width, width), 1, 1)

    @pl.when(step == shards - 1)
    def _():
        white, inverse = whiten(mixed[...])
        grad = total[...]
        sums[1:2] = column_sum(grad * white)
        sums[2:3] = column_sum(grad)
        grad_mixed[...] = grad_out[...].astype(F32) + whiten_back(white, inverse, gain[layer:layer + 1], grad)


def feed_back(layer, grad_out, mixed, gain, shift, active, slope, pieces, joint, ties):
    rows, width = mixed.shape
    shards = active.shape[0]
    whole = lambda shape: pl.BlockSpec(shape, lambda step: (0,) * len(shape))
    each = lambda shape: pl.BlockSpec((1,) + shape, lambda step: (step,) + (0,) * len(shape))
    if joint:
        grads = [(2, width, width)]
    else:
        grads = [(3, 2, 2, 2, width // 8, width // 3)] * 2
    turned = pltpu.VMEM((width, rows), BF16)
    return pl.pallas_call(
        functools.partial(feed_back_kernel, layer, pieces, joint, len(ties)),
        grid=(shards,),
        out_shape=[jax.ShapeDtypeStruct((rows, width), F32), jax.ShapeDtypeStruct((8, width), F32),
                   jax.ShapeDtypeStruct((shards, 1, width), F32)]
        + [jax.ShapeDtypeStruct((shards,) + shape, BF16) for shape in grads],
        in_specs=[pl.BlockSpec(memory_space=pltpu.SMEM), whole((rows, width)), whole((rows, width)), whole(gain.shape),
                  whole(shift.shape), each((rows, width)), each((rows, width))]
        + [pl.BlockSpec(memory_space=pl.ANY)] * (len(pieces.arrays) + len(ties)),
        out_specs=[whole((rows, width)), whole((8, width)), each((1, width))] + [each(shape) for shape in grads],
        scratch_shapes=[*pieces.held(width),
                        pltpu.VMEM((rows, width), BF16), turned, turned, pltpu.VMEM((width, rows), BF16),
                        pltpu.VMEM((rows, width), F32), pltpu.SemaphoreType.DMA((len(pieces.plan),))],
        compiler_params=pltpu.CompilerParams(vmem_limit_bytes=VMEM_BYTES),
        cost_estimate=pl.CostEstimate(flops=32 * rows * width * width, bytes_accessed=30 * 2**20, transcendentals=0),
    )(pieces.blocks, grad_out, mixed, gain, shift, active, slope, *pieces.arrays, *ties)


def attend_back_kernel(layer, crossed, joint, blocks, grad_mixed, resid, gain, shift, gate, q, k, v, p, context, branch,
                       wq, wk, wv, wo, resid_out, sums, outs, grad_resid, grads, landing,
                       held, turning, turned, gc, gq, gk, gv, sems, out_sems):
    pages, slots = p.shape[0], p.shape[3]
    width = resid.shape[1]
    pairs = HEADS // 2
    pair_width = width // pairs
    scale = 1.0 / (width // HEADS) ** 0.5
    number = iter(range(16))
    arrive = lambda source, target: Arriving(source, target, sems.at[next(number)])
    land = iter(landing)
    context, grad_mixed = arrive(context, next(land)), arrive(grad_mixed, next(land))
    if crossed:
        branch = arrive(branch, next(land))
    w_out = arrive(wo.at[layer], held.at[0])
    v, p, k, q = (arrive(value, next(land)) for value in (v, p, k, q))
    resid = arrive(resid, next(land))
    w_query, w_key, w_value = (arrive(w.at[layer], held.at[at + 1]) for at, w in enumerate((wq, wk, wv)))
    leaving = Leaving(out_sems)
    sums[...] = jnp.zeros_like(sums)

    def put(at, right):
        made = dot(turned[...], right, 1, 0).astype(BF16)
        if joint:
            grads[0][at] = made
            return
        tile = width // 3
        for col in range(3):
            put_blocks(made[:, col * tile:(col + 1) * tile], *grads,
                       lambda first, second: (at // 2, first, second, at % 2, col))

    def turn(rows):
        turning[...] = rows.T
        turn_rows(turning, turned, blocks, None if joint else ROWS_ORDER)

    grad = grad_mixed[...]
    if crossed:
        opened = jax.nn.sigmoid(gate[...])
        sums[2:3] = column_sum(grad * branch[...].astype(F32)) * (opened * (1.0 - opened))
        low = (grad * opened).astype(BF16)
    else:
        low = grad.astype(BF16)
    turn(context[...])
    put(3, low)
    gc[...] = dot(low, w_out[...], 1, 1).astype(BF16)

    for page in range(pages):
        rows = slice(page * slots, (page + 1) * slots)
        for pair in range(pairs):
            cols = slice(pair * pair_width, (pair + 1) * pair_width)
            probs_low = p[page, pair]
            probs = probs_low.astype(F32).reshape(2, slots, slots)
            grad_probs = dot(split_heads(v[rows, cols]), gc[rows, cols], 1, 1).reshape(2, slots, slots)
            delta = jnp.sum(probs * grad_probs, axis=1, keepdims=True)
            grad_scores = (probs * (grad_probs - delta)).astype(BF16).reshape(2 * slots, slots)
            gq[rows, cols] = (dot(grad_scores, split_heads(k[rows, cols]), 0, 0) * scale).astype(BF16)
            gk[rows, cols] = join_heads(dot(grad_scores, q[rows, cols], 1, 0)).astype(BF16)
            gv[rows, cols] = join_heads(dot(probs_low, gc[rows, cols], 1, 0)).astype(BF16)

    white, inverse = whiten(resid[...].astype(F32))
    normed = (white * gain[layer:layer + 1] + shift[layer:layer + 1]).astype(BF16)
    turn(normed)
    put(2, gv[...])
    if not joint:
        for made, out in zip(grads, outs):
            leaving.send(made.at[1], out.at[1])
    put(0, gq[...])
    put(1, gk[...])
    for made, out in zip(grads, outs):
        if joint:
            leaving.send(made, out)
        else:
            leaving.send(made.at[0], out.at[0])
    total = dot(gq[...], w_query[...], 1, 1) + dot(gk[...], w_key[...], 1, 1) + dot(gv[...], w_value[...], 1, 1)
    sums[0:1] = column_sum(total * white)
    sums[1:2] = column_sum(total)
    grad_resid[...] = grad + whiten_back(white, inverse, gain[layer:layer + 1], total)
    leaving.send(grad_resid, resid_out)
    leaving.wait()


def attend_back(layer, crossed, grad_mixed, resid, gain, shift, gate, kept, weights, blocks, joint, ties):
    rows, width = resid.shape
    vmem = pl.BlockSpec(memory_space=pltpu.VMEM)
    kept = list(kept)
    given = 6 + len(kept) + 4
    if joint:
        grads = [jax.ShapeDtypeStruct((4, width, width), BF16)]
    else:
        grads = [jax.ShapeDtypeStruct((2, 2, 2, 2, 3, width // 8, width // 3), BF16)] * 2

    def body(*refs):
        ins, rest = list(refs[:given]), refs[given + len(ties):]
        if not crossed:
            ins.insert(11, None)
        count = len(grads)
        resid_out, sums, outs, resid_made, rest = rest[0], rest[1], rest[2:2 + count], rest[2 + count], rest[3 + count:]
        attend_back_kernel(layer, crossed, joint, *ins, resid_out, sums, outs, resid_made, rest[:count],
                           rest[count:count + len(landing)], *rest[count + len(landing):])

    low = pltpu.VMEM((rows, width), BF16)
    like = lambda value: pltpu.VMEM(value.shape, value.dtype)
    q, k, v, p, context, *branch = kept
    landing = [like(value) for value in (context, grad_mixed, *branch, v, p, k, q, resid)]
    anywhere = pl.BlockSpec(memory_space=pl.ANY)
    return pl.pallas_call(
        body,
        out_shape=[jax.ShapeDtypeStruct((rows, width), F32), jax.ShapeDtypeStruct((8, width), F32)] + grads,
        in_specs=[pl.BlockSpec(memory_space=pltpu.SMEM)] + [anywhere] * 2 + [vmem] * 3
        + [anywhere] * (len(kept) + 4 + len(ties)),
        out_specs=[anywhere, vmem] + [anywhere] * len(grads),
        scratch_shapes=[pltpu.VMEM((rows, width), F32)] + [like(grad) for grad in grads] + landing
        + [pltpu.VMEM((4, width, width), BF16), pltpu.VMEM((width, rows), BF16), pltpu.VMEM((width, rows), BF16),
           low, low, low, low, pltpu.SemaphoreType.DMA((16,)), pltpu.SemaphoreType.DMA((5,))],
        compiler_params=pltpu.CompilerParams(vmem_limit_bytes=VMEM_BYTES),
        cost_estimate=pl.CostEstimate(flops=16 * rows * width * width, bytes_accessed=24 * 2**20, transcendentals=0),
    )(blocks, grad_mixed, resid, gain, shift, gate, *kept, *weights, *ties)


def pack_kernel(layers, rows, block, bias, w_up, w_down, *rest):
    outs, sems = rest[:layers], rest[layers]
    start = pl.multiple_of(block[0] * rows, rows)
    sources = [w.at[layer, pl.ds(start, rows)] for layer in range(layers) for w in (w_up, w_down)]
    targets = [out.at[pl.ds(kind * rows, rows)] for out in outs for kind in range(2)]
    copies = start_copies(sources, targets, sems)
    for layer, out in enumerate(outs):
        out[2 * rows:] = bias_terms(bias[layer:layer + 1])
    for copy in copies:
        copy.wait()


def bias_terms(bias):
    top = bias.astype(BF16)
    left = bias - top.astype(F32)
    middle = left.astype(BF16)
    bottom = (left - middle.astype(F32)).astype(BF16)
    row = lax.broadcasted_iota(jnp.int32, (16, bias.shape[1]), 0)
    terms = [jnp.broadcast_to(term.astype(F32), row.shape) for term in (top, middle, bottom)]
    zero = jnp.zeros(row.shape, F32)
    chosen = jnp.where(row == 0, terms[0], jnp.where(row == 1, terms[1], jnp.where(row == 2, terms[2], zero)))
    return chosen.astype(BF16)


def pack(w_up, w_down, b_up, block):
    layers, width, shard = w_up.shape
    rows = width // 8
    out = jax.ShapeDtypeStruct((2 * rows + 16, shard), BF16)
    vmem = pl.BlockSpec(memory_space=pltpu.VMEM)
    return pl.pallas_call(
        functools.partial(pack_kernel, layers, rows),
        out_shape=[out] * layers,
        in_specs=[pl.BlockSpec(memory_space=pltpu.SMEM), vmem] + [pl.BlockSpec(memory_space=pl.ANY)] * 2,
        out_specs=[vmem] * layers,
        scratch_shapes=[pltpu.SemaphoreType.DMA((2 * layers,))],
        cost_estimate=pl.CostEstimate(flops=0, bytes_accessed=4 * layers * rows * shard * 4, transcendentals=0),
    )(block, b_up, w_up, w_down)


class Chain:
    def __init__(self, token):
        self.token, self.pending = token, []

    def need(self, *places):
        self.pending += places

    def tie(self, *values):
        count = len(values)
        out = lax.optimization_barrier((*values, self.token, *(held[key] for held, key in self.pending)))
        self.token = out[count]
        for (held, key), value in zip(self.pending, out[count + 1:]):
            held[key] = value
        self.pending = []
        return out[0] if count == 1 else out[:count]

    def ties(self):
        out, self.pending = [self.token] + [held[key] for held, key in self.pending], []
        return out


def places(values):
    return [(values, at) for at in range(len(values))]


def swap(value, axis, bit):
    size = lax.axis_size(axis)
    return lax.ppermute(value, axis, [(at, at ^ bit) for at in range(size)])


class Flow:
    def __init__(self, keep, index, bits, stages):
        self.wide, self.index, self.bits, self.stages, self.terms = [keep], list(index), bits, stages, []
        self.tile = keep.shape[-2:]

    def halve(self):
        bit, self.bits = self.bits[0], self.bits[1:]
        leaves = list(self.index)
        leaves[bit], self.index[bit] = 1, 0
        return tuple(leaves)

    def order(self, shape):
        open_dims = [dim for dim, at in enumerate(self.index) if at is None]
        ranked = list(self.bits) + [dim for dim in open_dims if dim not in self.bits]
        sizes = [shape[dim] for dim in open_dims]
        places = [()]
        for dim in ranked:
            places = [place + (at,) for place in places for at in range(shape[dim])]
        return sizes, [tuple(place[ranked.index(dim)] for dim in open_dims) for place in places]


def feed_flows(layer, grads):
    keep = grads[0].reshape((2, 2) + grads[0].shape[1:])
    dims = {"u": 0, "v": 1, "x": 4, "y": 5}
    return [Flow(keep, (None, None, at, None, None, None), tuple(dims[letter] for letter in stages), stages)
            for at, stages in enumerate(PART_STAGES[layer])]


def attend_flows(grads):
    return [Flow(grads[0], (at, None, None, None, None), bits, stages)
            for at, (bits, stages) in enumerate((((1, 2), "xy"), ((2, 1), "yx")))]


class Reads:
    def __init__(self):
        self.arrays = []

    def at(self, array):
        for at, known in enumerate(self.arrays):
            if known is array:
                return at
        self.arrays.append(array)
        return len(self.arrays) - 1

    def places(self, terms):
        return [(self.at(array), place) for array, place in terms]


def as_block(value):
    tile = value.shape[1] // 3
    parts = [value[:, at * tile:(at + 1) * tile] for at in range(3)]
    return jnp.concatenate(parts + [jnp.zeros_like(parts[0])], axis=0).astype(BF16)


def from_block(block):
    value = block.astype(F32)
    rows = value.shape[0] // 4
    return jnp.concatenate([value[at * rows:(at + 1) * rows] for at in range(3)], axis=1)


def add_small_parts(parts, blocks, out):
    out[...] = jnp.zeros_like(out)
    for layer in range(2):
        fed, attended, up = parts[3 * layer:3 * layer + 3]
        base = 10 * layer
        out[base:base + 3] = fed[0:3]
        out[base + 3:base + 6] = attended[0:3]
        for slot in range(len(SHARD_ORDER)):
            out[pl.ds(base + 6 + blocks[8 + slot], 1)] = up[slot]


def exchange_kernel(plan, blocks, *refs):
    (sizes, reads, sends, column_count, ends, small, small_terms, small_ends,
     array_count, small_count, tie_count) = plan
    arrays, refs = refs[:array_count], refs[array_count:]
    small_ins, refs = refs[:small_count], refs[small_count + tie_count:]
    outs, refs = refs[:len(sizes)], list(refs[len(sizes):])
    own = refs.pop(0) if column_count else None
    small_out = refs.pop(0) if small == "new" else None
    out_sems, sems = refs.pop(), refs.pop()
    mades = [refs.pop(0) for _ in sizes]
    copies, groups = [], []

    def fetch(source, target):
        copies.append(pltpu.make_async_copy(source, target, sems.at[len(copies)]))
        copies[-1].start()
        return copies[-1]

    for wide, _, terms, size in reads:
        held_wide = refs.pop(0)
        held = refs.pop(0) if terms else None
        waits = [fetch(arrays[array].at[index], held_wide.at[at]) for at, (array, index) in enumerate(wide)]
        waits += [fetch(arrays[array].at[pl.ds(place, size)], held.at[at]) for at, (array, place) in enumerate(terms)]
        groups.append((waits, held_wide, held))
    held_small = refs.pop(0) if small_terms else None
    small_waits = [fetch(arrays[array].at[pl.ds(place, 1)], held_small.at[at]) for at, (array, place) in enumerate(small_terms)]

    def arrive(number):
        waits, held_wide, held = groups[number]
        for copy in waits:
            copy.wait()
        wide, _, terms, _ = reads[number]
        return lambda block, place: [held_wide[(at,) + place] for at in range(len(wide))] + [
            held[at, block] for at in range(len(terms))]

    for number, (out, start, order) in enumerate(sends):
        values_of = arrive(number)
        for block, place in enumerate(order):
            values = values_of(block, place)
            while len(values) > 1:
                values = [values[at] + values[at + 1] if at + 1 < len(values) else values[at]
                          for at in range(0, len(values), 2)]
            mades[out][start + block] = values[0]
    if column_count:
        turned = refs.pop(0)
        shards = len(SHARD_ORDER)
        share = turned.shape[2] // 4
        for flow in range(column_count):
            values_of = arrive(len(sends) + flow)
            lines, tiles = reads[len(sends) + flow][1]
            for line in range(lines):
                parts = []
                for tile in range(tiles):
                    total = None
                    for value in values_of(line * tiles + tile, (line, tile)):
                        total = value.astype(F32) if total is None else total + value.astype(F32)
                    parts.append(total)
                whole = jnp.concatenate(parts, axis=1)
                to = (2 * flow + line) * share
                for shard in range(shards):
                    turned[shard ^ blocks[8], :, to:to + share] = whole[:, shard * share:(shard + 1) * share]
        own[...] = turned[0]
        tile = mades[0].shape[2]
        for other in range(1, shards):
            out, start = ends[other - 1]
            for cut in range(3):
                mades[out][start + cut] = turned[other, :, cut * tile:(cut + 1) * tile].astype(BF16)
    if small:
        if small == "new":
            add_small_parts(small_ins, blocks, small_out)
            total = small_out[...]
        else:
            total = small_ins[0][...]
            for copy in small_waits:
                copy.wait()
            for term in range(len(small_terms)):
                total = total + from_block(held_small[term, 0])
        for out, start in small_ends:
            mades[out][start] = as_block(total)
    leaving = [pltpu.make_async_copy(made, outs[at], out_sems.at[at]) for at, made in enumerate(mades)]
    for copy in leaving:
        copy.start()
    for copy in leaving:
        copy.wait()


def pause_kernel(source, out):
    out[...] = jnp.zeros_like(out)


def pause(value):
    return pl.pallas_call(
        pause_kernel,
        out_shape=jax.ShapeDtypeStruct((8, 128), F32),
        in_specs=[pl.BlockSpec(memory_space=pl.ANY)],
        out_specs=pl.BlockSpec(memory_space=pltpu.VMEM),
        compiler_params=pltpu.CompilerParams(vmem_limit_bytes=VMEM_BYTES),
    )(value)


class Rounds:
    def __init__(self, blocks):
        self.blocks, self.arrived = blocks, []

    def exchange(self, flows, ending=(), small=None, ties=(), crossing=(), alone=False):
        known, reads, sends, sizes = Reads(), [], [], {}

        def room(letter, size):
            place = sizes.get(letter, 0)
            sizes[letter] = place + size
            return list(sizes).index(letter), place

        def read(flow, index, skipped):
            shape = flow.wide[0].shape
            open_sizes, order = flow.order(shape)
            size = len(order)
            wide = [(known.at(array), tuple(slice(None) if at is None else at for at in index)) for array in flow.wide]
            reads.append((wide, open_sizes, [(known.at(array), start + skipped * size) for array, start in flow.terms], size))
            return size, order

        moved = []
        for flow in flows:
            letter, flow.stages = flow.stages[0], flow.stages[1:]
            size, order = read(flow, flow.halve(), 1)
            out, place = room(letter, size)
            sends.append((out, place, order))
            moved.append((flow.terms, letter, place))
        tile = flows[0].tile
        width = 3 * tile[1]
        for pair in ending:
            for flow in pair:
                read(flow, flow.index, 0)
        column_count = len(reads) - len(sends)
        ends = [room(letter, 3) for letter in "uvw"] if column_count else []
        mode, small_terms, small_ins, small_ends = "", [], [], []
        if small is not None:
            mode, letters = small.next()
            small_ins = small.parts if mode == "new" else [small.own]
            small_terms = [] if mode == "new" else known.places(small.terms)
            small_ends = [room(letter, 1) for letter in letters]
        order = list(sizes)
        outs = [jax.ShapeDtypeStruct((sizes[letter],) + tile, BF16) for letter in order]
        held = [pltpu.VMEM((sizes[letter],) + tile, BF16) for letter in order]
        for wide, open_sizes, terms, size in reads:
            held.append(pltpu.VMEM((len(wide), *open_sizes) + tile, BF16))
            if terms:
                held.append(pltpu.VMEM((len(terms), size) + tile, BF16))
        if small_terms:
            held.append(pltpu.VMEM((len(small_terms), 1) + tile, BF16))
        more = []
        if column_count:
            held.append(pltpu.VMEM((len(SHARD_ORDER), tile[0], width), F32))
            more.append(jax.ShapeDtypeStruct((tile[0], width), F32))
        if mode == "new":
            more.append(jax.ShapeDtypeStruct((24, width), F32))
        ties = [*self.arrived, *ties]
        copies = sum(len(wide) + len(terms) for wide, _, terms, _ in reads) + len(small_terms)
        anywhere, vmem = pl.BlockSpec(memory_space=pl.ANY), pl.BlockSpec(memory_space=pltpu.VMEM)
        plan = ([sizes[letter] for letter in order], reads, sends, column_count, ends, mode, small_terms, small_ends,
                len(known.arrays), len(small_ins), len(ties))
        made = list(pl.pallas_call(
            functools.partial(exchange_kernel, plan),
            out_shape=outs + more,
            in_specs=[pl.BlockSpec(memory_space=pltpu.SMEM)] + [anywhere] * len(known.arrays) + [vmem] * len(small_ins)
            + [anywhere] * len(ties),
            out_specs=[anywhere] * len(outs) + [vmem] * len(more),
            scratch_shapes=held + [pltpu.SemaphoreType.DMA((copies,)), pltpu.SemaphoreType.DMA((len(outs),))],
            compiler_params=pltpu.CompilerParams(vmem_limit_bytes=VMEM_BYTES),
        )(self.blocks, *known.arrays, *small_ins, *ties))
        rest = made[len(outs):]
        self.made = made[:len(outs)]
        going = lax.optimization_barrier(self.made + [send for _, send in crossing])
        arrived = {letter: swap(value, *LINKS[letter]) for letter, value in zip(order, going)}
        self.arrived = list(arrived.values())
        if alone:
            self.arrived.append(pause(going[0]))
        for (crossed, _), send in zip(crossing, going[len(outs):]):
            self.cross(crossed, send)
        for terms, letter, place in moved:
            terms.append((arrived[letter], place))
        for pair in ending:
            pair[0].own = rest.pop(0)
            pair[0].far = [(arrived[letter], place) for letter, (_, place) in zip("uvw", ends)]
        if mode:
            if mode == "new":
                small.own = rest.pop(0)
            small.terms += [(arrived[letter], place) for letter, (_, place) in zip(letters, small_ends)]

    def cross(self, flows, send):
        arrived = swap(send, *LINKS["c"])
        self.arrived.append(arrived)
        for flow in flows:
            flow.wide.append(arrived.reshape(flow.wide[0].shape))


class Small:
    def __init__(self, parts):
        self.parts, self.terms, self.stages = parts, [], ["c", "x", "uvw", "y"]

    def next(self):
        letters = self.stages.pop(0)
        return ("new" if letters == "c" else "old"), letters


def finish_kernel(plan, array_count, blocks, *refs):
    wides, feeds, far, small = plan
    arrays, refs = refs[:array_count], refs[array_count:]
    owns, small_own, refs = refs[:2], refs[2], refs[3:]
    up, down, *attends = refs[:6]
    smalls, gate, hidden = refs[6:11], refs[11], refs[12]
    held_wide, held, held_far, held_small, sems = refs[13:]
    copies = []

    def fetch(array, place, size, target):
        copies.append(pltpu.make_async_copy(arrays[array].at[pl.ds(place, size)], target, sems.at[len(copies)]))
        copies[-1].start()

    for layer, term, array in wides:
        copies.append(pltpu.make_async_copy(
            arrays[array].at[0, 0, :, :, 0, 0], held_wide.at[layer, term], sems.at[len(copies)]))
        copies[-1].start()
    for layer, part, term, array, place in feeds:
        fetch(array, place, 2, held.at[layer, part, term])
    for layer, other, array, place in far:
        fetch(array, place, 3, held_far.at[layer, other])
    for term, (array, place) in enumerate(small):
        fetch(array, place, 1, held_small.at[term])
    for copy in copies:
        copy.wait()
    terms, tile = held.shape[2], held.shape[5]
    for layer in range(2):
        for part in range(3):
            total = held_wide[layer, 0, part].astype(F32) + held_wide[layer, 1, part].astype(F32)
            for term in range(terms):
                total = total + held[layer, part, term].astype(F32)
            up[layer, :, part * tile:(part + 1) * tile] = total[0]
            down[layer, :, part * tile:(part + 1) * tile] = total[1]
        total = owns[layer][...]
        for other in range(3):
            total = total + jnp.concatenate([held_far[layer, other, cut].astype(F32) for cut in range(3)], axis=1)
        share = total.shape[1] // 4
        for at, out in enumerate(attends):
            out[layer] = total[:, at * share:(at + 1) * share]
    total = small_own[...]
    for term in range(len(small)):
        total = total + from_block(held_small[term, 0])
    lines = total.shape[1] // 8
    mine = jnp.where(blocks[0] == 0, total[:, :lines], 0.0)
    for place in range(1, 8):
        mine = mine + jnp.where(blocks[0] == place, total[:, place * lines:(place + 1) * lines], 0.0)
    for layer in range(2):
        base = 10 * layer
        for row, out in zip((3, 4, 1, 2, 0), smalls):
            out[layer:layer + 1] = mine[base + row:base + row + 1]
        shard = jnp.zeros((1, total.shape[1]), F32)
        for at in range(4):
            shard = shard + jnp.where(blocks[8] == at, total[base + 6 + at:base + 7 + at], 0.0)
        hidden[layer:layer + 1] = shard
    gate[...] = mine[5:6]


def finish(feeds, attends, small, blocks):
    reads = Reads()
    wide_plan = [(layer, term, reads.at(array)) for layer, flows in enumerate(feeds)
                 for term, array in enumerate(flows[0].wide)]
    feed_plan = [(layer, part, term, reads.at(array), place) for layer, flows in enumerate(feeds)
                 for part, flow in enumerate(flows) for term, (array, place) in enumerate(flow.terms)]
    far_plan = [(layer, other, reads.at(array), place) for layer, pair in enumerate(attends)
                for other, (array, place) in enumerate(pair[0].far)]
    small_plan = reads.places(small.terms)
    rows, tile = feeds[0][0].tile
    width, terms = 3 * tile, len(feeds[0][0].terms)
    anywhere, vmem = pl.BlockSpec(memory_space=pl.ANY), pl.BlockSpec(memory_space=pltpu.VMEM)
    return pl.pallas_call(
        functools.partial(finish_kernel, (wide_plan, feed_plan, far_plan, small_plan), len(reads.arrays)),
        out_shape=[jax.ShapeDtypeStruct((2, rows, width), F32)] * 2
        + [jax.ShapeDtypeStruct((2, rows, width // 4), F32)] * 4 + [jax.ShapeDtypeStruct((2, rows), F32)] * 5
        + [jax.ShapeDtypeStruct((1, rows), F32), jax.ShapeDtypeStruct((2, width), F32)],
        in_specs=[pl.BlockSpec(memory_space=pltpu.SMEM)] + [anywhere] * len(reads.arrays) + [vmem] * 3,
        out_specs=[vmem] * 13,
        scratch_shapes=[pltpu.VMEM((2, 2, 3, 2, rows, tile), BF16), pltpu.VMEM((2, 3, terms, 2, rows, tile), BF16),
                        pltpu.VMEM((2, 3, 3, rows, tile), BF16),
                        pltpu.VMEM((len(small_plan), 1, rows, tile), BF16),
                        pltpu.SemaphoreType.DMA((len(wide_plan) + len(feed_plan) + len(far_plan) + len(small_plan),))],
        compiler_params=pltpu.CompilerParams(vmem_limit_bytes=VMEM_BYTES),
    )(blocks, *reads.arrays, attends[0][0].own, attends[1][0].own, small.own)


def eighths(weights):
    return weights.reshape(weights.shape[:-2] + (2, 2, 2, weights.shape[-2] // 8, weights.shape[-1]))


def in_order(bit, own, other):
    first = (lax.axis_index("dp") & bit) == 0
    return jnp.stack([jnp.where(first, own, other), jnp.where(first, other, own)])


def far_pieces(layer, w_up, w_down, tails, halves, crossed, blocks):
    arrays = [eighths(w_up), eighths(w_down)] + halves + crossed
    every, rest = slice(None), pl.ds(1, len(tails) - 1)
    plan = [(kind, layer, kind, lambda me: (every, every, every, 0)) for kind in range(2)]
    for core in range(2):
        for second in range(2):
            plan.append((2 + 4 * core + second, None, 0, lambda me, core=core, second=second: (
                ((me >> 2) & 1) ^ second, every, (me & 1) ^ core, rest)))
            plan.append((4 + 4 * core + second, None, 1, lambda me, core=core, second=second: (
                every, ((me >> 1) & 1) ^ second, (me & 1) ^ core, rest)))
    return Pieces(arrays, plan, blocks, tails)


def gathered_pieces(layer, w_up, w_down, b_up, blocks):
    arrays = [eighths(lax.all_gather(weights[layer], "mp")) for weights in (w_up, w_down)]
    shards = arrays[0].shape[0]
    plan = [(kind, at, kind, lambda me, at=at: (slice(None),) * 3 + (at,)) for at in range(shards) for kind in range(2)]
    bias = lax.all_gather(b_up[layer:layer + 1], "mp")
    return Pieces(arrays, plan, blocks, [bias_terms(bias[at]) for at in range(shards)])


def sum_feed_anywhere(grads):
    both = lax.psum_scatter(grads, "mp", scatter_dimension=0, tiled=True)[0]
    both = lax.psum_scatter(both.astype(F32), "dp", scatter_dimension=1, tiled=True)
    return both[0], both[1].T


def sum_attend_anywhere(grads):
    whole = lax.psum_scatter(grads, "mp", scatter_dimension=2, tiled=True)
    return lax.psum_scatter(whole.astype(F32), "dp", scatter_dimension=1, tiled=True)


def shards(inputs, slot_valid, ln1_gain, ln1_bias, w_query, w_key, w_value, w_out, gate_logit,
           ln2_gain, ln2_bias, w_up, b_up, w_down, b_down, cotangent):
    pages, slots, width = inputs.shape
    dp, mp = lax.axis_size("dp"), lax.axis_size("mp")
    paired = dp == 8 and mp == 4 and width % (16 * dp) == 0
    if paired:
        blocks = jnp.concatenate([
            lax.axis_index("dp") ^ jnp.arange(8, dtype=jnp.int32),
            lax.axis_index("mp") ^ jnp.array(SHARD_ORDER, jnp.int32)])
    else:
        blocks = jnp.arange(2, dtype=jnp.int32)

    own_valid = lax.dynamic_slice_in_dim(slot_valid, lax.axis_index("mp") * pages, pages, 0) == 1
    key_text = lax.broadcasted_iota(jnp.int32, (slots, slots), 0) < TEXT
    query_text = lax.broadcasted_iota(jnp.int32, (slots, slots), 1) < TEXT
    live = jnp.broadcast_to(own_valid[:, :, None], (pages, slots, slots))
    masks = [
        jnp.where(jnp.logical_and(live, (key_text != query_text)[None]), 0.0, -1e30).astype(F32),
        jnp.where(live, 0.0, -1e30).astype(F32),
    ]
    gate = gate_logit[None]
    weights = (w_query, w_key, w_value, w_out)
    first_rows = inputs.reshape(pages * slots, width)
    cotangent = cotangent.reshape(pages * slots, width)
    got = {"grad": None}

    def attend_layer(layer, rows, ties):
        return attend(layer, layer == 0, rows, masks[layer], ln1_gain, ln1_bias, gate, weights, ties)

    def feed_layer(layer, rows, pieces, ties):
        return feed(layer, rows, ln2_gain, ln2_bias, b_down, pieces, (F32, BF16)[layer], ties)

    def feed_back_layer(layer, ties):
        rows, active, slope, pieces = got["feed", layer]
        got["mixed_grad"], got["feed_sums", layer], got["up_sums", layer], *got["feed_grads", layer] = feed_back(
            layer, (got["grad"], cotangent)[layer], rows, ln2_gain, ln2_bias, active, slope, pieces, not paired, ties)

    def attend_back_layer(layer, ties):
        rows, kept = got["attend", layer]
        got["grad"], got["attend_sums", layer], *got["attend_grads", layer] = attend_back(
            layer, layer == 0, got["mixed_grad"], rows, ln1_gain, ln1_bias, gate, (*kept[:5], *kept[6:]), weights,
            blocks, not paired, ties)

    if paired:
        owns = pack(w_up, w_down, b_up, blocks)
        rows = width // 8
        chain = Chain(owns[0])
        far = lambda own: [swap(own, "mp", other) for other in SHARD_ORDER[1:]]
        split = lambda pieces: (jnp.stack([piece[:rows] for piece in pieces]),
                                jnp.stack([piece[rows:2 * rows] for piece in pieces]))
        other_core = lambda *values: [swap(value, "dp", 1) for value in values]

        far_0 = far(owns[0])
        kept_0 = list(attend_layer(0, first_rows, ()))
        chain.need((kept_0, 5))
        far_0 = list(chain.tie(*far_0))
        ups, downs = chain.tie(*split(far_0))
        near_0 = [swap(ups, "dp", 2), swap(downs, "dp", 4)]
        far_1 = far(chain.tie(owns[1]))
        near_0 = chain.tie(*near_0)
        ups_0, downs_0 = chain.tie(in_order(2, ups, near_0[0]), in_order(4, downs, near_0[1]))
        side_0 = [swap(ups_0, "dp", 4), swap(downs_0, "dp", 2)]
        ups_0, downs_0, *side_0 = chain.tie(ups_0, downs_0, *side_0)
        far_1 = list(chain.tie(*far_1))
        ups, downs = chain.tie(*split(far_1))
        near_1 = [swap(ups, "dp", 2), swap(downs, "dp", 4)]
        core_0 = other_core(ups_0, side_0[0], downs_0, side_0[1])
        pieces_0 = far_pieces(0, w_up, w_down, [owns[0]] + far_0, [ups_0, side_0[0], downs_0, side_0[1]], core_0, blocks)
        fed_0 = list(feed_layer(0, kept_0[5], pieces_0, chain.ties()))
        chain.need((fed_0, 0))
        near_1 = chain.tie(*near_1)
        result_0, active_0, slope_0 = fed_0
        ups_1, downs_1 = chain.tie(in_order(2, ups, near_1[0]), in_order(4, downs, near_1[1]))
        side_1 = [swap(ups_1, "dp", 4), swap(downs_1, "dp", 2)]
        kept_1 = list(attend_layer(1, result_0, chain.ties()))
        chain.need((kept_1, 5))
        side_1 = chain.tie(*side_1)
        core_1 = other_core(ups_1, side_1[0], downs_1, side_1[1])
        pieces_1 = far_pieces(1, w_up, w_down, [owns[1]] + far_1, [ups_1, side_1[0], downs_1, side_1[1]], core_1, blocks)
    else:
        pieces_0 = gathered_pieces(0, w_up, w_down, b_up, blocks)
        pieces_1 = gathered_pieces(1, w_up, w_down, b_up, blocks)
        kept_0 = attend_layer(0, first_rows, ())
        result_0, active_0, slope_0 = feed_layer(0, kept_0[5], pieces_0, ())
        kept_1 = attend_layer(1, result_0, ())

    result_1, active_1, slope_1 = feed_layer(1, kept_1[5], pieces_1, ())
    got["feed", 0] = kept_0[5], active_0, slope_0, pieces_0
    got["feed", 1] = kept_1[5], active_1, slope_1, pieces_1
    got["attend", 0], got["attend", 1] = (first_rows, kept_0), (result_0, kept_1)

    if paired:
        rounds = Rounds(blocks)
        feed_back_layer(1, ())
        feeds, attends = {1: feed_flows(1, got["feed_grads", 1])}, {}
        rounds.cross(feeds[1], got["feed_grads", 1][1])
        attend_back_layer(1, ())
        attends[1] = attend_flows(got["attend_grads", 1])
        rounds.exchange(feeds[1], ties=[got["attend_sums", 1]], crossing=[(attends[1], got["attend_grads", 1][1])])
        feed_back_layer(0, rounds.made)
        feeds[0] = feed_flows(0, got["feed_grads", 0])
        rounds.exchange(feeds[1] + attends[1], ties=[got["feed_sums", 0]], crossing=[(feeds[0], got["feed_grads", 0][1])])
        attend_back_layer(0, rounds.made)
        attends[0] = attend_flows(got["attend_grads", 0])
        small = Small([got[name, layer] for layer in (0, 1) for name in ("feed_sums", "attend_sums", "up_sums")])
        rounds.exchange(feeds[0] + feeds[1] + attends[1], small=small, crossing=[(attends[0], got["attend_grads", 0][1])], alone=True)
        rounds.exchange(feeds[0] + attends[0] + feeds[1], [attends[1]], small, alone=True)
        rounds.exchange(feeds[0] + attends[0], small=small, alone=True)
        rounds.exchange(feeds[0], [attends[0]], small, alone=True)
        up_grad, down_turned, *rest = finish([feeds[0], feeds[1]], [attends[0], attends[1]], small, blocks)
        down_grad = jnp.swapaxes(down_turned, 1, 2)
        attend_grads, small_grads, gate_grad, bup_grad = rest[:4], rest[4:9], rest[9][0], rest[10]
    else:
        for layer in (1, 0):
            feed_back_layer(layer, ())
            attend_back_layer(layer, ())
        feed_grads = [sum_feed_anywhere(got["feed_grads", layer][0]) for layer in (0, 1)]
        up_grad, down_grad = (jnp.stack([feed_grads[layer][at] for layer in (0, 1)]) for at in range(2))
        sums = [sum_attend_anywhere(got["attend_grads", layer][0]) for layer in (0, 1)]
        attend_grads = [jnp.stack([sums[0][at], sums[1][at]]) for at in range(4)]
        both = lax.psum(jnp.concatenate([part for layer in (0, 1) for part in (
            got["feed_sums", layer][:3], got["attend_sums", layer][:3], got["up_sums", layer][:, 0])]), ("dp", "mp"))
        later, lines, me = both.shape[0] // 2, width // dp, lax.axis_index("mp")
        mine = lax.dynamic_slice_in_dim(both, lax.axis_index("dp") * lines, lines, 1)
        small_grads = [jnp.stack([mine[row], mine[later + row]]) for row in (3, 4, 1, 2, 0)]
        gate_grad = mine[5]
        bup_grad = jnp.concatenate([lax.dynamic_slice_in_dim(both, row + me, 1, 0) for row in (6, later + 6)])

    return (
        result_1.reshape(pages, slots, width),
        got["grad"].reshape(pages, slots, width),
        small_grads[0],
        small_grads[1],
        *attend_grads,
        gate_grad,
        small_grads[2],
        small_grads[3],
        up_grad,
        bup_grad,
        down_grad,
        small_grads[4],
    )


def solution(mesh):
    rows = P(("dp", "mp"), None, None)
    return jax.shard_map(
        shards,
        mesh=mesh,
        in_specs=(rows, P("dp", None), P(), P(), P(), P(), P(), P(), P(), P(), P(), P(None, None, "mp"),
                  P(None, "mp"), P(None, "mp", None), P(), rows),
        out_specs=(rows, rows, P(None, "dp"), P(None, "dp"), P(None, "dp", "mp"), P(None, "dp", "mp"),
                   P(None, "dp", "mp"), P(None, "dp", "mp"), P("dp"), P(None, "dp"), P(None, "dp"),
                   P(None, "dp", "mp"), P(None, "mp"), P(None, "mp", "dp"), P(None, "dp")),
        check_vma=False,
    )
```

```python
import functools

import jax
import jax.numpy as jnp
from jax import lax
from jax.experimental import pallas as pl
from jax.experimental.pallas import tpu as pltpu
from jax.sharding import PartitionSpec as P

HEADS = 12
TEXT = 112
F32 = jnp.float32
BF16 = jnp.bfloat16
VMEM_BYTES = 62 * 2**20


def dot(a, b, a_dim, b_dim):
    return lax.dot_general(a, b, (((a_dim,), (b_dim,)), ((), ())), preferred_element_type=F32)


def whiten(rows):
    centered = rows - jnp.mean(rows, axis=-1, keepdims=True)
    spread = jnp.mean(centered * centered, axis=-1, keepdims=True)
    inverse = lax.rsqrt(spread + 1e-05)
    return centered * inverse, inverse


def whiten_back(white, inverse, gain, grad):
    scaled = grad * gain
    first = jnp.mean(scaled, axis=-1, keepdims=True)
    second = jnp.mean(scaled * white, axis=-1, keepdims=True)
    return inverse * (scaled - first - white * second)


def column_sum(rows):
    return jnp.sum(rows, axis=0, keepdims=True)


def gelu_and_slope(values):
    size = jnp.abs(values)
    t = 1.0 / (1.0 + (0.3275911 * 0.7071067811865476) * size)
    bell = jnp.exp(-0.5 * values * values)
    poly = 0.5 * 1.061405429
    poly = poly * t + 0.5 * -1.453152027
    poly = poly * t + 0.5 * 1.421413741
    poly = poly * t + 0.5 * -0.284496736
    poly = poly * t + 0.5 * 0.254829592
    tail = poly * t * bell
    phi = jnp.where(values >= 0.0, 1.0 - tail, tail)
    return values * phi, phi + values * bell * 0.3989422804014327


def split_heads(pair):
    lane = lax.broadcasted_iota(jnp.int32, pair.shape, 1)
    first = lane < pair.shape[1] // 2
    zero = jnp.zeros_like(pair)
    return jnp.concatenate([jnp.where(first, pair, zero), jnp.where(first, zero, pair)], axis=0)


def join_heads(both):
    slots = both.shape[0] // 2
    lane = lax.broadcasted_iota(jnp.int32, (slots, both.shape[1]), 1)
    return jnp.where(lane < both.shape[1] // 2, both[:slots], both[slots:])


def start_copies(sources, targets, sems):
    copies = [
        pltpu.make_async_copy(source, target, sems.at[at])
        for at, (source, target) in enumerate(zip(sources, targets))
    ]
    for copy in copies:
        copy.start()
    return copies


class Arriving:
    def __init__(self, source, held, sem):
        self.copy, self.held, self.here = pltpu.make_async_copy(source, held, sem), held, False
        self.copy.start()

    def __getitem__(self, at):
        if not self.here:
            self.copy.wait()
            self.here = True
        return self.held[at]


class Leaving:
    def __init__(self, sems):
        self.sems, self.copies = sems, []

    def send(self, held, target):
        self.copies.append(pltpu.make_async_copy(held, target, self.sems.at[len(self.copies)]))
        self.copies[-1].start()

    def wait(self):
        for copy in self.copies:
            copy.wait()


def attend_kernel(layer, crossed, resid, mask, gain, shift, gate, wq, wk, wv, wo,
                  outs, made, held, sems, out_sems):
    q_out, k_out, v_out, p_out, c_out, mixed, *branch_out = made
    leaving = Leaving(out_sems)
    pages, slots = mask.shape[0], mask.shape[1]
    width = resid.shape[1]
    pairs = HEADS // 2
    pair_width = width // pairs
    scale = 1.0 / (width // HEADS) ** 0.5
    copies = start_copies(
        [w.at[layer] for w in (wq, wk, wv, wo)], [held.at[at] for at in range(4)], sems
    )
    white, _ = whiten(resid[...].astype(F32))
    normed = (white * gain[layer:layer + 1] + shift[layer:layer + 1]).astype(BF16)
    copies[0].wait()
    q_out[...] = (dot(normed, held[0], 1, 0).astype(BF16).astype(F32) * scale).astype(BF16)
    leaving.send(q_out, outs[0])
    copies[1].wait()
    k_out[...] = dot(normed, held[1], 1, 0).astype(BF16)
    leaving.send(k_out, outs[1])
    copies[2].wait()
    v_out[...] = dot(normed, held[2], 1, 0).astype(BF16)
    leaving.send(v_out, outs[2])

    for page in range(pages):
        rows = slice(page * slots, (page + 1) * slots)
        bias = mask[page]
        for pair in range(pairs):
            cols = slice(pair * pair_width, (pair + 1) * pair_width)
            scores = dot(split_heads(k_out[rows, cols]), q_out[rows, cols], 1, 1)
            scores = scores.reshape(2, slots, slots) + bias[None]
            top = jnp.max(scores, axis=1, keepdims=True)
            raised = jnp.exp(scores - top)
            probs = raised * (1.0 / jnp.sum(raised, axis=1, keepdims=True))
            probs = probs.reshape(2 * slots, slots).astype(BF16)
            p_out[page, pair] = probs
            c_out[rows, cols] = dot(probs, split_heads(v_out[rows, cols]), 0, 0).astype(BF16)
        leaving.send(p_out.at[page], outs[3].at[page])
    leaving.send(c_out, outs[4])
    copies[3].wait()
    for page in range(pages):
        rows = slice(page * slots, (page + 1) * slots)
        branch = dot(c_out[rows], held[3], 1, 0)
        if crossed:
            branch_out[0][rows] = branch.astype(BF16)
            branch = branch * jax.nn.sigmoid(gate[...])
            leaving.send(branch_out[0].at[rows], outs[6].at[rows])
        mixed[rows] = resid[rows].astype(F32) + branch
        leaving.send(mixed.at[rows], outs[5].at[rows])
    leaving.wait()


def attend(layer, crossed, resid, mask, gain, shift, gate, weights, ties):
    rows, width = resid.shape
    pages, slots = mask.shape[:2]
    low = jax.ShapeDtypeStruct((rows, width), BF16)
    vmem = pl.BlockSpec(memory_space=pltpu.VMEM)
    outs = [low, low, low, jax.ShapeDtypeStruct((pages, HEADS // 2, 2 * slots, slots), BF16), low,
            jax.ShapeDtypeStruct((rows, width), F32)]
    if crossed:
        outs.append(low)

    def body(*refs):
        ins, rest = refs[:9], refs[9 + len(ties):]
        attend_kernel(layer, crossed, *ins, rest[:len(outs)], rest[len(outs):2 * len(outs)], *rest[2 * len(outs):])

    return pl.pallas_call(
        body,
        out_shape=outs,
        in_specs=[vmem] * 5 + [pl.BlockSpec(memory_space=pl.ANY)] * (4 + len(ties)),
        out_specs=[pl.BlockSpec(memory_space=pl.ANY)] * len(outs),
        scratch_shapes=[pltpu.VMEM(out.shape, out.dtype) for out in outs]
        + [pltpu.VMEM((4, width, width), BF16), pltpu.SemaphoreType.DMA((4,)),
           pltpu.SemaphoreType.DMA((4 + (2 + crossed) * pages,))],
        compiler_params=pltpu.CompilerParams(vmem_limit_bytes=VMEM_BYTES),
        cost_estimate=pl.CostEstimate(flops=8 * rows * width * width, bytes_accessed=14 * 2**20, transcendentals=0),
    )(resid, mask, gain, shift, gate, *weights, *ties)


class Pieces:
    def __init__(self, arrays, plan, blocks, tails):
        self.arrays, self.plan, self.blocks, self.tails = arrays, plan, blocks, tails

    def copies(self, refs, held, blocks, sems, first=0, last=None):
        return [
            pltpu.make_async_copy(refs[array] if index is None else refs[array].at[index],
                                  held[kind].at[target(blocks[0])], sems.at[at])
            for at, (array, index, kind, target) in list(enumerate(self.plan))[first:last]
        ]

    def held(self, width):
        shape = (2, 2, 2, len(self.tails), width // 8, width)
        return [pltpu.VMEM(shape, BF16), pltpu.VMEM(shape, BF16)]

    def tail_specs(self, width):
        return [pl.BlockSpec((16, width), lambda step, last=tail.shape[0] // 16 - 1: (last, 0)) for tail in self.tails]

    def start_and_wait(self, refs, held, blocks, sems):
        step = pl.program_id(0)

        @pl.when(step == 0)
        def _():
            for copy in self.copies(refs, held, blocks, sems):
                copy.start()

        def wait():
            @pl.when(step == 0)
            def _():
                for copy in self.copies(refs, held, blocks, sems, 0, 2):
                    copy.wait()

            @pl.when(step == 1)
            def _():
                for copy in self.copies(refs, held, blocks, sems, 2):
                    copy.wait()
        return wait


def feed_kernel(layer, pieces, ties, blocks, mixed, gain, shift, b_down, *rest):
    count = len(pieces.arrays)
    tails, rest = rest[:len(pieces.tails)], rest[len(pieces.tails):]
    refs, rest = rest[:count], rest[count + ties:]
    result, active_out, slope_out, up, down, low, total, bias, sems = rest
    shards, width = up.shape[3], up.shape[5]
    step = pl.program_id(0)
    wait = pieces.start_and_wait(refs, (up, down), blocks, sems)

    @pl.when(step == 0)
    def _():
        white, _ = whiten(mixed[...])
        low[...] = (white * gain[layer:layer + 1] + shift[layer:layer + 1]).astype(BF16)
        total[...] = mixed[...] + b_down[layer:layer + 1]
        for at, tail in enumerate(tails):
            bias[at] = column_sum(tail[...].astype(F32))

    wait()
    parts = 3
    part = width // parts
    for at in range(parts):
        cols = slice(at * part, (at + 1) * part)
        upper = dot(low[...], up[:, :, :, step, :, cols].reshape(width, part), 1, 0) + bias[step, :, cols]
        active, slope = gelu_and_slope(upper)
        active = active.astype(BF16)
        active_out[0, :, cols] = active
        slope_out[0, :, cols] = slope.astype(BF16)
        total[...] += dot(active, down[:, :, :, step].reshape(width, width)[cols], 1, 0)

    @pl.when(step == shards - 1)
    def _():
        result[...] = total[...].astype(result.dtype)


def feed(layer, mixed, gain, shift, b_down, pieces, out_type, ties):
    rows, width = mixed.shape
    shards = len(pieces.tails)
    whole = lambda shape: pl.BlockSpec(shape, lambda step: (0,) * len(shape))
    each = lambda shape: pl.BlockSpec((1,) + shape, lambda step: (step,) + (0,) * len(shape))
    return pl.pallas_call(
        functools.partial(feed_kernel, layer, pieces, len(ties)),
        grid=(shards,),
        out_shape=[jax.ShapeDtypeStruct((rows, width), out_type)]
        + [jax.ShapeDtypeStruct((shards, rows, width), BF16)] * 2,
        in_specs=[pl.BlockSpec(memory_space=pltpu.SMEM), whole((rows, width)), whole(gain.shape), whole(shift.shape),
                  whole(b_down.shape)] + pieces.tail_specs(width)
        + [pl.BlockSpec(memory_space=pl.ANY)] * (len(pieces.arrays) + len(ties)),
        out_specs=[whole((rows, width)), each((rows, width)), each((rows, width))],
        scratch_shapes=[*pieces.held(width),
                        pltpu.VMEM((rows, width), BF16), pltpu.VMEM((rows, width), F32),
                        pltpu.VMEM((shards, 1, width), F32), pltpu.SemaphoreType.DMA((len(pieces.plan),))],
        compiler_params=pltpu.CompilerParams(vmem_limit_bytes=VMEM_BYTES),
        cost_estimate=pl.CostEstimate(flops=16 * rows * width * width, bytes_accessed=20 * 2**20, transcendentals=0),
    )(pieces.blocks, mixed, gain, shift, b_down, *pieces.tails, *pieces.arrays, *ties)


ROWS_ORDER = (0, 4, 2, 6, 1, 5, 3, 7)
PART_STAGES = (("xyvu", "yuxv", "uxyv"), ("xyvu", "yuxv", "uxyv"))
SHARD_ORDER = (0, 2, 1, 3)
LINKS = {"c": ("dp", 1), "x": ("dp", 2), "y": ("dp", 4), "u": ("mp", 1), "v": ("mp", 2), "w": ("mp", 3)}


def turn_rows(held, turned, blocks, order):
    if order is None:
        turned[...] = held[...]
        return
    size = held.shape[0] // len(order)
    for at, place in enumerate(order):
        start = pl.multiple_of(blocks[place] * size, size)
        turned[at * size:(at + 1) * size] = held[pl.ds(start, size)]


def put_blocks(made, keep, send, place):
    rows = made.shape[0] // 8
    for half, out in enumerate((keep, send)):
        for first in range(2):
            for second in range(2):
                at = (4 * half + 2 * first + second) * rows
                out[place(first, second)] = made[at:at + rows]


def feed_back_kernel(layer, pieces, joint, ties, blocks, grad_out, mixed, gain, shift, active, slope, *rest):
    count = len(pieces.arrays)
    refs, rest = rest[:count], rest[count + ties:]
    grads_count = 1 if joint else 2
    grad_mixed, sums, up_sums, *grads = rest[:3 + grads_count]
    up, down, low, low_turned, normed_turned, held, total, sems = rest[3 + grads_count:]
    shards, width = up.shape[3], up.shape[5]
    part = width // 3
    step = pl.program_id(0)
    wait = pieces.start_and_wait(refs, (up, down), blocks, sems)

    def put(kind, turned, right):
        made = dot(turned[...], right, 1, 0).astype(BF16)
        if joint:
            grads[0][0, kind] = made
            return
        for at in range(3):
            put_blocks(made[:, at * part:(at + 1) * part], *grads, lambda first, second: (0, at, kind, first, second))

    @pl.when(step == 0)
    def _():
        rows = grad_out[...].astype(F32)
        low[...] = rows.astype(BF16)
        sums[...] = jnp.zeros_like(sums)
        sums[0:1] = column_sum(rows)
        white, _ = whiten(mixed[...])
        normed = (white * gain[layer:layer + 1] + shift[layer:layer + 1]).astype(BF16)
        for value, turned in ((low[...], low_turned), (normed, normed_turned)):
            held[...] = value.T
            turn_rows(held, turned, blocks, None if joint else ROWS_ORDER)
        total[...] = jnp.zeros_like(total)

    wait()
    put(1, low_turned, active[0])
    upper = dot(low[...], down[:, :, :, step].reshape(width, width), 1, 1) * slope[0].astype(F32)
    up_sums[0] = column_sum(upper)
    upper_low = upper.astype(BF16)
    put(0, normed_turned, upper_low)
    total[...] += dot(upper_low, up[:, :, :, step].reshape(width, width), 1, 1)

    @pl.when(step == shards - 1)
    def _():
        white, inverse = whiten(mixed[...])
        grad = total[...]
        sums[1:2] = column_sum(grad * white)
        sums[2:3] = column_sum(grad)
        grad_mixed[...] = grad_out[...].astype(F32) + whiten_back(white, inverse, gain[layer:layer + 1], grad)


def feed_back(layer, grad_out, mixed, gain, shift, active, slope, pieces, joint, ties):
    rows, width = mixed.shape
    shards = active.shape[0]
    whole = lambda shape: pl.BlockSpec(shape, lambda step: (0,) * len(shape))
    each = lambda shape: pl.BlockSpec((1,) + shape, lambda step: (step,) + (0,) * len(shape))
    if joint:
        grads = [(2, width, width)]
    else:
        grads = [(3, 2, 2, 2, width // 8, width // 3)] * 2
    turned = pltpu.VMEM((width, rows), BF16)
    return pl.pallas_call(
        functools.partial(feed_back_kernel, layer, pieces, joint, len(ties)),
        grid=(shards,),
        out_shape=[jax.ShapeDtypeStruct((rows, width), F32), jax.ShapeDtypeStruct((8, width), F32),
                   jax.ShapeDtypeStruct((shards, 1, width), F32)]
        + [jax.ShapeDtypeStruct((shards,) + shape, BF16) for shape in grads],
        in_specs=[pl.BlockSpec(memory_space=pltpu.SMEM), whole((rows, width)), whole((rows, width)), whole(gain.shape),
                  whole(shift.shape), each((rows, width)), each((rows, width))]
        + [pl.BlockSpec(memory_space=pl.ANY)] * (len(pieces.arrays) + len(ties)),
        out_specs=[whole((rows, width)), whole((8, width)), each((1, width))] + [each(shape) for shape in grads],
        scratch_shapes=[*pieces.held(width),
                        pltpu.VMEM((rows, width), BF16), turned, turned, pltpu.VMEM((width, rows), BF16),
                        pltpu.VMEM((rows, width), F32), pltpu.SemaphoreType.DMA((len(pieces.plan),))],
        compiler_params=pltpu.CompilerParams(vmem_limit_bytes=VMEM_BYTES),
        cost_estimate=pl.CostEstimate(flops=32 * rows * width * width, bytes_accessed=30 * 2**20, transcendentals=0),
    )(pieces.blocks, grad_out, mixed, gain, shift, active, slope, *pieces.arrays, *ties)


def attend_back_kernel(layer, crossed, joint, blocks, grad_mixed, resid, gain, shift, gate, q, k, v, p, context, branch,
                       wq, wk, wv, wo, resid_out, sums, outs, grad_resid, grads, landing,
                       held, turning, turned, gc, gq, gk, gv, sems, out_sems):
    pages, slots = p.shape[0], p.shape[3]
    width = resid.shape[1]
    pairs = HEADS // 2
    pair_width = width // pairs
    scale = 1.0 / (width // HEADS) ** 0.5
    number = iter(range(16))
    arrive = lambda source, target: Arriving(source, target, sems.at[next(number)])
    land = iter(landing)
    context, grad_mixed = arrive(context, next(land)), arrive(grad_mixed, next(land))
    if crossed:
        branch = arrive(branch, next(land))
    w_out = arrive(wo.at[layer], held.at[0])
    v, p, k, q = (arrive(value, next(land)) for value in (v, p, k, q))
    resid = arrive(resid, next(land))
    w_query, w_key, w_value = (arrive(w.at[layer], held.at[at + 1]) for at, w in enumerate((wq, wk, wv)))
    leaving = Leaving(out_sems)
    sums[...] = jnp.zeros_like(sums)

    def put(at, right):
        made = dot(turned[...], right, 1, 0).astype(BF16)
        if joint:
            grads[0][at] = made
            return
        tile = width // 3
        for col in range(3):
            put_blocks(made[:, col * tile:(col + 1) * tile], *grads,
                       lambda first, second: (at // 2, first, second, at % 2, col))

    def turn(rows):
        turning[...] = rows.T
        turn_rows(turning, turned, blocks, None if joint else ROWS_ORDER)

    grad = grad_mixed[...]
    if crossed:
        opened = jax.nn.sigmoid(gate[...])
        sums[2:3] = column_sum(grad * branch[...].astype(F32)) * (opened * (1.0 - opened))
        low = (grad * opened).astype(BF16)
    else:
        low = grad.astype(BF16)
    turn(context[...])
    put(3, low)
    gc[...] = dot(low, w_out[...], 1, 1).astype(BF16)

    for page in range(pages):
        rows = slice(page * slots, (page + 1) * slots)
        for pair in range(pairs):
            cols = slice(pair * pair_width, (pair + 1) * pair_width)
            probs_low = p[page, pair]
            probs = probs_low.astype(F32).reshape(2, slots, slots)
            grad_probs = dot(split_heads(v[rows, cols]), gc[rows, cols], 1, 1).reshape(2, slots, slots)
            delta = jnp.sum(probs * grad_probs, axis=1, keepdims=True)
            grad_scores = (probs * (grad_probs - delta)).astype(BF16).reshape(2 * slots, slots)
            gq[rows, cols] = (dot(grad_scores, split_heads(k[rows, cols]), 0, 0) * scale).astype(BF16)
            gk[rows, cols] = join_heads(dot(grad_scores, q[rows, cols], 1, 0)).astype(BF16)
            gv[rows, cols] = join_heads(dot(probs_low, gc[rows, cols], 1, 0)).astype(BF16)

    white, inverse = whiten(resid[...].astype(F32))
    normed = (white * gain[layer:layer + 1] + shift[layer:layer + 1]).astype(BF16)
    turn(normed)
    put(2, gv[...])
    if not joint:
        for made, out in zip(grads, outs):
            leaving.send(made.at[1], out.at[1])
    put(0, gq[...])
    put(1, gk[...])
    for made, out in zip(grads, outs):
        if joint:
            leaving.send(made, out)
        else:
            leaving.send(made.at[0], out.at[0])
    total = dot(gq[...], w_query[...], 1, 1) + dot(gk[...], w_key[...], 1, 1) + dot(gv[...], w_value[...], 1, 1)
    sums[0:1] = column_sum(total * white)
    sums[1:2] = column_sum(total)
    grad_resid[...] = grad + whiten_back(white, inverse, gain[layer:layer + 1], total)
    leaving.send(grad_resid, resid_out)
    leaving.wait()


def attend_back(layer, crossed, grad_mixed, resid, gain, shift, gate, kept, weights, blocks, joint, ties):
    rows, width = resid.shape
    vmem = pl.BlockSpec(memory_space=pltpu.VMEM)
    kept = list(kept)
    given = 6 + len(kept) + 4
    if joint:
        grads = [jax.ShapeDtypeStruct((4, width, width), BF16)]
    else:
        grads = [jax.ShapeDtypeStruct((2, 2, 2, 2, 3, width // 8, width // 3), BF16)] * 2

    def body(*refs):
        ins, rest = list(refs[:given]), refs[given + len(ties):]
        if not crossed:
            ins.insert(11, None)
        count = len(grads)
        resid_out, sums, outs, resid_made, rest = rest[0], rest[1], rest[2:2 + count], rest[2 + count], rest[3 + count:]
        attend_back_kernel(layer, crossed, joint, *ins, resid_out, sums, outs, resid_made, rest[:count],
                           rest[count:count + len(landing)], *rest[count + len(landing):])

    low = pltpu.VMEM((rows, width), BF16)
    like = lambda value: pltpu.VMEM(value.shape, value.dtype)
    q, k, v, p, context, *branch = kept
    landing = [like(value) for value in (context, grad_mixed, *branch, v, p, k, q, resid)]
    anywhere = pl.BlockSpec(memory_space=pl.ANY)
    return pl.pallas_call(
        body,
        out_shape=[jax.ShapeDtypeStruct((rows, width), F32), jax.ShapeDtypeStruct((8, width), F32)] + grads,
        in_specs=[pl.BlockSpec(memory_space=pltpu.SMEM)] + [anywhere] * 2 + [vmem] * 3
        + [anywhere] * (len(kept) + 4 + len(ties)),
        out_specs=[anywhere, vmem] + [anywhere] * len(grads),
        scratch_shapes=[pltpu.VMEM((rows, width), F32)] + [like(grad) for grad in grads] + landing
        + [pltpu.VMEM((4, width, width), BF16), pltpu.VMEM((width, rows), BF16), pltpu.VMEM((width, rows), BF16),
           low, low, low, low, pltpu.SemaphoreType.DMA((16,)), pltpu.SemaphoreType.DMA((5,))],
        compiler_params=pltpu.CompilerParams(vmem_limit_bytes=VMEM_BYTES),
        cost_estimate=pl.CostEstimate(flops=16 * rows * width * width, bytes_accessed=24 * 2**20, transcendentals=0),
    )(blocks, grad_mixed, resid, gain, shift, gate, *kept, *weights, *ties)


def pack_kernel(layers, rows, block, bias, w_up, w_down, *rest):
    outs, sems = rest[:layers], rest[layers]
    start = pl.multiple_of(block[0] * rows, rows)
    sources = [w.at[layer, pl.ds(start, rows)] for layer in range(layers) for w in (w_up, w_down)]
    targets = [out.at[pl.ds(kind * rows, rows)] for out in outs for kind in range(2)]
    copies = start_copies(sources, targets, sems)
    for layer, out in enumerate(outs):
        out[2 * rows:] = bias_terms(bias[layer:layer + 1])
    for copy in copies:
        copy.wait()


def bias_terms(bias):
    top = bias.astype(BF16)
    left = bias - top.astype(F32)
    middle = left.astype(BF16)
    bottom = (left - middle.astype(F32)).astype(BF16)
    row = lax.broadcasted_iota(jnp.int32, (16, bias.shape[1]), 0)
    terms = [jnp.broadcast_to(term.astype(F32), row.shape) for term in (top, middle, bottom)]
    zero = jnp.zeros(row.shape, F32)
    chosen = jnp.where(row == 0, terms[0], jnp.where(row == 1, terms[1], jnp.where(row == 2, terms[2], zero)))
    return chosen.astype(BF16)


def pack(w_up, w_down, b_up, block):
    layers, width, shard = w_up.shape
    rows = width // 8
    out = jax.ShapeDtypeStruct((2 * rows + 16, shard), BF16)
    vmem = pl.BlockSpec(memory_space=pltpu.VMEM)
    return pl.pallas_call(
        functools.partial(pack_kernel, layers, rows),
        out_shape=[out] * layers,
        in_specs=[pl.BlockSpec(memory_space=pltpu.SMEM), vmem] + [pl.BlockSpec(memory_space=pl.ANY)] * 2,
        out_specs=[vmem] * layers,
        scratch_shapes=[pltpu.SemaphoreType.DMA((2 * layers,))],
        cost_estimate=pl.CostEstimate(flops=0, bytes_accessed=4 * layers * rows * shard * 4, transcendentals=0),
    )(block, b_up, w_up, w_down)


class Chain:
    def __init__(self, token):
        self.token, self.pending = token, []

    def need(self, *places):
        self.pending += places

    def tie(self, *values):
        count = len(values)
        out = lax.optimization_barrier((*values, self.token, *(held[key] for held, key in self.pending)))
        self.token = out[count]
        for (held, key), value in zip(self.pending, out[count + 1:]):
            held[key] = value
        self.pending = []
        return out[0] if count == 1 else out[:count]

    def ties(self):
        out, self.pending = [self.token] + [held[key] for held, key in self.pending], []
        return out


def places(values):
    return [(values, at) for at in range(len(values))]


def swap(value, axis, bit):
    size = lax.axis_size(axis)
    return lax.ppermute(value, axis, [(at, at ^ bit) for at in range(size)])


class Flow:
    def __init__(self, keep, index, bits, stages):
        self.wide, self.index, self.bits, self.stages, self.terms = [keep], list(index), bits, stages, []
        self.tile = keep.shape[-2:]

    def halve(self):
        bit, self.bits = self.bits[0], self.bits[1:]
        leaves = list(self.index)
        leaves[bit], self.index[bit] = 1, 0
        return tuple(leaves)

    def order(self, shape):
        open_dims = [dim for dim, at in enumerate(self.index) if at is None]
        ranked = list(self.bits) + [dim for dim in open_dims if dim not in self.bits]
        sizes = [shape[dim] for dim in open_dims]
        places = [()]
        for dim in ranked:
            places = [place + (at,) for place in places for at in range(shape[dim])]
        return sizes, [tuple(place[ranked.index(dim)] for dim in open_dims) for place in places]


def feed_flows(layer, grads):
    keep = grads[0].reshape((2, 2) + grads[0].shape[1:])
    dims = {"u": 0, "v": 1, "x": 4, "y": 5}
    return [Flow(keep, (None, None, at, None, None, None), tuple(dims[letter] for letter in stages), stages)
            for at, stages in enumerate(PART_STAGES[layer])]


def attend_flows(grads):
    return [Flow(grads[0], (at, None, None, None, None), bits, stages)
            for at, (bits, stages) in enumerate((((1, 2), "xy"), ((2, 1), "yx")))]


class Reads:
    def __init__(self):
        self.arrays = []

    def at(self, array):
        for at, known in enumerate(self.arrays):
            if known is array:
                return at
        self.arrays.append(array)
        return len(self.arrays) - 1

    def places(self, terms):
        return [(self.at(array), place) for array, place in terms]


def as_block(value):
    tile = value.shape[1] // 3
    parts = [value[:, at * tile:(at + 1) * tile] for at in range(3)]
    return jnp.concatenate(parts + [jnp.zeros_like(parts[0])], axis=0).astype(BF16)


def from_block(block):
    value = block.astype(F32)
    rows = value.shape[0] // 4
    return jnp.concatenate([value[at * rows:(at + 1) * rows] for at in range(3)], axis=1)


def add_small_parts(parts, blocks, out):
    out[...] = jnp.zeros_like(out)
    for layer in range(2):
        fed, attended, up = parts[3 * layer:3 * layer + 3]
        base = 10 * layer
        out[base:base + 3] = fed[0:3]
        out[base + 3:base + 6] = attended[0:3]
        for slot in range(len(SHARD_ORDER)):
            out[pl.ds(base + 6 + blocks[8 + slot], 1)] = up[slot]


def exchange_kernel(plan, blocks, *refs):
    (sizes, reads, sends, column_count, ends, small, small_terms, small_ends,
     array_count, small_count, tie_count) = plan
    arrays, refs = refs[:array_count], refs[array_count:]
    small_ins, refs = refs[:small_count], refs[small_count + tie_count:]
    outs, refs = refs[:len(sizes)], list(refs[len(sizes):])
    own = refs.pop(0) if column_count else None
    small_out = refs.pop(0) if small == "new" else None
    out_sems, sems = refs.pop(), refs.pop()
    mades = [refs.pop(0) for _ in sizes]
    copies, groups = [], []

    def fetch(source, target):
        copies.append(pltpu.make_async_copy(source, target, sems.at[len(copies)]))
        copies[-1].start()
        return copies[-1]

    for wide, _, terms, size in reads:
        held_wide = refs.pop(0)
        held = refs.pop(0) if terms else None
        waits = [fetch(arrays[array].at[index], held_wide.at[at]) for at, (array, index) in enumerate(wide)]
        waits += [fetch(arrays[array].at[pl.ds(place, size)], held.at[at]) for at, (array, place) in enumerate(terms)]
        groups.append((waits, held_wide, held))
    held_small = refs.pop(0) if small_terms else None
    small_waits = [fetch(arrays[array].at[pl.ds(place, 1)], held_small.at[at]) for at, (array, place) in enumerate(small_terms)]

    def arrive(number):
        waits, held_wide, held = groups[number]
        for copy in waits:
            copy.wait()
        wide, _, terms, _ = reads[number]
        return lambda block, place: [held_wide[(at,) + place] for at in range(len(wide))] + [
            held[at, block] for at in range(len(terms))]

    for number, (out, start, order) in enumerate(sends):
        values_of = arrive(number)
        for block, place in enumerate(order):
            values = values_of(block, place)
            while len(values) > 1:
                values = [values[at] + values[at + 1] if at + 1 < len(values) else values[at]
                          for at in range(0, len(values), 2)]
            mades[out][start + block] = values[0]
    if column_count:
        turned = refs.pop(0)
        shards = len(SHARD_ORDER)
        share = turned.shape[2] // 4
        for flow in range(column_count):
            values_of = arrive(len(sends) + flow)
            lines, tiles = reads[len(sends) + flow][1]
            for line in range(lines):
                parts = []
                for tile in range(tiles):
                    total = None
                    for value in values_of(line * tiles + tile, (line, tile)):
                        total = value.astype(F32) if total is None else total + value.astype(F32)
                    parts.append(total)
                whole = jnp.concatenate(parts, axis=1)
                to = (2 * flow + line) * share
                for shard in range(shards):
                    turned[shard ^ blocks[8], :, to:to + share] = whole[:, shard * share:(shard + 1) * share]
        own[...] = turned[0]
        tile = mades[0].shape[2]
        for other in range(1, shards):
            out, start = ends[other - 1]
            for cut in range(3):
                mades[out][start + cut] = turned[other, :, cut * tile:(cut + 1) * tile].astype(BF16)
    if small:
        if small == "new":
            add_small_parts(small_ins, blocks, small_out)
            total = small_out[...]
        else:
            total = small_ins[0][...]
            for copy in small_waits:
                copy.wait()
            for term in range(len(small_terms)):
                total = total + from_block(held_small[term, 0])
        for out, start in small_ends:
            mades[out][start] = as_block(total)
    leaving = [pltpu.make_async_copy(made, outs[at], out_sems.at[at]) for at, made in enumerate(mades)]
    for copy in leaving:
        copy.start()
    for copy in leaving:
        copy.wait()


def pause_kernel(source, out):
    out[...] = jnp.zeros_like(out)


def pause(value):
    return pl.pallas_call(
        pause_kernel,
        out_shape=jax.ShapeDtypeStruct((8, 128), F32),
        in_specs=[pl.BlockSpec(memory_space=pl.ANY)],
        out_specs=pl.BlockSpec(memory_space=pltpu.VMEM),
        compiler_params=pltpu.CompilerParams(vmem_limit_bytes=VMEM_BYTES),
    )(value)


class Rounds:
    def __init__(self, blocks):
        self.blocks, self.arrived = blocks, []

    def exchange(self, flows, ending=(), small=None, ties=(), crossing=(), alone=False):
        known, reads, sends, sizes = Reads(), [], [], {}

        def room(letter, size):
            place = sizes.get(letter, 0)
            sizes[letter] = place + size
            return list(sizes).index(letter), place

        def read(flow, index, skipped):
            shape = flow.wide[0].shape
            open_sizes, order = flow.order(shape)
            size = len(order)
            wide = [(known.at(array), tuple(slice(None) if at is None else at for at in index)) for array in flow.wide]
            reads.append((wide, open_sizes, [(known.at(array), start + skipped * size) for array, start in flow.terms], size))
            return size, order

        moved = []
        for flow in flows:
            letter, flow.stages = flow.stages[0], flow.stages[1:]
            size, order = read(flow, flow.halve(), 1)
            out, place = room(letter, size)
            sends.append((out, place, order))
            moved.append((flow.terms, letter, place))
        tile = flows[0].tile
        width = 3 * tile[1]
        for pair in ending:
            for flow in pair:
                read(flow, flow.index, 0)
        column_count = len(reads) - len(sends)
        ends = [room(letter, 3) for letter in "uvw"] if column_count else []
        mode, small_terms, small_ins, small_ends = "", [], [], []
        if small is not None:
            mode, letters = small.next()
            small_ins = small.parts if mode == "new" else [small.own]
            small_terms = [] if mode == "new" else known.places(small.terms)
            small_ends = [room(letter, 1) for letter in letters]
        order = list(sizes)
        outs = [jax.ShapeDtypeStruct((sizes[letter],) + tile, BF16) for letter in order]
        held = [pltpu.VMEM((sizes[letter],) + tile, BF16) for letter in order]
        for wide, open_sizes, terms, size in reads:
            held.append(pltpu.VMEM((len(wide), *open_sizes) + tile, BF16))
            if terms:
                held.append(pltpu.VMEM((len(terms), size) + tile, BF16))
        if small_terms:
            held.append(pltpu.VMEM((len(small_terms), 1) + tile, BF16))
        more = []
        if column_count:
            held.append(pltpu.VMEM((len(SHARD_ORDER), tile[0], width), F32))
            more.append(jax.ShapeDtypeStruct((tile[0], width), F32))
        if mode == "new":
            more.append(jax.ShapeDtypeStruct((24, width), F32))
        ties = [*self.arrived, *ties]
        copies = sum(len(wide) + len(terms) for wide, _, terms, _ in reads) + len(small_terms)
        anywhere, vmem = pl.BlockSpec(memory_space=pl.ANY), pl.BlockSpec(memory_space=pltpu.VMEM)
        plan = ([sizes[letter] for letter in order], reads, sends, column_count, ends, mode, small_terms, small_ends,
                len(known.arrays), len(small_ins), len(ties))
        made = list(pl.pallas_call(
            functools.partial(exchange_kernel, plan),
            out_shape=outs + more,
            in_specs=[pl.BlockSpec(memory_space=pltpu.SMEM)] + [anywhere] * len(known.arrays) + [vmem] * len(small_ins)
            + [anywhere] * len(ties),
            out_specs=[anywhere] * len(outs) + [vmem] * len(more),
            scratch_shapes=held + [pltpu.SemaphoreType.DMA((copies,)), pltpu.SemaphoreType.DMA((len(outs),))],
            compiler_params=pltpu.CompilerParams(vmem_limit_bytes=VMEM_BYTES),
        )(self.blocks, *known.arrays, *small_ins, *ties))
        rest = made[len(outs):]
        self.made = made[:len(outs)]
        going = lax.optimization_barrier(self.made + [send for _, send in crossing])
        arrived = {letter: swap(value, *LINKS[letter]) for letter, value in zip(order, going)}
        self.arrived = list(arrived.values())
        self.going = going[0]
        if alone:
            self.arrived.append(pause(going[0]))
        for (crossed, _), send in zip(crossing, going[len(outs):]):
            self.cross(crossed, send)
        for terms, letter, place in moved:
            terms.append((arrived[letter], place))
        for pair in ending:
            pair[0].own = rest.pop(0)
            pair[0].far = [(arrived[letter], place) for letter, (_, place) in zip("uvw", ends)]
        if mode:
            if mode == "new":
                small.own = rest.pop(0)
            small.terms += [(arrived[letter], place) for letter, (_, place) in zip(letters, small_ends)]

    def cross(self, flows, send):
        arrived = swap(send, *LINKS["c"])
        self.arrived.append(arrived)
        for flow in flows:
            flow.wide.append(arrived.reshape(flow.wide[0].shape))


class Small:
    def __init__(self, parts):
        self.parts, self.terms, self.stages = parts, [], ["c", "x", "uvw", "y"]

    def next(self):
        letters = self.stages.pop(0)
        return ("new" if letters == "c" else "old"), letters


def finish_kernel(plan, layer, counts, blocks, *refs):
    wides, feeds, far, small = plan
    array_count, other_count = counts
    arrays, own, refs = refs[:array_count], refs[array_count], refs[array_count + 1:]
    if small:
        small_own, refs = refs[0], refs[1:]
    refs = refs[other_count:]
    outs, refs = refs[:6], refs[6:]
    if small:
        smalls, gate, hidden, refs = refs[:5], refs[5], refs[6], refs[7:]
    up, down, attends, held_wide, held, held_far, held_small, sems, out_sems = refs
    copies = []

    def fetch(source, target):
        copies.append(pltpu.make_async_copy(source, target, sems.at[len(copies)]))
        copies[-1].start()

    for term, array in wides:
        fetch(arrays[array].at[0, 0, :, :, 0, 0], held_wide.at[term])
    for part, term, array, place in feeds:
        fetch(arrays[array].at[pl.ds(place, 2)], held.at[part, term])
    for other, array, place in far:
        fetch(arrays[array].at[pl.ds(place, 3)], held_far.at[other])
    for term, (array, place) in enumerate(small):
        fetch(arrays[array].at[pl.ds(place, 1)], held_small.at[term])
    for copy in copies:
        copy.wait()
    leaving = Leaving(out_sems)
    terms, tile = held.shape[1], held.shape[4]
    for part in range(3):
        total = held_wide[0, part].astype(F32) + held_wide[1, part].astype(F32)
        for term in range(terms):
            total = total + held[part, term].astype(F32)
        up[:, part * tile:(part + 1) * tile] = total[0]
        down[:, part * tile:(part + 1) * tile] = total[1]
    leaving.send(up, outs[0].at[layer])
    leaving.send(down, outs[1].at[layer])
    total = own[...]
    for other in range(3):
        total = total + jnp.concatenate([held_far[other, cut].astype(F32) for cut in range(3)], axis=1)
    share = total.shape[1] // 4
    for at in range(4):
        attends[at] = total[:, at * share:(at + 1) * share]
        leaving.send(attends.at[at], outs[2 + at].at[layer])
    if small:
        total = small_own[...]
        for term in range(len(small)):
            total = total + from_block(held_small[term, 0])
        lines = total.shape[1] // 8
        mine = jnp.where(blocks[0] == 0, total[:, :lines], 0.0)
        for place in range(1, 8):
            mine = mine + jnp.where(blocks[0] == place, total[:, place * lines:(place + 1) * lines], 0.0)
        for at in range(2):
            base = 10 * at
            for row, out in zip((3, 4, 1, 2, 0), smalls):
                out[at:at + 1] = mine[base + row:base + row + 1]
            shard = jnp.zeros((1, total.shape[1]), F32)
            for index in range(4):
                shard = shard + jnp.where(blocks[8] == index, total[base + 6 + index:base + 7 + index], 0.0)
            hidden[at:at + 1] = shard
        gate[...] = mine[5:6]
    leaving.wait()


def finish(layer, feeds, attends, blocks, before, small=None):
    reads = Reads()
    wide_plan = [(term, reads.at(array)) for term, array in enumerate(feeds[0].wide)]
    feed_plan = [(part, term, reads.at(array), place) for part, flow in enumerate(feeds)
                 for term, (array, place) in enumerate(flow.terms)]
    far_plan = [(other, reads.at(array), place) for other, (array, place) in enumerate(attends[0].far)]
    small_plan = reads.places(small.terms) if small else []
    rows, tile = feeds[0].tile
    width, terms = 3 * tile, len(feeds[0].terms)
    anywhere, vmem = pl.BlockSpec(memory_space=pl.ANY), pl.BlockSpec(memory_space=pltpu.VMEM)
    outs = [jax.ShapeDtypeStruct((2, rows, width), F32)] * 2 + [jax.ShapeDtypeStruct((2, rows, width // 4), F32)] * 4
    more = [jax.ShapeDtypeStruct((2, rows), F32)] * 5 + [
        jax.ShapeDtypeStruct((1, rows), F32), jax.ShapeDtypeStruct((2, width), F32)] if small else []
    given = 2 + len(reads.arrays) + (1 if small else 0)
    return pl.pallas_call(
        functools.partial(finish_kernel, (wide_plan, feed_plan, far_plan, small_plan), layer, (len(reads.arrays), len(before))),
        out_shape=outs + more,
        in_specs=[pl.BlockSpec(memory_space=pltpu.SMEM)] + [anywhere] * len(reads.arrays) + [vmem] * (given - 1 - len(reads.arrays))
        + [anywhere] * len(before),
        out_specs=[anywhere] * 6 + [vmem] * len(more),
        scratch_shapes=[pltpu.VMEM((rows, width), F32), pltpu.VMEM((rows, width), F32), pltpu.VMEM((4, rows, width // 4), F32),
                        pltpu.VMEM((2, 3, 2, rows, tile), BF16), pltpu.VMEM((3, terms, 2, rows, tile), BF16),
                        pltpu.VMEM((3, 3, rows, tile), BF16), pltpu.VMEM((max(len(small_plan), 1), 1, rows, tile), BF16),
                        pltpu.SemaphoreType.DMA((len(wide_plan) + len(feed_plan) + len(far_plan) + len(small_plan),)),
                        pltpu.SemaphoreType.DMA((6,))],
        input_output_aliases={given + at: at for at in range(6)} if small else {},
        compiler_params=pltpu.CompilerParams(vmem_limit_bytes=VMEM_BYTES),
    )(blocks, *reads.arrays, attends[0].own, *([small.own] if small else []), *before)


def eighths(weights):
    return weights.reshape(weights.shape[:-2] + (2, 2, 2, weights.shape[-2] // 8, weights.shape[-1]))


def in_order(bit, own, other):
    first = (lax.axis_index("dp") & bit) == 0
    return jnp.stack([jnp.where(first, own, other), jnp.where(first, other, own)])


def far_pieces(layer, w_up, w_down, tails, halves, crossed, blocks):
    arrays = [eighths(w_up), eighths(w_down)] + halves + crossed
    every, rest = slice(None), pl.ds(1, len(tails) - 1)
    plan = [(kind, layer, kind, lambda me: (every, every, every, 0)) for kind in range(2)]
    for core in range(2):
        for second in range(2):
            plan.append((2 + 4 * core + second, None, 0, lambda me, core=core, second=second: (
                ((me >> 2) & 1) ^ second, every, (me & 1) ^ core, rest)))
            plan.append((4 + 4 * core + second, None, 1, lambda me, core=core, second=second: (
                every, ((me >> 1) & 1) ^ second, (me & 1) ^ core, rest)))
    return Pieces(arrays, plan, blocks, tails)


def gathered_pieces(layer, w_up, w_down, b_up, blocks):
    arrays = [eighths(lax.all_gather(weights[layer], "mp")) for weights in (w_up, w_down)]
    shards = arrays[0].shape[0]
    plan = [(kind, at, kind, lambda me, at=at: (slice(None),) * 3 + (at,)) for at in range(shards) for kind in range(2)]
    bias = lax.all_gather(b_up[layer:layer + 1], "mp")
    return Pieces(arrays, plan, blocks, [bias_terms(bias[at]) for at in range(shards)])


def sum_feed_anywhere(grads):
    both = lax.psum_scatter(grads, "mp", scatter_dimension=0, tiled=True)[0]
    both = lax.psum_scatter(both.astype(F32), "dp", scatter_dimension=1, tiled=True)
    return both[0], both[1].T


def sum_attend_anywhere(grads):
    whole = lax.psum_scatter(grads, "mp", scatter_dimension=2, tiled=True)
    return lax.psum_scatter(whole.astype(F32), "dp", scatter_dimension=1, tiled=True)


def shards(inputs, slot_valid, ln1_gain, ln1_bias, w_query, w_key, w_value, w_out, gate_logit,
           ln2_gain, ln2_bias, w_up, b_up, w_down, b_down, cotangent):
    pages, slots, width = inputs.shape
    dp, mp = lax.axis_size("dp"), lax.axis_size("mp")
    paired = dp == 8 and mp == 4 and width % (16 * dp) == 0
    if paired:
        place = jnp.arange(12, dtype=jnp.int32)
        slot = place & 3
        blocks = jnp.where(place < 8, lax.axis_index("dp") ^ place, lax.axis_index("mp") ^ ((slot & 1) * 2 + slot // 2))
    else:
        blocks = jnp.arange(2, dtype=jnp.int32)

    own_valid = lax.dynamic_slice_in_dim(slot_valid, lax.axis_index("mp") * pages, pages, 0) == 1
    key_text = lax.broadcasted_iota(jnp.int32, (slots, slots), 0) < TEXT
    query_text = lax.broadcasted_iota(jnp.int32, (slots, slots), 1) < TEXT
    live = jnp.broadcast_to(own_valid[:, :, None], (pages, slots, slots))
    masks = [
        jnp.where(jnp.logical_and(live, (key_text != query_text)[None]), 0.0, -1e30).astype(F32),
        jnp.where(live, 0.0, -1e30).astype(F32),
    ]
    gate = gate_logit[None]
    weights = (w_query, w_key, w_value, w_out)
    first_rows = inputs.reshape(pages * slots, width)
    cotangent = cotangent.reshape(pages * slots, width)
    got = {"grad": None}

    def attend_layer(layer, rows, ties):
        return attend(layer, layer == 0, rows, masks[layer], ln1_gain, ln1_bias, gate, weights, ties)

    def feed_layer(layer, rows, pieces, ties):
        return feed(layer, rows, ln2_gain, ln2_bias, b_down, pieces, (F32, BF16)[layer], ties)

    def feed_back_layer(layer, ties):
        rows, active, slope, pieces = got["feed", layer]
        got["mixed_grad"], got["feed_sums", layer], got["up_sums", layer], *got["feed_grads", layer] = feed_back(
            layer, (got["grad"], cotangent)[layer], rows, ln2_gain, ln2_bias, active, slope, pieces, not paired, ties)

    def attend_back_layer(layer, ties):
        rows, kept = got["attend", layer]
        got["grad"], got["attend_sums", layer], *got["attend_grads", layer] = attend_back(
            layer, layer == 0, got["mixed_grad"], rows, ln1_gain, ln1_bias, gate, (*kept[:5], *kept[6:]), weights,
            blocks, not paired, ties)

    if paired:
        owns = pack(w_up, w_down, b_up, blocks)
        rows = width // 8
        chain = Chain(owns[0])
        far = lambda own: [swap(own, "mp", other) for other in SHARD_ORDER[1:]]
        split = lambda pieces: (jnp.stack([piece[:rows] for piece in pieces]),
                                jnp.stack([piece[rows:2 * rows] for piece in pieces]))
        other_core = lambda *values: [swap(value, "dp", 1) for value in values]

        far_0 = far(owns[0])
        kept_0 = list(attend_layer(0, first_rows, ()))
        chain.need((kept_0, 5))
        far_0 = list(chain.tie(*far_0))
        ups, downs = chain.tie(*split(far_0))
        near_0 = [swap(ups, "dp", 2), swap(downs, "dp", 4)]
        far_1 = far(chain.tie(owns[1]))
        near_0 = chain.tie(*near_0)
        ups_0, downs_0 = chain.tie(in_order(2, ups, near_0[0]), in_order(4, downs, near_0[1]))
        side_0 = [swap(ups_0, "dp", 4), swap(downs_0, "dp", 2)]
        ups_0, downs_0, *side_0 = chain.tie(ups_0, downs_0, *side_0)
        far_1 = list(chain.tie(*far_1))
        ups, downs = chain.tie(*split(far_1))
        near_1 = [swap(ups, "dp", 2), swap(downs, "dp", 4)]
        core_0 = other_core(ups_0, side_0[0], downs_0, side_0[1])
        pieces_0 = far_pieces(0, w_up, w_down, [owns[0]] + far_0, [ups_0, side_0[0], downs_0, side_0[1]], core_0, blocks)
        fed_0 = list(feed_layer(0, kept_0[5], pieces_0, chain.ties()))
        chain.need((fed_0, 0))
        near_1 = chain.tie(*near_1)
        result_0, active_0, slope_0 = fed_0
        ups_1, downs_1 = chain.tie(in_order(2, ups, near_1[0]), in_order(4, downs, near_1[1]))
        side_1 = [swap(ups_1, "dp", 4), swap(downs_1, "dp", 2)]
        kept_1 = list(attend_layer(1, result_0, chain.ties()))
        chain.need((kept_1, 5))
        side_1 = chain.tie(*side_1)
        core_1 = other_core(ups_1, side_1[0], downs_1, side_1[1])
        pieces_1 = far_pieces(1, w_up, w_down, [owns[1]] + far_1, [ups_1, side_1[0], downs_1, side_1[1]], core_1, blocks)
    else:
        pieces_0 = gathered_pieces(0, w_up, w_down, b_up, blocks)
        pieces_1 = gathered_pieces(1, w_up, w_down, b_up, blocks)
        kept_0 = attend_layer(0, first_rows, ())
        result_0, active_0, slope_0 = feed_layer(0, kept_0[5], pieces_0, ())
        kept_1 = attend_layer(1, result_0, ())

    result_1, active_1, slope_1 = feed_layer(1, kept_1[5], pieces_1, ())
    got["feed", 0] = kept_0[5], active_0, slope_0, pieces_0
    got["feed", 1] = kept_1[5], active_1, slope_1, pieces_1
    got["attend", 0], got["attend", 1] = (first_rows, kept_0), (result_0, kept_1)

    if paired:
        rounds = Rounds(blocks)
        feed_back_layer(1, ())
        feeds, attends = {1: feed_flows(1, got["feed_grads", 1])}, {}
        rounds.cross(feeds[1], got["feed_grads", 1][1])
        attend_back_layer(1, ())
        attends[1] = attend_flows(got["attend_grads", 1])
        rounds.exchange(feeds[1], ties=[got["attend_sums", 1]], crossing=[(attends[1], got["attend_grads", 1][1])])
        feed_back_layer(0, rounds.made)
        feeds[0] = feed_flows(0, got["feed_grads", 0])
        rounds.exchange(feeds[1] + attends[1], ties=[got["feed_sums", 0]], crossing=[(feeds[0], got["feed_grads", 0][1])])
        attend_back_layer(0, rounds.made)
        attends[0] = attend_flows(got["attend_grads", 0])
        small = Small([got[name, layer] for layer in (0, 1) for name in ("feed_sums", "attend_sums", "up_sums")])
        rounds.exchange(feeds[0] + feeds[1] + attends[1], small=small, crossing=[(attends[0], got["attend_grads", 0][1])], alone=True)
        rounds.exchange(feeds[0] + attends[0] + feeds[1], [attends[1]], small, alone=True)
        rounds.exchange(feeds[0] + attends[0], small=small, alone=True)
        rounds.exchange(feeds[0], [attends[0]], small)
        made = finish(1, feeds[1], attends[1], blocks, [rounds.going])
        up_grad, down_turned, *rest = finish(0, feeds[0], attends[0], blocks, made, small)
        down_grad = jnp.swapaxes(down_turned, 1, 2)
        attend_grads, small_grads, gate_grad, bup_grad = rest[:4], rest[4:9], rest[9][0], rest[10]
    else:
        for layer in (1, 0):
            feed_back_layer(layer, ())
            attend_back_layer(layer, ())
        feed_grads = [sum_feed_anywhere(got["feed_grads", layer][0]) for layer in (0, 1)]
        up_grad, down_grad = (jnp.stack([feed_grads[layer][at] for layer in (0, 1)]) for at in range(2))
        sums = [sum_attend_anywhere(got["attend_grads", layer][0]) for layer in (0, 1)]
        attend_grads = [jnp.stack([sums[0][at], sums[1][at]]) for at in range(4)]
        both = lax.psum(jnp.concatenate([part for layer in (0, 1) for part in (
            got["feed_sums", layer][:3], got["attend_sums", layer][:3], got["up_sums", layer][:, 0])]), ("dp", "mp"))
        later, lines, me = both.shape[0] // 2, width // dp, lax.axis_index("mp")
        mine = lax.dynamic_slice_in_dim(both, lax.axis_index("dp") * lines, lines, 1)
        small_grads = [jnp.stack([mine[row], mine[later + row]]) for row in (3, 4, 1, 2, 0)]
        gate_grad = mine[5]
        bup_grad = jnp.concatenate([lax.dynamic_slice_in_dim(both, row + me, 1, 0) for row in (6, later + 6)])

    return (
        result_1.reshape(pages, slots, width),
        got["grad"].reshape(pages, slots, width),
        small_grads[0],
        small_grads[1],
        *attend_grads,
        gate_grad,
        small_grads[2],
        small_grads[3],
        up_grad,
        bup_grad,
        down_grad,
        small_grads[4],
    )


def solution(mesh):
    rows = P(("dp", "mp"), None, None)
    return jax.shard_map(
        shards,
        mesh=mesh,
        in_specs=(rows, P("dp", None), P(), P(), P(), P(), P(), P(), P(), P(), P(), P(None, None, "mp"),
                  P(None, "mp"), P(None, "mp", None), P(), rows),
        out_specs=(rows, rows, P(None, "dp"), P(None, "dp"), P(None, "dp", "mp"), P(None, "dp", "mp"),
                   P(None, "dp", "mp"), P(None, "dp", "mp"), P("dp"), P(None, "dp"), P(None, "dp"),
                   P(None, "dp", "mp"), P(None, "mp"), P(None, "mp", "dp"), P(None, "dp")),
        check_vma=False,
    )
```

```python
import functools

import jax
import jax.numpy as jnp
from jax import lax
from jax.experimental import pallas as pl
from jax.experimental.pallas import tpu as pltpu
from jax.sharding import PartitionSpec as P

HEADS = 12
TEXT = 112
F32 = jnp.float32
BF16 = jnp.bfloat16
VMEM_BYTES = 62 * 2**20


def dot(a, b, a_dim, b_dim):
    return lax.dot_general(a, b, (((a_dim,), (b_dim,)), ((), ())), preferred_element_type=F32)


def whiten(rows):
    centered = rows - jnp.mean(rows, axis=-1, keepdims=True)
    spread = jnp.mean(centered * centered, axis=-1, keepdims=True)
    inverse = lax.rsqrt(spread + 1e-05)
    return centered * inverse, inverse


def whiten_back(white, inverse, gain, grad):
    scaled = grad * gain
    first = jnp.mean(scaled, axis=-1, keepdims=True)
    second = jnp.mean(scaled * white, axis=-1, keepdims=True)
    return inverse * (scaled - first - white * second)


def column_sum(rows):
    return jnp.sum(rows, axis=0, keepdims=True)


def gelu_and_slope(values):
    size = jnp.abs(values)
    t = 1.0 / (1.0 + (0.3275911 * 0.7071067811865476) * size)
    bell = jnp.exp(-0.5 * values * values)
    poly = 0.5 * 1.061405429
    poly = poly * t + 0.5 * -1.453152027
    poly = poly * t + 0.5 * 1.421413741
    poly = poly * t + 0.5 * -0.284496736
    poly = poly * t + 0.5 * 0.254829592
    tail = poly * t * bell
    phi = jnp.where(values >= 0.0, 1.0 - tail, tail)
    return values * phi, phi + values * bell * 0.3989422804014327


def split_heads(pair):
    lane = lax.broadcasted_iota(jnp.int32, pair.shape, 1)
    first = lane < pair.shape[1] // 2
    zero = jnp.zeros_like(pair)
    return jnp.concatenate([jnp.where(first, pair, zero), jnp.where(first, zero, pair)], axis=0)


def join_heads(both):
    slots = both.shape[0] // 2
    lane = lax.broadcasted_iota(jnp.int32, (slots, both.shape[1]), 1)
    return jnp.where(lane < both.shape[1] // 2, both[:slots], both[slots:])


def start_copies(sources, targets, sems):
    copies = [
        pltpu.make_async_copy(source, target, sems.at[at])
        for at, (source, target) in enumerate(zip(sources, targets))
    ]
    for copy in copies:
        copy.start()
    return copies


class Arriving:
    def __init__(self, source, held, sem):
        self.copy, self.held, self.here = pltpu.make_async_copy(source, held, sem), held, False
        self.copy.start()

    def __getitem__(self, at):
        if not self.here:
            self.copy.wait()
            self.here = True
        return self.held[at]


class Leaving:
    def __init__(self, sems):
        self.sems, self.copies = sems, []

    def send(self, held, target):
        self.copies.append(pltpu.make_async_copy(held, target, self.sems.at[len(self.copies)]))
        self.copies[-1].start()

    def wait(self):
        for copy in self.copies:
            copy.wait()


def attend_kernel(layer, crossed, resid, mask, gain, shift, gate, wq, wk, wv, wo,
                  outs, made, held, sems, out_sems):
    q_out, k_out, v_out, p_out, c_out, mixed, *branch_out = made
    leaving = Leaving(out_sems)
    pages, slots = mask.shape[0], mask.shape[1]
    width = resid.shape[1]
    pairs = HEADS // 2
    pair_width = width // pairs
    scale = 1.0 / (width // HEADS) ** 0.5
    copies = start_copies(
        [w.at[layer] for w in (wq, wk, wv, wo)], [held.at[at] for at in range(4)], sems
    )
    white, _ = whiten(resid[...].astype(F32))
    normed = (white * gain[layer:layer + 1] + shift[layer:layer + 1]).astype(BF16)
    copies[0].wait()
    q_out[...] = (dot(normed, held[0], 1, 0).astype(BF16).astype(F32) * scale).astype(BF16)
    leaving.send(q_out, outs[0])
    copies[1].wait()
    k_out[...] = dot(normed, held[1], 1, 0).astype(BF16)
    leaving.send(k_out, outs[1])
    copies[2].wait()
    v_out[...] = dot(normed, held[2], 1, 0).astype(BF16)
    leaving.send(v_out, outs[2])

    for page in range(pages):
        rows = slice(page * slots, (page + 1) * slots)
        bias = mask[page]
        for pair in range(pairs):
            cols = slice(pair * pair_width, (pair + 1) * pair_width)
            scores = dot(split_heads(k_out[rows, cols]), q_out[rows, cols], 1, 1)
            scores = scores.reshape(2, slots, slots) + bias[None]
            top = jnp.max(scores, axis=1, keepdims=True)
            raised = jnp.exp(scores - top)
            probs = raised * (1.0 / jnp.sum(raised, axis=1, keepdims=True))
            probs = probs.reshape(2 * slots, slots).astype(BF16)
            p_out[page, pair] = probs
            c_out[rows, cols] = dot(probs, split_heads(v_out[rows, cols]), 0, 0).astype(BF16)
        leaving.send(p_out.at[page], outs[3].at[page])
    leaving.send(c_out, outs[4])
    copies[3].wait()
    for page in range(pages):
        rows = slice(page * slots, (page + 1) * slots)
        branch = dot(c_out[rows], held[3], 1, 0)
        if crossed:
            branch_out[0][rows] = branch.astype(BF16)
            branch = branch * jax.nn.sigmoid(gate[...])
            leaving.send(branch_out[0].at[rows], outs[6].at[rows])
        mixed[rows] = resid[rows].astype(F32) + branch
        leaving.send(mixed.at[rows], outs[5].at[rows])
    leaving.wait()


def attend(layer, crossed, resid, mask, gain, shift, gate, weights, ties):
    rows, width = resid.shape
    pages, slots = mask.shape[:2]
    low = jax.ShapeDtypeStruct((rows, width), BF16)
    vmem = pl.BlockSpec(memory_space=pltpu.VMEM)
    outs = [low, low, low, jax.ShapeDtypeStruct((pages, HEADS // 2, 2 * slots, slots), BF16), low,
            jax.ShapeDtypeStruct((rows, width), F32)]
    if crossed:
        outs.append(low)

    def body(*refs):
        ins, rest = refs[:9], refs[9 + len(ties):]
        attend_kernel(layer, crossed, *ins, rest[:len(outs)], rest[len(outs):2 * len(outs)], *rest[2 * len(outs):])

    return pl.pallas_call(
        body,
        out_shape=outs,
        in_specs=[vmem] * 5 + [pl.BlockSpec(memory_space=pl.ANY)] * (4 + len(ties)),
        out_specs=[pl.BlockSpec(memory_space=pl.ANY)] * len(outs),
        scratch_shapes=[pltpu.VMEM(out.shape, out.dtype) for out in outs]
        + [pltpu.VMEM((4, width, width), BF16), pltpu.SemaphoreType.DMA((4,)),
           pltpu.SemaphoreType.DMA((4 + (2 + crossed) * pages,))],
        compiler_params=pltpu.CompilerParams(vmem_limit_bytes=VMEM_BYTES),
        cost_estimate=pl.CostEstimate(flops=8 * rows * width * width, bytes_accessed=14 * 2**20, transcendentals=0),
    )(resid, mask, gain, shift, gate, *weights, *ties)


class Pieces:
    def __init__(self, arrays, plan, blocks, tails):
        self.arrays, self.plan, self.blocks, self.tails = arrays, plan, blocks, tails

    def copies(self, refs, held, blocks, sems, first=0, last=None):
        return [
            pltpu.make_async_copy(refs[array] if index is None else refs[array].at[index],
                                  held[kind].at[target(blocks[0])], sems.at[at])
            for at, (array, index, kind, target) in list(enumerate(self.plan))[first:last]
        ]

    def held(self, width):
        shape = (2, 2, 2, len(self.tails), width // 8, width)
        return [pltpu.VMEM(shape, BF16), pltpu.VMEM(shape, BF16)]

    def tail_specs(self, width):
        return [pl.BlockSpec((16, width), lambda step, last=tail.shape[0] // 16 - 1: (last, 0)) for tail in self.tails]

    def start_and_wait(self, refs, held, blocks, sems):
        step = pl.program_id(0)

        @pl.when(step == 0)
        def _():
            for copy in self.copies(refs, held, blocks, sems):
                copy.start()

        def wait():
            @pl.when(step == 0)
            def _():
                for copy in self.copies(refs, held, blocks, sems, 0, 2):
                    copy.wait()

            @pl.when(step == 1)
            def _():
                for copy in self.copies(refs, held, blocks, sems, 2):
                    copy.wait()
        return wait


def feed_kernel(layer, pieces, ties, blocks, mixed, gain, shift, b_down, *rest):
    count = len(pieces.arrays)
    tails, rest = rest[:len(pieces.tails)], rest[len(pieces.tails):]
    refs, rest = rest[:count], rest[count + ties:]
    result, active_out, slope_out, up, down, low, total, bias, sems = rest
    shards, width = up.shape[3], up.shape[5]
    step = pl.program_id(0)
    wait = pieces.start_and_wait(refs, (up, down), blocks, sems)

    @pl.when(step == 0)
    def _():
        white, _ = whiten(mixed[...])
        low[...] = (white * gain[layer:layer + 1] + shift[layer:layer + 1]).astype(BF16)
        total[...] = mixed[...] + b_down[layer:layer + 1]
        for at, tail in enumerate(tails):
            bias[at] = column_sum(tail[...].astype(F32))

    wait()
    parts = 3
    part = width // parts
    for at in range(parts):
        cols = slice(at * part, (at + 1) * part)
        upper = dot(low[...], up[:, :, :, step, :, cols].reshape(width, part), 1, 0) + bias[step, :, cols]
        active, slope = gelu_and_slope(upper)
        active = active.astype(BF16)
        active_out[0, :, cols] = active
        slope_out[0, :, cols] = slope.astype(BF16)
        total[...] += dot(active, down[:, :, :, step].reshape(width, width)[cols], 1, 0)

    @pl.when(step == shards - 1)
    def _():
        result[...] = total[...].astype(result.dtype)


def feed(layer, mixed, gain, shift, b_down, pieces, out_type, ties):
    rows, width = mixed.shape
    shards = len(pieces.tails)
    whole = lambda shape: pl.BlockSpec(shape, lambda step: (0,) * len(shape))
    each = lambda shape: pl.BlockSpec((1,) + shape, lambda step: (step,) + (0,) * len(shape))
    return pl.pallas_call(
        functools.partial(feed_kernel, layer, pieces, len(ties)),
        grid=(shards,),
        out_shape=[jax.ShapeDtypeStruct((rows, width), out_type)]
        + [jax.ShapeDtypeStruct((shards, rows, width), BF16)] * 2,
        in_specs=[pl.BlockSpec(memory_space=pltpu.SMEM), whole((rows, width)), whole(gain.shape), whole(shift.shape),
                  whole(b_down.shape)] + pieces.tail_specs(width)
        + [pl.BlockSpec(memory_space=pl.ANY)] * (len(pieces.arrays) + len(ties)),
        out_specs=[whole((rows, width)), each((rows, width)), each((rows, width))],
        scratch_shapes=[*pieces.held(width),
                        pltpu.VMEM((rows, width), BF16), pltpu.VMEM((rows, width), F32),
                        pltpu.VMEM((shards, 1, width), F32), pltpu.SemaphoreType.DMA((len(pieces.plan),))],
        compiler_params=pltpu.CompilerParams(vmem_limit_bytes=VMEM_BYTES),
        cost_estimate=pl.CostEstimate(flops=16 * rows * width * width, bytes_accessed=20 * 2**20, transcendentals=0),
    )(pieces.blocks, mixed, gain, shift, b_down, *pieces.tails, *pieces.arrays, *ties)


ROWS_ORDER = (0, 4, 2, 6, 1, 5, 3, 7)
PART_STAGES = (("xyvu", "yuxv", "uxyv"), ("xyvu", "yuxv", "uxyv"))
SHARD_ORDER = (0, 2, 1, 3)
LINKS = {"c": ("dp", 1), "x": ("dp", 2), "y": ("dp", 4), "u": ("mp", 1), "v": ("mp", 2), "w": ("mp", 3)}


def turn_rows(held, turned, blocks, order):
    if order is None:
        turned[...] = held[...]
        return
    size = held.shape[0] // len(order)
    for at, place in enumerate(order):
        start = pl.multiple_of(blocks[place] * size, size)
        turned[at * size:(at + 1) * size] = held[pl.ds(start, size)]


def put_blocks(made, keep, send, place):
    rows = made.shape[0] // 8
    for half, out in enumerate((keep, send)):
        for first in range(2):
            for second in range(2):
                at = (4 * half + 2 * first + second) * rows
                out[place(first, second)] = made[at:at + rows]


def feed_back_kernel(layer, pieces, joint, ties, blocks, grad_out, mixed, gain, shift, active, slope, *rest):
    count = len(pieces.arrays)
    refs, rest = rest[:count], rest[count + ties:]
    grads_count = 1 if joint else 2
    grad_mixed, sums, up_sums, *grads = rest[:3 + grads_count]
    up, down, low, low_turned, normed_turned, held, total, sems = rest[3 + grads_count:]
    shards, width = up.shape[3], up.shape[5]
    part = width // 3
    step = pl.program_id(0)
    wait = pieces.start_and_wait(refs, (up, down), blocks, sems)

    def put(kind, turned, right):
        made = dot(turned[...], right, 1, 0).astype(BF16)
        if joint:
            grads[0][0, kind] = made
            return
        for at in range(3):
            put_blocks(made[:, at * part:(at + 1) * part], *grads, lambda first, second: (0, at, kind, first, second))

    @pl.when(step == 0)
    def _():
        rows = grad_out[...].astype(F32)
        low[...] = rows.astype(BF16)
        sums[...] = jnp.zeros_like(sums)
        sums[0:1] = column_sum(rows)
        white, _ = whiten(mixed[...])
        normed = (white * gain[layer:layer + 1] + shift[layer:layer + 1]).astype(BF16)
        for value, turned in ((low[...], low_turned), (normed, normed_turned)):
            held[...] = value.T
            turn_rows(held, turned, blocks, None if joint else ROWS_ORDER)
        total[...] = jnp.zeros_like(total)

    wait()
    put(1, low_turned, active[0])
    upper = dot(low[...], down[:, :, :, step].reshape(width, width), 1, 1) * slope[0].astype(F32)
    up_sums[0] = column_sum(upper)
    upper_low = upper.astype(BF16)
    put(0, normed_turned, upper_low)
    total[...] += dot(upper_low, up[:, :, :, step].reshape(width, width), 1, 1)

    @pl.when(step == shards - 1)
    def _():
        white, inverse = whiten(mixed[...])
        grad = total[...]
        sums[1:2] = column_sum(grad * white)
        sums[2:3] = column_sum(grad)
        grad_mixed[...] = grad_out[...].astype(F32) + whiten_back(white, inverse, gain[layer:layer + 1], grad)


def feed_back(layer, grad_out, mixed, gain, shift, active, slope, pieces, joint, ties):
    rows, width = mixed.shape
    shards = active.shape[0]
    whole = lambda shape: pl.BlockSpec(shape, lambda step: (0,) * len(shape))
    each = lambda shape: pl.BlockSpec((1,) + shape, lambda step: (step,) + (0,) * len(shape))
    if joint:
        grads = [(2, width, width)]
    else:
        grads = [(3, 2, 2, 2, width // 8, width // 3)] * 2
    turned = pltpu.VMEM((width, rows), BF16)
    return pl.pallas_call(
        functools.partial(feed_back_kernel, layer, pieces, joint, len(ties)),
        grid=(shards,),
        out_shape=[jax.ShapeDtypeStruct((rows, width), F32), jax.ShapeDtypeStruct((8, width), F32),
                   jax.ShapeDtypeStruct((shards, 1, width), F32)]
        + [jax.ShapeDtypeStruct((shards,) + shape, BF16) for shape in grads],
        in_specs=[pl.BlockSpec(memory_space=pltpu.SMEM), whole((rows, width)), whole((rows, width)), whole(gain.shape),
                  whole(shift.shape), each((rows, width)), each((rows, width))]
        + [pl.BlockSpec(memory_space=pl.ANY)] * (len(pieces.arrays) + len(ties)),
        out_specs=[whole((rows, width)), whole((8, width)), each((1, width))] + [each(shape) for shape in grads],
        scratch_shapes=[*pieces.held(width),
                        pltpu.VMEM((rows, width), BF16), turned, turned, pltpu.VMEM((width, rows), BF16),
                        pltpu.VMEM((rows, width), F32), pltpu.SemaphoreType.DMA((len(pieces.plan),))],
        compiler_params=pltpu.CompilerParams(vmem_limit_bytes=VMEM_BYTES),
        cost_estimate=pl.CostEstimate(flops=32 * rows * width * width, bytes_accessed=30 * 2**20, transcendentals=0),
    )(pieces.blocks, grad_out, mixed, gain, shift, active, slope, *pieces.arrays, *ties)


def attend_back_kernel(layer, crossed, joint, blocks, grad_mixed, resid, gain, shift, gate, q, k, v, p, context, branch,
                       wq, wk, wv, wo, resid_out, sums, outs, grad_resid, grads, landing,
                       held, turning, turned, gc, gq, gk, gv, sems, out_sems):
    pages, slots = p.shape[0], p.shape[3]
    width = resid.shape[1]
    pairs = HEADS // 2
    pair_width = width // pairs
    scale = 1.0 / (width // HEADS) ** 0.5
    number = iter(range(16))
    arrive = lambda source, target: Arriving(source, target, sems.at[next(number)])
    land = iter(landing)
    context, grad_mixed = arrive(context, next(land)), arrive(grad_mixed, next(land))
    if crossed:
        branch = arrive(branch, next(land))
    w_out = arrive(wo.at[layer], held.at[0])
    v, p, k, q = (arrive(value, next(land)) for value in (v, p, k, q))
    resid = arrive(resid, next(land))
    w_query, w_key, w_value = (arrive(w.at[layer], held.at[at + 1]) for at, w in enumerate((wq, wk, wv)))
    leaving = Leaving(out_sems)
    sums[...] = jnp.zeros_like(sums)

    def put(at, right):
        made = dot(turned[...], right, 1, 0).astype(BF16)
        if joint:
            grads[0][at] = made
            return
        tile = width // 3
        for col in range(3):
            put_blocks(made[:, col * tile:(col + 1) * tile], *grads,
                       lambda first, second: (at // 2, first, second, at % 2, col))

    def turn(rows):
        turning[...] = rows.T
        turn_rows(turning, turned, blocks, None if joint else ROWS_ORDER)

    grad = grad_mixed[...]
    if crossed:
        opened = jax.nn.sigmoid(gate[...])
        sums[2:3] = column_sum(grad * branch[...].astype(F32)) * (opened * (1.0 - opened))
        low = (grad * opened).astype(BF16)
    else:
        low = grad.astype(BF16)
    turn(context[...])
    put(3, low)
    gc[...] = dot(low, w_out[...], 1, 1).astype(BF16)

    for page in range(pages):
        rows = slice(page * slots, (page + 1) * slots)
        for pair in range(pairs):
            cols = slice(pair * pair_width, (pair + 1) * pair_width)
            probs_low = p[page, pair]
            probs = probs_low.astype(F32).reshape(2, slots, slots)
            grad_probs = dot(split_heads(v[rows, cols]), gc[rows, cols], 1, 1).reshape(2, slots, slots)
            delta = jnp.sum(probs * grad_probs, axis=1, keepdims=True)
            grad_scores = (probs * (grad_probs - delta)).astype(BF16).reshape(2 * slots, slots)
            gq[rows, cols] = (dot(grad_scores, split_heads(k[rows, cols]), 0, 0) * scale).astype(BF16)
            gk[rows, cols] = join_heads(dot(grad_scores, q[rows, cols], 1, 0)).astype(BF16)
            gv[rows, cols] = join_heads(dot(probs_low, gc[rows, cols], 1, 0)).astype(BF16)

    white, inverse = whiten(resid[...].astype(F32))
    normed = (white * gain[layer:layer + 1] + shift[layer:layer + 1]).astype(BF16)
    turn(normed)
    put(2, gv[...])
    if not joint:
        for made, out in zip(grads, outs):
            leaving.send(made.at[1], out.at[1])
    put(0, gq[...])
    put(1, gk[...])
    for made, out in zip(grads, outs):
        if joint:
            leaving.send(made, out)
        else:
            leaving.send(made.at[0], out.at[0])
    total = dot(gq[...], w_query[...], 1, 1) + dot(gk[...], w_key[...], 1, 1) + dot(gv[...], w_value[...], 1, 1)
    sums[0:1] = column_sum(total * white)
    sums[1:2] = column_sum(total)
    grad_resid[...] = grad + whiten_back(white, inverse, gain[layer:layer + 1], total)
    leaving.send(grad_resid, resid_out)
    leaving.wait()


def attend_back(layer, crossed, grad_mixed, resid, gain, shift, gate, kept, weights, blocks, joint, ties):
    rows, width = resid.shape
    vmem = pl.BlockSpec(memory_space=pltpu.VMEM)
    kept = list(kept)
    given = 6 + len(kept) + 4
    if joint:
        grads = [jax.ShapeDtypeStruct((4, width, width), BF16)]
    else:
        grads = [jax.ShapeDtypeStruct((2, 2, 2, 2, 3, width // 8, width // 3), BF16)] * 2

    def body(*refs):
        ins, rest = list(refs[:given]), refs[given + len(ties):]
        if not crossed:
            ins.insert(11, None)
        count = len(grads)
        resid_out, sums, outs, resid_made, rest = rest[0], rest[1], rest[2:2 + count], rest[2 + count], rest[3 + count:]
        attend_back_kernel(layer, crossed, joint, *ins, resid_out, sums, outs, resid_made, rest[:count],
                           rest[count:count + len(landing)], *rest[count + len(landing):])

    low = pltpu.VMEM((rows, width), BF16)
    like = lambda value: pltpu.VMEM(value.shape, value.dtype)
    q, k, v, p, context, *branch = kept
    landing = [like(value) for value in (context, grad_mixed, *branch, v, p, k, q, resid)]
    anywhere = pl.BlockSpec(memory_space=pl.ANY)
    return pl.pallas_call(
        body,
        out_shape=[jax.ShapeDtypeStruct((rows, width), F32), jax.ShapeDtypeStruct((8, width), F32)] + grads,
        in_specs=[pl.BlockSpec(memory_space=pltpu.SMEM)] + [anywhere] * 2 + [vmem] * 3
        + [anywhere] * (len(kept) + 4 + len(ties)),
        out_specs=[anywhere, vmem] + [anywhere] * len(grads),
        scratch_shapes=[pltpu.VMEM((rows, width), F32)] + [like(grad) for grad in grads] + landing
        + [pltpu.VMEM((4, width, width), BF16), pltpu.VMEM((width, rows), BF16), pltpu.VMEM((width, rows), BF16),
           low, low, low, low, pltpu.SemaphoreType.DMA((16,)), pltpu.SemaphoreType.DMA((5,))],
        compiler_params=pltpu.CompilerParams(vmem_limit_bytes=VMEM_BYTES),
        cost_estimate=pl.CostEstimate(flops=16 * rows * width * width, bytes_accessed=24 * 2**20, transcendentals=0),
    )(blocks, grad_mixed, resid, gain, shift, gate, *kept, *weights, *ties)


def pack_kernel(layers, rows, block, bias, w_up, w_down, *rest):
    outs, sems = rest[:layers], rest[layers]
    start = pl.multiple_of(block[0] * rows, rows)
    sources = [w.at[layer, pl.ds(start, rows)] for layer in range(layers) for w in (w_up, w_down)]
    targets = [out.at[pl.ds(kind * rows, rows)] for out in outs for kind in range(2)]
    copies = start_copies(sources, targets, sems)
    for layer, out in enumerate(outs):
        out[2 * rows:] = bias_terms(bias[layer:layer + 1])
    for copy in copies:
        copy.wait()


def bias_terms(bias):
    top = bias.astype(BF16)
    left = bias - top.astype(F32)
    middle = left.astype(BF16)
    bottom = (left - middle.astype(F32)).astype(BF16)
    row = lax.broadcasted_iota(jnp.int32, (16, bias.shape[1]), 0)
    terms = [jnp.broadcast_to(term.astype(F32), row.shape) for term in (top, middle, bottom)]
    zero = jnp.zeros(row.shape, F32)
    chosen = jnp.where(row == 0, terms[0], jnp.where(row == 1, terms[1], jnp.where(row == 2, terms[2], zero)))
    return chosen.astype(BF16)


def pack(w_up, w_down, b_up, block):
    layers, width, shard = w_up.shape
    rows = width // 8
    out = jax.ShapeDtypeStruct((2 * rows + 16, shard), BF16)
    vmem = pl.BlockSpec(memory_space=pltpu.VMEM)
    return pl.pallas_call(
        functools.partial(pack_kernel, layers, rows),
        out_shape=[out] * layers,
        in_specs=[pl.BlockSpec(memory_space=pltpu.SMEM), vmem] + [pl.BlockSpec(memory_space=pl.ANY)] * 2,
        out_specs=[vmem] * layers,
        scratch_shapes=[pltpu.SemaphoreType.DMA((2 * layers,))],
        cost_estimate=pl.CostEstimate(flops=0, bytes_accessed=4 * layers * rows * shard * 4, transcendentals=0),
    )(block, b_up, w_up, w_down)


class Chain:
    def __init__(self, token):
        self.token, self.pending = token, []

    def need(self, *places):
        self.pending += places

    def tie(self, *values):
        count = len(values)
        out = lax.optimization_barrier((*values, self.token, *(held[key] for held, key in self.pending)))
        self.token = out[count]
        for (held, key), value in zip(self.pending, out[count + 1:]):
            held[key] = value
        self.pending = []
        return out[0] if count == 1 else out[:count]

    def ties(self):
        out, self.pending = [self.token] + [held[key] for held, key in self.pending], []
        return out


def places(values):
    return [(values, at) for at in range(len(values))]


def swap(value, axis, bit):
    size = lax.axis_size(axis)
    return lax.ppermute(value, axis, [(at, at ^ bit) for at in range(size)])


class Flow:
    def __init__(self, keep, index, bits, stages):
        self.wide, self.index, self.bits, self.stages, self.terms = [keep], list(index), bits, stages, []
        self.tile = keep.shape[-2:]

    def halve(self):
        bit, self.bits = self.bits[0], self.bits[1:]
        leaves = list(self.index)
        leaves[bit], self.index[bit] = 1, 0
        return tuple(leaves)

    def order(self, shape):
        open_dims = [dim for dim, at in enumerate(self.index) if at is None]
        ranked = list(self.bits) + [dim for dim in open_dims if dim not in self.bits]
        sizes = [shape[dim] for dim in open_dims]
        places = [()]
        for dim in ranked:
            places = [place + (at,) for place in places for at in range(shape[dim])]
        return sizes, [tuple(place[ranked.index(dim)] for dim in open_dims) for place in places]


def feed_flows(layer, grads):
    keep = grads[0].reshape((2, 2) + grads[0].shape[1:])
    dims = {"u": 0, "v": 1, "x": 4, "y": 5}
    return [Flow(keep, (None, None, at, None, None, None), tuple(dims[letter] for letter in stages), stages)
            for at, stages in enumerate(PART_STAGES[layer])]


def attend_flows(grads):
    return [Flow(grads[0], (at, None, None, None, None), bits, stages)
            for at, (bits, stages) in enumerate((((1, 2), "xy"), ((2, 1), "yx")))]


class Reads:
    def __init__(self):
        self.arrays = []

    def at(self, array):
        for at, known in enumerate(self.arrays):
            if known is array:
                return at
        self.arrays.append(array)
        return len(self.arrays) - 1

    def places(self, terms):
        return [(self.at(array), place) for array, place in terms]


def as_block(value):
    tile = value.shape[1] // 3
    parts = [value[:, at * tile:(at + 1) * tile] for at in range(3)]
    return jnp.concatenate(parts + [jnp.zeros_like(parts[0])], axis=0).astype(BF16)


def from_block(block):
    value = block.astype(F32)
    rows = value.shape[0] // 4
    return jnp.concatenate([value[at * rows:(at + 1) * rows] for at in range(3)], axis=1)


def add_small_parts(parts, blocks, out):
    out[...] = jnp.zeros_like(out)
    for layer in range(2):
        fed, attended, up = parts[3 * layer:3 * layer + 3]
        base = 10 * layer
        out[base:base + 3] = fed[0:3]
        out[base + 3:base + 6] = attended[0:3]
        for slot in range(len(SHARD_ORDER)):
            out[pl.ds(base + 6 + blocks[8 + slot], 1)] = up[slot]


def exchange_kernel(plan, blocks, *refs):
    (sizes, reads, sends, column_count, ends, small, small_terms, small_ends,
     array_count, small_count, tie_count) = plan
    arrays, refs = refs[:array_count], refs[array_count:]
    small_ins, refs = refs[:small_count], refs[small_count + tie_count:]
    outs, refs = refs[:len(sizes)], list(refs[len(sizes):])
    own = refs.pop(0) if column_count else None
    small_out = refs.pop(0) if small == "new" else None
    out_sems, sems = refs.pop(), refs.pop()
    mades = [refs.pop(0) for _ in sizes]
    copies, groups = [], []

    def fetch(source, target):
        copies.append(pltpu.make_async_copy(source, target, sems.at[len(copies)]))
        copies[-1].start()
        return copies[-1]

    for wide, _, terms, size in reads:
        held_wide = refs.pop(0)
        held = refs.pop(0) if terms else None
        waits = [fetch(arrays[array].at[index], held_wide.at[at]) for at, (array, index) in enumerate(wide)]
        waits += [fetch(arrays[array].at[pl.ds(place, size)], held.at[at]) for at, (array, place) in enumerate(terms)]
        groups.append((waits, held_wide, held))
    held_small = refs.pop(0) if small_terms else None
    small_waits = [fetch(arrays[array].at[pl.ds(place, 1)], held_small.at[at]) for at, (array, place) in enumerate(small_terms)]

    def arrive(number):
        waits, held_wide, held = groups[number]
        for copy in waits:
            copy.wait()
        wide, _, terms, _ = reads[number]
        return lambda block, place: [held_wide[(at,) + place] for at in range(len(wide))] + [
            held[at, block] for at in range(len(terms))]

    for number, (out, start, order) in enumerate(sends):
        values_of = arrive(number)
        for block, place in enumerate(order):
            values = values_of(block, place)
            while len(values) > 1:
                values = [values[at] + values[at + 1] if at + 1 < len(values) else values[at]
                          for at in range(0, len(values), 2)]
            mades[out][start + block] = values[0]
    if column_count:
        turned = refs.pop(0)
        shards = len(SHARD_ORDER)
        share = turned.shape[2] // 4
        for flow in range(column_count):
            values_of = arrive(len(sends) + flow)
            lines, tiles = reads[len(sends) + flow][1]
            for line in range(lines):
                parts = []
                for tile in range(tiles):
                    total = None
                    for value in values_of(line * tiles + tile, (line, tile)):
                        total = value.astype(F32) if total is None else total + value.astype(F32)
                    parts.append(total)
                whole = jnp.concatenate(parts, axis=1)
                to = (2 * flow + line) * share
                for shard in range(shards):
                    turned[shard ^ blocks[8], :, to:to + share] = whole[:, shard * share:(shard + 1) * share]
        own[...] = turned[0]
        tile = mades[0].shape[2]
        for other in range(1, shards):
            out, start = ends[other - 1]
            for cut in range(3):
                mades[out][start + cut] = turned[other, :, cut * tile:(cut + 1) * tile].astype(BF16)
    if small:
        if small == "new":
            add_small_parts(small_ins, blocks, small_out)
            total = small_out[...]
        else:
            total = small_ins[0][...]
            for copy in small_waits:
                copy.wait()
            for term in range(len(small_terms)):
                total = total + from_block(held_small[term, 0])
        for out, start in small_ends:
            mades[out][start] = as_block(total)
    leaving = [pltpu.make_async_copy(made, outs[at], out_sems.at[at]) for at, made in enumerate(mades)]
    for copy in leaving:
        copy.start()
    for copy in leaving:
        copy.wait()


def pause_kernel(source, out):
    out[...] = jnp.zeros_like(out)


def pause(value):
    return pl.pallas_call(
        pause_kernel,
        out_shape=jax.ShapeDtypeStruct((8, 128), F32),
        in_specs=[pl.BlockSpec(memory_space=pl.ANY)],
        out_specs=pl.BlockSpec(memory_space=pltpu.VMEM),
        compiler_params=pltpu.CompilerParams(vmem_limit_bytes=VMEM_BYTES),
    )(value)


class Rounds:
    def __init__(self, blocks):
        self.blocks, self.arrived = blocks, []

    def exchange(self, flows, ending=(), small=None, ties=(), crossing=(), alone=False):
        known, reads, sends, sizes = Reads(), [], [], {}

        def room(letter, size):
            place = sizes.get(letter, 0)
            sizes[letter] = place + size
            return list(sizes).index(letter), place

        def read(flow, index, skipped):
            shape = flow.wide[0].shape
            open_sizes, order = flow.order(shape)
            size = len(order)
            wide = [(known.at(array), tuple(slice(None) if at is None else at for at in index)) for array in flow.wide]
            reads.append((wide, open_sizes, [(known.at(array), start + skipped * size) for array, start in flow.terms], size))
            return size, order

        moved = []
        for flow in flows:
            letter, flow.stages = flow.stages[0], flow.stages[1:]
            size, order = read(flow, flow.halve(), 1)
            out, place = room(letter, size)
            sends.append((out, place, order))
            moved.append((flow.terms, letter, place))
        tile = flows[0].tile
        width = 3 * tile[1]
        for pair in ending:
            for flow in pair:
                read(flow, flow.index, 0)
        column_count = len(reads) - len(sends)
        ends = [room(letter, 3) for letter in "uvw"] if column_count else []
        mode, small_terms, small_ins, small_ends = "", [], [], []
        if small is not None:
            mode, letters = small.next()
            small_ins = small.parts if mode == "new" else [small.own]
            small_terms = [] if mode == "new" else known.places(small.terms)
            small_ends = [room(letter, 1) for letter in letters]
        order = list(sizes)
        outs = [jax.ShapeDtypeStruct((sizes[letter],) + tile, BF16) for letter in order]
        held = [pltpu.VMEM((sizes[letter],) + tile, BF16) for letter in order]
        for wide, open_sizes, terms, size in reads:
            held.append(pltpu.VMEM((len(wide), *open_sizes) + tile, BF16))
            if terms:
                held.append(pltpu.VMEM((len(terms), size) + tile, BF16))
        if small_terms:
            held.append(pltpu.VMEM((len(small_terms), 1) + tile, BF16))
        more = []
        if column_count:
            held.append(pltpu.VMEM((len(SHARD_ORDER), tile[0], width), F32))
            more.append(jax.ShapeDtypeStruct((tile[0], width), F32))
        if mode == "new":
            more.append(jax.ShapeDtypeStruct((24, width), F32))
        ties = [*self.arrived, *ties]
        copies = sum(len(wide) + len(terms) for wide, _, terms, _ in reads) + len(small_terms)
        anywhere, vmem = pl.BlockSpec(memory_space=pl.ANY), pl.BlockSpec(memory_space=pltpu.VMEM)
        plan = ([sizes[letter] for letter in order], reads, sends, column_count, ends, mode, small_terms, small_ends,
                len(known.arrays), len(small_ins), len(ties))
        made = list(pl.pallas_call(
            functools.partial(exchange_kernel, plan),
            out_shape=outs + more,
            in_specs=[pl.BlockSpec(memory_space=pltpu.SMEM)] + [anywhere] * len(known.arrays) + [vmem] * len(small_ins)
            + [anywhere] * len(ties),
            out_specs=[anywhere] * len(outs) + [vmem] * len(more),
            scratch_shapes=held + [pltpu.SemaphoreType.DMA((copies,)), pltpu.SemaphoreType.DMA((len(outs),))],
            compiler_params=pltpu.CompilerParams(vmem_limit_bytes=VMEM_BYTES),
        )(self.blocks, *known.arrays, *small_ins, *ties))
        rest = made[len(outs):]
        self.made = made[:len(outs)]
        going = lax.optimization_barrier(self.made + [send for _, send in crossing])
        arrived = {letter: swap(value, *LINKS[letter]) for letter, value in zip(order, going)}
        self.arrived = list(arrived.values())
        self.going = going[0]
        if alone:
            self.arrived.append(pause(going[0]))
        for (crossed, _), send in zip(crossing, going[len(outs):]):
            self.cross(crossed, send)
        for terms, letter, place in moved:
            terms.append((arrived[letter], place))
        for pair in ending:
            pair[0].own = rest.pop(0)
            pair[0].far = [(arrived[letter], place) for letter, (_, place) in zip("uvw", ends)]
        if mode:
            if mode == "new":
                small.own = rest.pop(0)
            small.terms += [(arrived[letter], place) for letter, (_, place) in zip(letters, small_ends)]

    def cross(self, flows, send):
        arrived = swap(send, *LINKS["c"])
        self.arrived.append(arrived)
        for flow in flows:
            flow.wide.append(arrived.reshape(flow.wide[0].shape))


class Small:
    def __init__(self, parts):
        self.parts, self.terms, self.stages = parts, [], ["c", "x", "uvw", "y"]

    def next(self):
        letters = self.stages.pop(0)
        return ("new" if letters == "c" else "old"), letters


def finish_kernel(plan, layer, counts, blocks, *refs):
    wides, feeds, far, small = plan
    array_count, other_count = counts
    arrays, own, refs = refs[:array_count], refs[array_count], refs[array_count + 1:]
    if small:
        small_own, refs = refs[0], refs[1:]
    refs = refs[other_count:]
    outs, refs = refs[:6], refs[6:]
    if small:
        smalls, gate, hidden, refs = refs[:5], refs[5], refs[6], refs[7:]
    up, down, attends, held_wide, held, held_far, held_small, sems, out_sems = refs
    copies = []

    def fetch(source, target):
        copies.append(pltpu.make_async_copy(source, target, sems.at[len(copies)]))
        copies[-1].start()

    for term, array in wides:
        fetch(arrays[array].at[0, 0, :, :, 0, 0], held_wide.at[term])
    for part, term, array, place in feeds:
        fetch(arrays[array].at[pl.ds(place, 2)], held.at[part, term])
    for other, array, place in far:
        fetch(arrays[array].at[pl.ds(place, 3)], held_far.at[other])
    for term, (array, place) in enumerate(small):
        fetch(arrays[array].at[pl.ds(place, 1)], held_small.at[term])
    for copy in copies:
        copy.wait()
    leaving = Leaving(out_sems)
    terms, tile = held.shape[1], held.shape[4]
    for part in range(3):
        total = held_wide[0, part].astype(F32) + held_wide[1, part].astype(F32)
        for term in range(terms):
            total = total + held[part, term].astype(F32)
        up[:, part * tile:(part + 1) * tile] = total[0]
        down[:, part * tile:(part + 1) * tile] = total[1]
    leaving.send(up, outs[0].at[layer])
    leaving.send(down, outs[1].at[layer])
    total = own[...]
    for other in range(3):
        total = total + jnp.concatenate([held_far[other, cut].astype(F32) for cut in range(3)], axis=1)
    share = total.shape[1] // 4
    for at in range(4):
        attends[at] = total[:, at * share:(at + 1) * share]
        leaving.send(attends.at[at], outs[2 + at].at[layer])
    if small:
        total = small_own[...]
        for term in range(len(small)):
            total = total + from_block(held_small[term, 0])
        lines = total.shape[1] // 8
        mine = jnp.where(blocks[0] == 0, total[:, :lines], 0.0)
        for place in range(1, 8):
            mine = mine + jnp.where(blocks[0] == place, total[:, place * lines:(place + 1) * lines], 0.0)
        for at in range(2):
            base = 10 * at
            for row, out in zip((3, 4, 1, 2, 0), smalls):
                out[at:at + 1] = mine[base + row:base + row + 1]
            shard = jnp.zeros((1, total.shape[1]), F32)
            for index in range(4):
                shard = shard + jnp.where(blocks[8] == index, total[base + 6 + index:base + 7 + index], 0.0)
            hidden[at:at + 1] = shard
        gate[...] = mine[5:6]
    leaving.wait()


def finish(layer, feeds, attends, blocks, before, small=None):
    reads = Reads()
    wide_plan = [(term, reads.at(array)) for term, array in enumerate(feeds[0].wide)]
    feed_plan = [(part, term, reads.at(array), place) for part, flow in enumerate(feeds)
                 for term, (array, place) in enumerate(flow.terms)]
    far_plan = [(other, reads.at(array), place) for other, (array, place) in enumerate(attends[0].far)]
    small_plan = reads.places(small.terms) if small else []
    rows, tile = feeds[0].tile
    width, terms = 3 * tile, len(feeds[0].terms)
    anywhere, vmem = pl.BlockSpec(memory_space=pl.ANY), pl.BlockSpec(memory_space=pltpu.VMEM)
    outs = [jax.ShapeDtypeStruct((2, rows, width), F32)] * 2 + [jax.ShapeDtypeStruct((2, rows, width // 4), F32)] * 4
    more = [jax.ShapeDtypeStruct((2, rows), F32)] * 5 + [
        jax.ShapeDtypeStruct((1, rows), F32), jax.ShapeDtypeStruct((2, width), F32)] if small else []
    given = 2 + len(reads.arrays) + (1 if small else 0)
    return pl.pallas_call(
        functools.partial(finish_kernel, (wide_plan, feed_plan, far_plan, small_plan), layer, (len(reads.arrays), len(before))),
        out_shape=outs + more,
        in_specs=[pl.BlockSpec(memory_space=pltpu.SMEM)] + [anywhere] * len(reads.arrays) + [vmem] * (given - 1 - len(reads.arrays))
        + [anywhere] * len(before),
        out_specs=[anywhere] * 6 + [vmem] * len(more),
        scratch_shapes=[pltpu.VMEM((rows, width), F32), pltpu.VMEM((rows, width), F32), pltpu.VMEM((4, rows, width // 4), F32),
                        pltpu.VMEM((2, 3, 2, rows, tile), BF16), pltpu.VMEM((3, terms, 2, rows, tile), BF16),
                        pltpu.VMEM((3, 3, rows, tile), BF16), pltpu.VMEM((max(len(small_plan), 1), 1, rows, tile), BF16),
                        pltpu.SemaphoreType.DMA((len(wide_plan) + len(feed_plan) + len(far_plan) + len(small_plan),)),
                        pltpu.SemaphoreType.DMA((6,))],
        input_output_aliases={given + at: at for at in range(6)} if small else {},
        compiler_params=pltpu.CompilerParams(vmem_limit_bytes=VMEM_BYTES),
    )(blocks, *reads.arrays, attends[0].own, *([small.own] if small else []), *before)


def eighths(weights):
    return weights.reshape(weights.shape[:-2] + (2, 2, 2, weights.shape[-2] // 8, weights.shape[-1]))


def in_order(bit, own, other):
    first = (lax.axis_index("dp") & bit) == 0
    return jnp.stack([jnp.where(first, own, other), jnp.where(first, other, own)])


def far_pieces(layer, w_up, w_down, tails, halves, crossed, blocks):
    arrays = [eighths(w_up), eighths(w_down)] + halves + crossed
    every, rest = slice(None), pl.ds(1, len(tails) - 1)
    plan = [(kind, layer, kind, lambda me: (every, every, every, 0)) for kind in range(2)]
    for core in range(2):
        for second in range(2):
            plan.append((2 + 4 * core + second, None, 0, lambda me, core=core, second=second: (
                ((me >> 2) & 1) ^ second, every, (me & 1) ^ core, rest)))
            plan.append((4 + 4 * core + second, None, 1, lambda me, core=core, second=second: (
                every, ((me >> 1) & 1) ^ second, (me & 1) ^ core, rest)))
    return Pieces(arrays, plan, blocks, tails)


def gathered_pieces(layer, w_up, w_down, b_up, blocks):
    arrays = [eighths(lax.all_gather(weights[layer], "mp")) for weights in (w_up, w_down)]
    shards = arrays[0].shape[0]
    plan = [(kind, at, kind, lambda me, at=at: (slice(None),) * 3 + (at,)) for at in range(shards) for kind in range(2)]
    bias = lax.all_gather(b_up[layer:layer + 1], "mp")
    return Pieces(arrays, plan, blocks, [bias_terms(bias[at]) for at in range(shards)])


def sum_feed_anywhere(grads):
    both = lax.psum_scatter(grads, "mp", scatter_dimension=0, tiled=True)[0]
    both = lax.psum_scatter(both.astype(F32), "dp", scatter_dimension=1, tiled=True)
    return both[0], both[1].T


def sum_attend_anywhere(grads):
    whole = lax.psum_scatter(grads, "mp", scatter_dimension=2, tiled=True)
    return lax.psum_scatter(whole.astype(F32), "dp", scatter_dimension=1, tiled=True)


def shards(inputs, slot_valid, ln1_gain, ln1_bias, w_query, w_key, w_value, w_out, gate_logit,
           ln2_gain, ln2_bias, w_up, b_up, w_down, b_down, cotangent):
    pages, slots, width = inputs.shape
    dp, mp = lax.axis_size("dp"), lax.axis_size("mp")
    paired = dp == 8 and mp == 4 and width % (16 * dp) == 0
    if paired:
        place = jnp.arange(12, dtype=jnp.int32)
        slot = place & 3
        blocks = jnp.where(place < 8, lax.axis_index("dp") ^ place, lax.axis_index("mp") ^ ((slot & 1) * 2 + slot // 2))
    else:
        blocks = jnp.arange(2, dtype=jnp.int32)

    own_valid = lax.dynamic_slice_in_dim(slot_valid, lax.axis_index("mp") * pages, pages, 0) == 1
    key_text = lax.broadcasted_iota(jnp.int32, (slots, slots), 0) < TEXT
    query_text = lax.broadcasted_iota(jnp.int32, (slots, slots), 1) < TEXT
    live = jnp.broadcast_to(own_valid[:, :, None], (pages, slots, slots))
    masks = [
        jnp.where(jnp.logical_and(live, (key_text != query_text)[None]), 0.0, -1e30).astype(F32),
        jnp.where(live, 0.0, -1e30).astype(F32),
    ]
    gate = gate_logit[None]
    weights = (w_query, w_key, w_value, w_out)
    first_rows = inputs.reshape(pages * slots, width)
    cotangent = cotangent.reshape(pages * slots, width)
    got = {"grad": None}

    def attend_layer(layer, rows, ties):
        return attend(layer, layer == 0, rows, masks[layer], ln1_gain, ln1_bias, gate, weights, ties)

    def feed_layer(layer, rows, pieces, ties):
        return feed(layer, rows, ln2_gain, ln2_bias, b_down, pieces, (F32, BF16)[layer], ties)

    def feed_back_layer(layer, ties):
        rows, active, slope, pieces = got["feed", layer]
        got["mixed_grad"], got["feed_sums", layer], got["up_sums", layer], *got["feed_grads", layer] = feed_back(
            layer, (got["grad"], cotangent)[layer], rows, ln2_gain, ln2_bias, active, slope, pieces, not paired, ties)

    def attend_back_layer(layer, ties):
        rows, kept = got["attend", layer]
        got["grad"], got["attend_sums", layer], *got["attend_grads", layer] = attend_back(
            layer, layer == 0, got["mixed_grad"], rows, ln1_gain, ln1_bias, gate, (*kept[:5], *kept[6:]), weights,
            blocks, not paired, ties)

    if paired:
        owns = pack(w_up, w_down, b_up, blocks)
        rows = width // 8
        chain = Chain(owns[0])
        far = lambda own: [swap(own, "mp", other) for other in SHARD_ORDER[1:]]
        split = lambda pieces: (jnp.stack([piece[:rows] for piece in pieces]),
                                jnp.stack([piece[rows:2 * rows] for piece in pieces]))
        other_core = lambda *values: [swap(value, "dp", 1) for value in values]

        far_0 = far(owns[0])
        kept_0 = list(attend_layer(0, first_rows, ()))
        chain.need((kept_0, 5))
        far_0 = list(chain.tie(*far_0))
        ups, downs = chain.tie(*split(far_0))
        near_0 = [swap(ups, "dp", 2), swap(downs, "dp", 4)]
        far_1 = far(chain.tie(owns[1]))
        near_0 = chain.tie(*near_0)
        ups_0, downs_0 = chain.tie(in_order(2, ups, near_0[0]), in_order(4, downs, near_0[1]))
        side_0 = [swap(ups_0, "dp", 4), swap(downs_0, "dp", 2)]
        ups_0, downs_0, *side_0 = chain.tie(ups_0, downs_0, *side_0)
        far_1 = list(chain.tie(*far_1))
        ups, downs = chain.tie(*split(far_1))
        near_1 = [swap(ups, "dp", 2), swap(downs, "dp", 4)]
        core_0 = other_core(ups_0, side_0[0], downs_0, side_0[1])
        pieces_0 = far_pieces(0, w_up, w_down, [owns[0]] + far_0, [ups_0, side_0[0], downs_0, side_0[1]], core_0, blocks)
        near_1 = chain.tie(*near_1)
        ups_1, downs_1 = chain.tie(in_order(2, ups, near_1[0]), in_order(4, downs, near_1[1]))
        side_1 = [swap(ups_1, "dp", 4), swap(downs_1, "dp", 2)]
        fed_0 = list(feed_layer(0, kept_0[5], pieces_0, chain.ties()))
        chain.need((fed_0, 0))
        ups_1, downs_1, *side_1 = chain.tie(ups_1, downs_1, *side_1)
        result_0, active_0, slope_0 = fed_0
        core_1 = other_core(ups_1, side_1[0], downs_1, side_1[1])
        kept_1 = list(attend_layer(1, result_0, side_1))
        pieces_1 = far_pieces(1, w_up, w_down, [owns[1]] + far_1, [ups_1, side_1[0], downs_1, side_1[1]], core_1, blocks)
    else:
        pieces_0 = gathered_pieces(0, w_up, w_down, b_up, blocks)
        pieces_1 = gathered_pieces(1, w_up, w_down, b_up, blocks)
        kept_0 = attend_layer(0, first_rows, ())
        result_0, active_0, slope_0 = feed_layer(0, kept_0[5], pieces_0, ())
        kept_1 = attend_layer(1, result_0, ())

    result_1, active_1, slope_1 = feed_layer(1, kept_1[5], pieces_1, ())
    got["feed", 0] = kept_0[5], active_0, slope_0, pieces_0
    got["feed", 1] = kept_1[5], active_1, slope_1, pieces_1
    got["attend", 0], got["attend", 1] = (first_rows, kept_0), (result_0, kept_1)

    if paired:
        rounds = Rounds(blocks)
        feed_back_layer(1, ())
        feeds, attends = {1: feed_flows(1, got["feed_grads", 1])}, {}
        rounds.cross(feeds[1], got["feed_grads", 1][1])
        attend_back_layer(1, ())
        attends[1] = attend_flows(got["attend_grads", 1])
        rounds.exchange(feeds[1], ties=[got["attend_sums", 1]], crossing=[(attends[1], got["attend_grads", 1][1])])
        feed_back_layer(0, rounds.made)
        feeds[0] = feed_flows(0, got["feed_grads", 0])
        rounds.exchange(feeds[1] + attends[1], ties=[got["feed_sums", 0]], crossing=[(feeds[0], got["feed_grads", 0][1])])
        attend_back_layer(0, rounds.made)
        attends[0] = attend_flows(got["attend_grads", 0])
        small = Small([got[name, layer] for layer in (0, 1) for name in ("feed_sums", "attend_sums", "up_sums")])
        rounds.exchange(feeds[0] + feeds[1] + attends[1], small=small, crossing=[(attends[0], got["attend_grads", 0][1])], alone=True)
        rounds.exchange(feeds[0] + attends[0] + feeds[1], [attends[1]], small, alone=True)
        rounds.exchange(feeds[0] + attends[0], small=small, alone=True)
        rounds.exchange(feeds[0], [attends[0]], small)
        made = finish(1, feeds[1], attends[1], blocks, [rounds.going])
        up_grad, down_turned, *rest = finish(0, feeds[0], attends[0], blocks, made, small)
        down_grad = jnp.swapaxes(down_turned, 1, 2)
        attend_grads, small_grads, gate_grad, bup_grad = rest[:4], rest[4:9], rest[9][0], rest[10]
    else:
        for layer in (1, 0):
            feed_back_layer(layer, ())
            attend_back_layer(layer, ())
        feed_grads = [sum_feed_anywhere(got["feed_grads", layer][0]) for layer in (0, 1)]
        up_grad, down_grad = (jnp.stack([feed_grads[layer][at] for layer in (0, 1)]) for at in range(2))
        sums = [sum_attend_anywhere(got["attend_grads", layer][0]) for layer in (0, 1)]
        attend_grads = [jnp.stack([sums[0][at], sums[1][at]]) for at in range(4)]
        both = lax.psum(jnp.concatenate([part for layer in (0, 1) for part in (
            got["feed_sums", layer][:3], got["attend_sums", layer][:3], got["up_sums", layer][:, 0])]), ("dp", "mp"))
        later, lines, me = both.shape[0] // 2, width // dp, lax.axis_index("mp")
        mine = lax.dynamic_slice_in_dim(both, lax.axis_index("dp") * lines, lines, 1)
        small_grads = [jnp.stack([mine[row], mine[later + row]]) for row in (3, 4, 1, 2, 0)]
        gate_grad = mine[5]
        bup_grad = jnp.concatenate([lax.dynamic_slice_in_dim(both, row + me, 1, 0) for row in (6, later + 6)])

    return (
        result_1.reshape(pages, slots, width),
        got["grad"].reshape(pages, slots, width),
        small_grads[0],
        small_grads[1],
        *attend_grads,
        gate_grad,
        small_grads[2],
        small_grads[3],
        up_grad,
        bup_grad,
        down_grad,
        small_grads[4],
    )


def solution(mesh):
    rows = P(("dp", "mp"), None, None)
    return jax.shard_map(
        shards,
        mesh=mesh,
        in_specs=(rows, P("dp", None), P(), P(), P(), P(), P(), P(), P(), P(), P(), P(None, None, "mp"),
                  P(None, "mp"), P(None, "mp", None), P(), rows),
        out_specs=(rows, rows, P(None, "dp"), P(None, "dp"), P(None, "dp", "mp"), P(None, "dp", "mp"),
                   P(None, "dp", "mp"), P(None, "dp", "mp"), P("dp"), P(None, "dp"), P(None, "dp"),
                   P(None, "dp", "mp"), P(None, "mp"), P(None, "mp", "dp"), P(None, "dp")),
        check_vma=False,
    )
```
